32 devices in a mesh: band: 8 (over z, core), dom: 4 (over y, x).
Axes of the slice: x: 2, y: 2, z: 4, core: 2. Of those that a mesh axis runs over, the one named last changes fastest.
Arguments:
- orbitals: bfloat16 [512, 24576], P('band', 'dom'), may hold values from -6 to 6
- rotation: bfloat16 [512, 256], P('band'), may hold values from -0.375 to 0.375
- projectors: bfloat16 [32, 16, 24576], P(None, None, 'dom'), may hold values from -0.078125 to 0.078125
- coupling: float32 [64, 16, 16], P('dom'), may hold values from -5 to 5
- slot_atom: int32 [4, 32], replicated, may hold values from 0 to 63, as said below
Outputs:
- updated_orbitals: bfloat16 [512, 24576], P('band', 'dom')
The draws below stay inside these ranges and needn't reach their ends.
Inputs may be any that keep to these rules, and one draw needn't show every extreme that they name: `slot_atom`: the atoms of one row are distinct. Atom a is owned by domain a // 16. A row names at most 16 atoms of any one owner; domain 4 - 1 is named exactly 16 times by every row. Other owners are named between 0 and 16 times, unevenly.
All inputs are finite; a program needn't handle non-finite values.
Results may differ from the reference program's by a relative error of at most 0.0057.
Values may be sent and summed in bfloat16 or wider, within the bound.
No kernel may reach another device: no remote copies, remote signals or barrier semaphores. Data moves between devices by JAX's collectives and lax.ppermute only.
A program may use at most 64 MiB of HBM per device.

```python
import jax
import jax.numpy as jnp
from jax import lax

BLOCK = 64
STOPS = 4
NPROJ = 16
GDEV = 6144
ATOM_DEV = 16
K_LOC = 32
REGION_COUNT = 4
NORB = 512
NGRID = 24576
NATOM = 64
CAP = 16


def draw_slot_atom(key, part):
    starting_key = jax.random.fold_in(key, 101)
    extra_seed = jax.random.fold_in(starting_key, 1)
    rating_seed = jax.random.fold_in(starting_key, 2)
    nearness_seed = jax.random.fold_in(starting_key, 3)
    reorder_seed = jax.random.fold_in(starting_key, 4)
    total_slots = REGION_COUNT * CAP
    preferred_owner = REGION_COUNT - 1
    owner_indices = jnp.arange(REGION_COUNT, dtype=jnp.int32)
    holder_gain = jax.random.randint(extra_seed, (REGION_COUNT,), 0, 3)
    holder_gain = jnp.where(owner_indices == preferred_owner, 3, holder_gain)
    owner_of_slot = jnp.arange(total_slots, dtype=jnp.int32) // CAP
    score_values = jax.random.randint(rating_seed, (REGION_COUNT, total_slots), 0, 1024) + holder_gain[owner_of_slot][None, :] * 1024
    score_values = score_values * total_slots + jnp.arange(total_slots, dtype=jnp.int32)[None, :]
    picked = lax.top_k(score_values, K_LOC)[1].astype(jnp.int32)
    local_keys = jax.random.randint(nearness_seed, (REGION_COUNT, REGION_COUNT, ATOM_DEV), 0, 1 << 20) * ATOM_DEV + jnp.arange(ATOM_DEV, dtype=jnp.int32)
    row_iota = jnp.arange(REGION_COUNT, dtype=jnp.int32)[:, None, None]
    owner_iota = jnp.arange(REGION_COUNT, dtype=jnp.int32)[None, :, None]
    atom_iota = jnp.arange(ATOM_DEV, dtype=jnp.int32)[None, None, :]
    forced = (row_iota == 0) & (owner_iota == REGION_COUNT - 1) & (atom_iota == ATOM_DEV - 1)
    local_keys = jnp.where(forced, -1, local_keys)
    chosen = jnp.argsort(local_keys, axis=-1, stable=True)[..., :CAP].astype(jnp.int32).reshape(REGION_COUNT, total_slots)
    local_atom = jnp.take_along_axis(chosen, picked, axis=-1)
    atom_ids = picked // CAP * ATOM_DEV + local_atom
    shuffle_keys = jax.random.randint(reorder_seed, (REGION_COUNT, K_LOC), 0, 1 << 20) * K_LOC + jnp.arange(K_LOC, dtype=jnp.int32)
    shuffle = jnp.argsort(shuffle_keys, axis=-1, stable=True)
    return jnp.take_along_axis(atom_ids, shuffle, axis=-1).astype(jnp.int32)


def shard_levels(stream_key, extent, cuts, low, top_value):
    level, own = 1.0, jax.random.fold_in(stream_key, 6)
    for position, shards_of in cuts:
        draws = jnp.exp(jax.random.uniform(jax.random.fold_in(own, position), (shards_of,), jnp.float32, low / len(cuts), top_value / len(cuts)))
        level = level * jnp.repeat(draws, extent[position] // shards_of).reshape([-1 if axis == position else 1 for axis in range(len(extent))])
    return level


def scatter_about(stream_key, extent, width, bound, pieces=(), held_as=jnp.bfloat16):
    entries = width * jax.random.normal(stream_key, extent, jnp.float32)
    if pieces:
        entries = entries * shard_levels(stream_key, extent, pieces, -0.22, 0.18)
    return jnp.clip(entries, -bound, bound).astype(held_as)


def setup_inputs(seed: int = 0) -> dict:
    key_of = jax.random.split(jax.random.key(seed), 6)
    orbitals = scatter_about(key_of[0], (NORB, NGRID), 1.0, 6.0, ((0, 8), (1, 4)))
    rotation = scatter_about(key_of[1], (NORB, STOPS * BLOCK), (STOPS * BLOCK) ** -0.5, 0.375, ((0, 8),))
    projectors = scatter_about(key_of[2], (K_LOC, NPROJ, NGRID), GDEV ** -0.5, 0.078125, ((2, 4),))
    coupling = scatter_about(key_of[3], (NATOM, NPROJ, NPROJ), 1.0, 5.0, ((0, 4),), jnp.float32)
    slot_atom = draw_slot_atom(jax.random.fold_in(key_of[5], 71), 0)
    return dict(orbitals=orbitals, rotation=rotation, projectors=projectors, coupling=coupling, slot_atom=slot_atom)


def reference(orbitals, rotation, projectors, coupling, slot_atom):
    band_count = NORB // BLOCK
    groups_all = orbitals.reshape(band_count, BLOCK, NGRID)
    tiles = rotation.reshape(band_count, BLOCK, STOPS * BLOCK)
    proj_wide = projectors.astype(jnp.float32).reshape(K_LOC, NPROJ, REGION_COUNT, GDEV)
    flat_atoms = slot_atom.reshape(-1).astype(jnp.int32)

    def one_band(band_index):
        running = jnp.zeros((BLOCK, NGRID), jnp.float32)
        tile_rows = lax.dynamic_index_in_dim(tiles, band_index, 0, keepdims=False)
        for stop_index in range(STOPS):
            source_index = ((band_index - stop_index) % band_count).astype(jnp.int32)
            source = lax.dynamic_index_in_dim(groups_all, source_index, 0, keepdims=False)
            running = running + jnp.dot(tile_rows[:, stop_index * BLOCK:(stop_index + 1) * BLOCK], source, preferred_element_type=jnp.float32)
        rotated = running.astype(jnp.bfloat16)
        rot_wide = rotated.astype(jnp.float32).reshape(BLOCK, REGION_COUNT, GDEV)
        partial_value = jnp.einsum("kpdg,odg->dkpo", proj_wide, rot_wide, precision=lax.Precision.HIGHEST)
        summed = jax.ops.segment_sum(partial_value.reshape(REGION_COUNT * K_LOC, NPROJ, BLOCK), flat_atoms, num_segments=NATOM)
        coupled = jnp.einsum("apq,aqo->apo", coupling, summed, precision=lax.Precision.HIGHEST).astype(jnp.bfloat16)
        returned = jnp.take(coupled, flat_atoms, axis=0).astype(jnp.float32).reshape(REGION_COUNT, K_LOC, NPROJ, BLOCK)
        applied = jnp.einsum("kpdg,dkpo->odg", proj_wide, returned, precision=lax.Precision.HIGHEST).reshape(BLOCK, NGRID)
        return (rotated.astype(jnp.float32) + applied).astype(jnp.bfloat16)

    outputs = lax.map(one_band, jnp.arange(band_count, dtype=jnp.int32))
    return outputs.reshape(NORB, NGRID)
```

```python
import jax
import jax.numpy as jnp
from jax import lax
from jax.sharding import PartitionSpec as P

PARTS = 4


def passed_along(block, axis, distance):
    devices = range(lax.axis_size(axis))
    route = [((i - distance) % len(devices), i) for i in devices]
    return lax.ppermute(block, axis, route)


def from_all_domains(block):
    count = lax.axis_size("dom")
    me = lax.axis_index("dom")
    if count <= 8 and count & (count - 1) == 0:
        pairs = [(me, block)]
        for mask in range(1, count):
            route = [(i, i ^ mask) for i in range(count)]
            pairs.append((me ^ mask, lax.ppermute(block, "dom", route)))
        return pairs
    whole = lax.all_gather(block, "dom")
    return [(jnp.int32(d), whole[d]) for d in range(count)]


def on_device(orbitals, rotation, projectors, coupling, slot_atom):
    width, points = orbitals.shape
    stop_count = rotation.shape[1] // width
    slot_count, proj_count, _ = projectors.shape
    flat = slot_count * proj_count
    proj = projectors.reshape(flat, points)
    tiles = [rotation[:, s * width : (s + 1) * width] for s in range(stop_count)]
    step = points // PARTS

    coef = lax.dot_general(
        orbitals, proj, (((1,), (1,)), ((), ())), preferred_element_type=jnp.float32
    ).astype(jnp.bfloat16)

    held = [[orbitals[:, j * step : (j + 1) * step]] for j in range(PARTS)]
    held_coef = [coef]
    for s in range(1, stop_count):
        for j in range(PARTS):
            held[j].append(passed_along(held[j][-1], "band", 1))
        held_coef.append(passed_along(held_coef[-1], "band", 1))

    def rotate(blocks):
        return sum(
            jnp.dot(t, x, preferred_element_type=jnp.float32) for t, x in zip(tiles, blocks)
        )

    me = lax.axis_index("dom")
    own_atoms = lax.dynamic_index_in_dim(slot_atom, me, 0, keepdims=False)
    coupling_all = lax.all_gather(coupling, "dom", tiled=True)
    mine = jnp.take(coupling_all, own_atoms, axis=0)
    columns = mine.transpose(2, 0, 1).reshape(proj_count, flat)
    own_wide = jnp.repeat(own_atoms, proj_count)[None, :]
    tall = jnp.broadcast_to(columns[None], (slot_count, proj_count, flat)).reshape(flat, flat)

    rotated_coef = rotate(held_coef)
    coupled = None
    for d, block in from_all_domains(rotated_coef):
        theirs = lax.dynamic_index_in_dim(slot_atom, d, 0, keepdims=False)
        weights = jnp.where(jnp.repeat(theirs, proj_count)[:, None] == own_wide, tall, 0.0)
        term = jnp.dot(block, weights, precision=lax.Precision.HIGHEST)
        coupled = term if coupled is None else coupled + term
    coupled = coupled.astype(jnp.bfloat16)

    outs = []
    for j in range(PARTS):
        applied = jnp.dot(
            coupled, proj[:, j * step : (j + 1) * step], preferred_element_type=jnp.float32
        )
        rotated = rotate(held[j]).astype(jnp.bfloat16).astype(jnp.float32)
        outs.append((rotated + applied).astype(jnp.bfloat16))
    return jnp.concatenate(outs, axis=1)


def solution(mesh):
    in_specs = (P("band", "dom"), P("band", None), P(None, None, "dom"), P("dom", None, None), P())
    out_specs = P("band", "dom")
    return jax.shard_map(
        on_device, mesh=mesh, in_specs=in_specs, out_specs=out_specs, check_vma=False
    )
```

```python
import functools

import jax
import jax.numpy as jnp
from jax import lax
from jax.experimental import pallas as pl
from jax.experimental.pallas import tpu as pltpu
from jax.sharding import PartitionSpec as P

PARTS = 2
F32 = jnp.float32
BF16 = jnp.bfloat16
SMALL = pl.CostEstimate(flops=0, bytes_accessed=0, transcendentals=0)
NT = (((1,), (1,)), ((), ()))


def passed_along(block, distance):
    count = lax.axis_size("band")
    return lax.ppermute(block, "band", [((i - distance) % count, i) for i in range(count)])


def swapped(block):
    count = lax.axis_size("band")
    return lax.ppermute(block, "band", [(i, i ^ 1) for i in range(count)])


def by_permutes():
    count = lax.axis_size("dom")
    return count <= 8 and count & (count - 1) == 0


def from_all_domains(block):
    count = lax.axis_size("dom")
    if by_permutes():
        routes = [[(i, i ^ mask) for i in range(count)] for mask in range(1, count)]
        return [block] + [lax.ppermute(block, "dom", route) for route in routes]
    whole = lax.all_gather(block, "dom")
    return [whole[d] for d in range(count)]


def domain_at(place):
    return lax.axis_index("dom") ^ place if by_permutes() else place


def tile_of(extent, most):
    return max(w for w in range(128, most + 1, 128) if extent % w == 0)


def project_kernel(orb_ref, proj_ref, out_ref, total):
    @pl.when(pl.program_id(0) == 0)
    def _():
        total[...] = jnp.zeros_like(total)

    total[...] += lax.dot_general(orb_ref[...], proj_ref[...], NT, preferred_element_type=F32)

    @pl.when(pl.program_id(0) == pl.num_programs(0) - 1)
    def _():
        out_ref[...] = total[...].astype(out_ref.dtype)


def project(orbitals, proj):
    width, points = orbitals.shape
    flat = proj.shape[0]
    tile = tile_of(points, 1024)
    return pl.pallas_call(
        project_kernel,
        grid=(points // tile,),
        in_specs=[
            pl.BlockSpec((width, tile), lambda g: (0, g)),
            pl.BlockSpec((flat, tile), lambda g: (0, g)),
        ],
        out_specs=pl.BlockSpec((width, flat), lambda g: (0, 0)),
        out_shape=jax.ShapeDtypeStruct((width, flat), BF16),
        scratch_shapes=[pltpu.VMEM((width, flat), F32)],
        cost_estimate=SMALL,
        name="project",
    )(orbitals, proj)


def couple_kernel(count, slots, slot_ref, *refs):
    coefs, couplings = refs[:count], refs[count : 2 * count]
    out_ref, columns, weights = refs[2 * count :]
    rank = couplings[0].shape[0]
    owned = couplings[0].shape[1] // rank
    flat = slots * rank
    me = lax.axis_index("dom")
    lane_slot = lax.broadcasted_iota(jnp.int32, (8, flat), 1) // rank

    def note_atom(k, atoms):
        return jnp.where(lane_slot == k, slot_ref[me, k], atoms)

    atoms = lax.fori_loop(0, slots, note_atom, jnp.zeros((8, flat), jnp.int32))
    for place in range(count):
        owner = domain_at(place)
        whole = couplings[place][...]
        a = owner * owned + lax.broadcasted_iota(jnp.int32, (owned * rank, flat), 0) // rank
        same = lax.broadcasted_iota(jnp.int32, (owned * rank, flat), 0) % rank == (
            lax.broadcasted_iota(jnp.int32, (owned * rank, flat), 1) % rank
        )
        pick = jnp.where(same & (a == atoms[:1]), 1.0, 0.0).astype(BF16)
        high = whole.astype(BF16)
        rest = whole - high.astype(F32)
        mid = rest.astype(BF16)
        low = (rest - mid.astype(F32)).astype(BF16)
        part = sum(jnp.dot(x, pick, preferred_element_type=F32) for x in (high, mid, low))
        columns[...] = part if place == 0 else columns[...] + part

    total = None
    for place in range(count):
        domain = domain_at(place)

        @pl.loop(0, slots)
        def _(k):
            hit = atoms[:1] == slot_ref[domain, k]
            rows = pl.ds(pl.multiple_of(k * rank, rank), rank)
            weights[rows, :] = jnp.where(hit, columns[...], 0.0)

        full = weights[...]
        high = full.astype(BF16)
        low = (full - high.astype(F32)).astype(BF16)
        block = coefs[place][...]
        term = jnp.dot(block, high, preferred_element_type=F32)
        term += jnp.dot(block, low, preferred_element_type=F32)
        total = term if total is None else total + term
    out_ref[...] = total.astype(out_ref.dtype)


def couple(slot_atom, coefs, couplings):
    width, flat = coefs[0].shape
    rank = couplings[0].shape[0]
    count = len(coefs)
    vmem = pl.BlockSpec(memory_space=pltpu.VMEM)
    return pl.pallas_call(
        functools.partial(couple_kernel, count, flat // rank),
        in_specs=[pl.BlockSpec(memory_space=pltpu.SMEM)] + [vmem] * (2 * count),
        out_specs=vmem,
        out_shape=jax.ShapeDtypeStruct((width, flat), BF16),
        scratch_shapes=[pltpu.VMEM((rank, flat), F32), pltpu.VMEM((flat, flat), F32)],
        cost_estimate=SMALL,
        name="couple",
    )(slot_atom, *coefs, *couplings)


def finish_kernel(rot_ref, k0, k1, k2, k3, x0, x1, x2, x3, proj_ref, *rest):
    out_ref, coupled, stack = rest[-3:]
    width = x0.shape[0]

    @pl.when(pl.program_id(0) == 0)
    def _():
        for s, ref in enumerate((k0, k1, k2, k3)):
            coupled[s * width : (s + 1) * width, :] = ref[...]
        mixed = jnp.dot(rot_ref[...], coupled[...], preferred_element_type=F32)
        coupled[:width, :] = mixed.astype(BF16)

    for s, ref in enumerate((x0, x1, x2, x3)):
        stack[s * width : (s + 1) * width, :] = ref[...]
    rotated = jnp.dot(rot_ref[...], stack[...], preferred_element_type=F32)
    applied = jnp.dot(coupled[:width, :], proj_ref[...], preferred_element_type=F32)
    out_ref[...] = (rotated.astype(BF16).astype(F32) + applied).astype(out_ref.dtype)


def finish(rotation, coupled, own, arrived, proj, start, so_far):
    width, points = own.shape
    flat = proj.shape[0]
    extent = arrived[0].shape[1]
    tile = tile_of(extent, 768)
    first = start // tile
    fixed = lambda g: (0, 0)
    here = pl.BlockSpec((width, tile), lambda g: (0, g))
    there = pl.BlockSpec((width, tile), lambda g: (0, first + g))
    args = [rotation, *coupled, own, *arrived, proj]
    specs = [pl.BlockSpec(rotation.shape, fixed)] + [pl.BlockSpec((width, flat), fixed)] * 4
    specs += [there] + [here] * 3 + [pl.BlockSpec((flat, tile), lambda g: (0, first + g))]
    alias = {}
    if so_far is not None:
        alias = {len(args): 0}
        args.append(so_far)
        specs.append(pl.BlockSpec(memory_space=pl.ANY))
    return pl.pallas_call(
        finish_kernel,
        grid=(extent // tile,),
        in_specs=specs,
        out_specs=there,
        out_shape=jax.ShapeDtypeStruct((width, points), BF16),
        scratch_shapes=[pltpu.VMEM((4 * width, flat), BF16), pltpu.VMEM((4 * width, tile), BF16)],
        input_output_aliases=alias,
        cost_estimate=SMALL,
        name="finish",
    )(*args)


def three_before(block, even):
    two = passed_along(block, 2)
    one = swapped(jnp.where(even, block, two))
    three = passed_along(two, 1)
    return one, two, three


def on_device(orbitals, rotation, projectors, coupling, slot_atom):
    width, points = orbitals.shape
    slot_count, proj_count, _ = projectors.shape
    proj = projectors.reshape(slot_count * proj_count, points)
    step = points // PARTS
    even = lax.axis_index("band") % 2 == 0

    parts = [
        three_before(orbitals[:, j * step : (j + 1) * step], even) for j in range(PARTS)
    ]
    own_coupling = coupling.transpose(2, 0, 1).reshape(proj_count, -1)
    couplings = from_all_domains(own_coupling)
    coefs = from_all_domains(project(orbitals, proj))
    mine = couple(slot_atom, coefs, couplings)
    coupled = [mine, *three_before(mine, even)]
    out = None
    for j in range(PARTS):
        out = finish(rotation, coupled, orbitals, parts[j], proj, j * step, out)
    return out


def solution(mesh):
    in_specs = (P("band", "dom"), P("band", None), P(None, None, "dom"), P("dom", None, None), P())
    out_specs = P("band", "dom")
    return jax.shard_map(
        on_device, mesh=mesh, in_specs=in_specs, out_specs=out_specs, check_vma=False
    )
```

```python
import functools

import jax
import jax.numpy as jnp
from jax import lax
from jax.experimental import pallas as pl
from jax.experimental.pallas import tpu as pltpu
from jax.sharding import PartitionSpec as P

F32 = jnp.float32
BF16 = jnp.bfloat16
SMALL = pl.CostEstimate(flops=0, bytes_accessed=0, transcendentals=0)
ROOM = pltpu.CompilerParams(vmem_limit_bytes=8 * 2**20)
NT = (((1,), (1,)), ((), ()))
VMEM = pl.BlockSpec(memory_space=pltpu.VMEM)
SMEM = pl.BlockSpec(memory_space=pltpu.SMEM)


def call(kernel, name, outs, args, scratch=(), first=VMEM):
    shapes = [jax.ShapeDtypeStruct(*o) for o in outs]
    return pl.pallas_call(
        kernel,
        in_specs=[first] + [VMEM] * (len(args) - 1),
        out_specs=[VMEM] * len(outs),
        out_shape=shapes,
        scratch_shapes=list(scratch),
        compiler_params=ROOM,
        cost_estimate=SMALL,
        name=name,
    )(*args)


def along_bands(block, distance, senders=(0, 1)):
    count = lax.axis_size("band")
    route = [(i, (i + distance) % count) for i in range(count) if i % 2 in senders]
    return lax.ppermute(block, "band", route)


def swapped(block):
    count = lax.axis_size("band")
    return lax.ppermute(block, "band", [(i, i ^ 1) for i in range(count)])


def on_even():
    return lax.axis_index("band") % 2 == 0


def by_permutes():
    count = lax.axis_size("dom")
    return count <= 8 and count & (count - 1) == 0


def from_all_domains(block):
    count = lax.axis_size("dom")
    if by_permutes():
        routes = [[(i, i ^ mask) for i in range(count)] for mask in range(1, count)]
        return [block] + [lax.ppermute(block, "dom", route) for route in routes]
    whole = lax.all_gather(block, "dom")
    return [whole[d] for d in range(count)]


def domain_at(place):
    return lax.axis_index("dom") ^ place if by_permutes() else place


def tile_of(extent, most):
    return max(w for w in range(128, most + 1, 128) if extent % w == 0)


def project_kernel(orb_ref, proj_ref, coupling_ref, out_ref, copy_ref):
    width, points = orb_ref.shape
    flat = proj_ref.shape[0]
    rank, owned = coupling_ref.shape
    tile = tile_of(points, 1024)
    total = None
    for at in range(0, points, tile):
        term = lax.dot_general(
            proj_ref[:, at : at + tile], orb_ref[:, at : at + tile], NT, preferred_element_type=F32
        )
        total = term if total is None else total + term
    out_ref[:width, :] = total.T.astype(BF16)
    whole = coupling_ref[...]
    high = whole.astype(BF16)
    out_ref[width:, :owned] = high
    out_ref[width:, owned : 2 * owned] = (whole - high.astype(F32)).astype(BF16)
    copy_ref[...] = orb_ref[...]


def project(orbitals, proj, coupling):
    width, flat = orbitals.shape[0], proj.shape[0]
    outs = [((width + coupling.shape[0], flat), BF16), (orbitals.shape, BF16)]
    return call(project_kernel, "project", outs, [orbitals, proj, coupling])


def couple_kernel(count, slots, owned, slot_ref, *refs):
    loads = refs[:count]
    out_ref, pick, high_ref, low_ref = refs[count:]
    width, flat = out_ref.shape
    rank = flat // slots
    me = lax.axis_index("dom")
    lanes = lax.broadcasted_iota(jnp.int32, (rank, flat), 1)
    unit = lanes % rank == lax.broadcasted_iota(jnp.int32, (rank, flat), 0)
    lane_slot = lanes // rank

    atoms = jnp.zeros((rank, flat), jnp.int32)
    for k in range(slots):
        atoms = jnp.where(lane_slot == k, slot_ref[me, k], atoms)

    columns = None
    for place in range(count):
        owner = domain_at(place)
        for a in range(owned):
            hit = unit & (atoms == owner * owned + a)
            pick[a * rank : (a + 1) * rank, :] = jnp.where(hit, 1.0, 0.0).astype(BF16)
        parts = [loads[place][width:, i * owned * rank : (i + 1) * owned * rank] for i in (0, 1)]
        term = jnp.dot(jnp.concatenate(parts, 0), pick[...], preferred_element_type=F32)
        columns = term if columns is None else columns + term
    high, low = columns[:rank], columns[rank:]

    total = None
    for place in range(count):
        domain = domain_at(place)
        for k in range(slots):
            hit = atoms == slot_ref[domain, k]
            rows = slice(k * rank, (k + 1) * rank)
            high_ref[rows, :] = jnp.where(hit, high, 0.0).astype(BF16)
            low_ref[rows, :] = jnp.where(hit, low, 0.0).astype(BF16)
        block = loads[place][:width, :]
        term = jnp.dot(block, high_ref[...], preferred_element_type=F32)
        term += jnp.dot(block, low_ref[...], preferred_element_type=F32)
        total = term if total is None else total + term
    out_ref[...] = total.astype(BF16)


def couple(slot_atom, loads, width, owned):
    flat = loads[0].shape[1]
    slots = slot_atom.shape[1]
    return call(
        functools.partial(couple_kernel, len(loads), slots, owned),
        "couple",
        [((width, flat), BF16)],
        [slot_atom, *loads],
        [
            pltpu.VMEM((owned * (flat // slots), flat), BF16),
            pltpu.VMEM((flat, flat), BF16),
            pltpu.VMEM((flat, flat), BF16),
        ],
        first=SMEM,
    )[0]


def choose_kernel(even_ref, odd_ref, after_ref, out_ref):
    @pl.when(on_even())
    def _():
        out_ref[...] = even_ref[...]

    @pl.when(jnp.logical_not(on_even()))
    def _():
        out_ref[...] = odd_ref[...]


def choose(for_even, for_odd, after):
    return call(
        choose_kernel, "choose", [(for_even.shape, for_even.dtype)], [for_even, for_odd, after]
    )[0]


def by_distance(rot_ref, width):
    tiles = [rot_ref[:, s * width : (s + 1) * width] for s in range(4)]
    even = on_even()
    one, three = tiles[1].astype(F32), tiles[3].astype(F32)
    by_swap = jnp.where(even, one, three).astype(BF16)
    by_ring = jnp.where(even, three, one).astype(BF16)
    return [tiles[0], by_swap, tiles[2], by_ring]


def apply_kernel(rot_ref, mine, one, two, three, proj_ref, out_ref):
    width, flat = mine.shape
    points = proj_ref.shape[1]
    mixed = None
    blocks = [mine, one, two, three]
    for s, block in enumerate(blocks):
        term = jnp.dot(
            rot_ref[:, s * width : (s + 1) * width], block[...], preferred_element_type=F32
        )
        mixed = term if mixed is None else mixed + term
    mixed = mixed.astype(BF16)
    tile = tile_of(points, 1024)
    for at in range(0, points, tile):
        out_ref[:, at : at + tile] = jnp.dot(
            mixed, proj_ref[:, at : at + tile], preferred_element_type=F32
        )


def finish_kernel(rot_ref, own, swap, two, ring, applied, out_ref, stack):
    width, tile = out_ref.shape
    at = pl.multiple_of(pl.program_id(0) * tile, tile)
    for s, ref in enumerate((own, swap, two, ring)):
        stack[s * width : (s + 1) * width, :] = ref[:, pl.ds(at, tile)]
    turn = jnp.concatenate(by_distance(rot_ref, width), axis=1)
    rotated = jnp.dot(turn, stack[...], preferred_element_type=F32)
    added = rotated.astype(BF16).astype(F32) + applied[:, pl.ds(at, tile)]
    out_ref[...] = added.astype(out_ref.dtype)


def finish(args):
    width, points = args[1].shape
    tile = tile_of(points, 1536)
    return pl.pallas_call(
        finish_kernel,
        grid=(points // tile,),
        in_specs=[VMEM] * len(args),
        out_specs=pl.BlockSpec((width, tile), lambda g: (0, g)),
        out_shape=jax.ShapeDtypeStruct((width, points), BF16),
        scratch_shapes=[pltpu.VMEM((4 * width, tile), BF16)],
        compiler_params=ROOM,
        cost_estimate=SMALL,
        name="finish",
    )(*args)


def on_device(orbitals, rotation, projectors, coupling, slot_atom):
    width, points = orbitals.shape
    slot_count, rank, _ = projectors.shape
    owned = coupling.shape[0]
    proj = projectors.reshape(slot_count * rank, points)
    turned = coupling.transpose(2, 0, 1).reshape(rank, owned * rank)

    two_odd = along_bands(orbitals, 2, (1,))
    load, own = project(orbitals, proj, turned)
    loads = from_all_domains(load)
    two_even = along_bands(own, 2, (0,))
    mine = couple(slot_atom, loads, width, owned)
    mine_two = along_bands(mine, 2)
    chosen = choose(own, two_odd, mine)
    ring = along_bands(chosen, 1)
    mine_three = along_bands(mine_two, 1)
    mine_one = swapped(choose(mine, mine_two, chosen))
    applied = call(
        apply_kernel,
        "apply",
        [((width, points), F32)],
        [rotation, mine, mine_one, mine_two, mine_three, proj],
    )[0]
    two = choose(two_even, two_odd, applied)
    swap = swapped(two)
    return finish([rotation, own, swap, two, ring, applied])


def solution(mesh):
    in_specs = (P("band", "dom"), P("band", None), P(None, None, "dom"), P("dom", None, None), P())
    out_specs = P("band", "dom")
    return jax.shard_map(
        on_device, mesh=mesh, in_specs=in_specs, out_specs=out_specs, check_vma=False
    )
```

```python
import functools

import jax
import jax.numpy as jnp
from jax import lax
from jax.experimental import pallas as pl
from jax.experimental.pallas import tpu as pltpu
from jax.sharding import PartitionSpec as P

PIECES = 4
F32 = jnp.float32
BF16 = jnp.bfloat16
SMALL = pl.CostEstimate(flops=0, bytes_accessed=0, transcendentals=0)
ROOM = pltpu.CompilerParams(vmem_limit_bytes=8 * 2**20)
NT = (((1,), (1,)), ((), ()))
VMEM = pl.BlockSpec(memory_space=pltpu.VMEM)
SMEM = pl.BlockSpec(memory_space=pltpu.SMEM)


def call(kernel, name, outs, args, scratch=(), first=VMEM, cost=SMALL):
    shapes = [jax.ShapeDtypeStruct(*o) for o in outs]
    return pl.pallas_call(
        kernel,
        in_specs=[first] + [VMEM] * (len(args) - 1),
        out_specs=[VMEM] * len(outs),
        out_shape=shapes,
        scratch_shapes=list(scratch),
        compiler_params=ROOM,
        cost_estimate=cost,
        name=name,
    )(*args)


def along_bands(block, distance, senders=(0, 1)):
    count = lax.axis_size("band")
    route = [(i, (i + distance) % count) for i in range(count) if i % 2 in senders]
    return lax.ppermute(block, "band", route)


def swapped(block):
    count = lax.axis_size("band")
    return lax.ppermute(block, "band", [(i, i ^ 1) for i in range(count)])


def on_even():
    return lax.axis_index("band") % 2 == 0


def by_permutes():
    count = lax.axis_size("dom")
    return count <= 8 and count & (count - 1) == 0


def from_all_domains(block):
    count = lax.axis_size("dom")
    if by_permutes():
        routes = [[(i, i ^ mask) for i in range(count)] for mask in range(1, count)]
        return [block] + [lax.ppermute(block, "dom", route) for route in routes]
    whole = lax.all_gather(block, "dom")
    return [whole[d] for d in range(count)]


def domain_at(place):
    return lax.axis_index("dom") ^ place if by_permutes() else place


def tile_of(extent, most):
    return max(w for w in range(128, most + 1, 128) if extent % w == 0)


def project_kernel(orb_hbm, proj_hbm, coupling_ref, out_ref, orb_ref, proj_ref, orb_sems, sems):
    width, points = orb_ref.shape
    owned, rank = coupling_ref.shape
    tile = tile_of(points, 1024)
    copies = []
    for i in range(points // tile):
        part = (slice(None), pl.ds(i * tile, tile))
        copies.append(
            (
                pltpu.make_async_copy(orb_hbm.at[part], orb_ref.at[part], orb_sems.at[i]),
                pltpu.make_async_copy(proj_hbm.at[part], proj_ref.at[part], sems.at[i]),
            )
        )
        for copy in copies[-1]:
            copy.start()

    whole = coupling_ref[...]
    high = whole.astype(BF16)
    unit = lax.broadcasted_iota(jnp.int32, (rank, rank), 0) == lax.broadcasted_iota(
        jnp.int32, (rank, rank), 1
    )
    unit = jnp.where(unit, 1.0, 0.0).astype(BF16)
    for i, piece in enumerate((high, (whole - high.astype(F32)).astype(BF16))):
        turned = lax.dot_general(unit, piece, NT, preferred_element_type=F32)
        out_ref[width:, i * owned : (i + 1) * owned] = turned.astype(BF16)

    total = None
    for i, pair in enumerate(copies):
        for copy in pair:
            copy.wait()
        part = slice(i * tile, (i + 1) * tile)
        term = lax.dot_general(
            proj_ref[:, part], orb_ref[:, part], NT, preferred_element_type=F32
        )
        total = term if total is None else total + term
    out_ref[:width, :] = total.T.astype(BF16)


def project(orbitals, proj, coupling):
    width, points = orbitals.shape
    flat = proj.shape[0]
    rank = coupling.shape[1]
    pieces = points // tile_of(points, 1024)
    shapes = [((width + rank, flat), BF16), (orbitals.shape, BF16)]
    return pl.pallas_call(
        project_kernel,
        in_specs=[pl.BlockSpec(memory_space=pl.ANY)] * 2 + [VMEM],
        out_specs=[VMEM] * 2,
        out_shape=[jax.ShapeDtypeStruct(*shape) for shape in shapes],
        scratch_shapes=[pltpu.VMEM(proj.shape, BF16)] + [pltpu.SemaphoreType.DMA((pieces,))] * 2,
        compiler_params=pltpu.CompilerParams(vmem_limit_bytes=56 * 2**20),
        cost_estimate=SMALL,
        name="project",
    )(orbitals, proj, coupling)


def couple_kernel(count, slots, owned, slot_ref, *refs):
    loads = refs[:count]
    out_ref, pick, high_ref, low_ref = refs[count:]
    width, flat = out_ref.shape
    rank = flat // slots
    me = lax.axis_index("dom")
    lanes = lax.broadcasted_iota(jnp.int32, (rank, flat), 1)
    unit = lanes % rank == lax.broadcasted_iota(jnp.int32, (rank, flat), 0)
    lane_slot = lanes // rank

    atoms = jnp.zeros((rank, flat), jnp.int32)
    for k in range(slots):
        atoms = jnp.where(lane_slot == k, slot_ref[me, k], atoms)

    columns = None
    for place in range(count):
        owner = domain_at(place)
        for a in range(owned):
            hit = unit & (atoms == owner * owned + a)
            pick[a * rank : (a + 1) * rank, :] = jnp.where(hit, 1.0, 0.0).astype(BF16)
        parts = [loads[place][width:, i * owned * rank : (i + 1) * owned * rank] for i in (0, 1)]
        term = jnp.dot(jnp.concatenate(parts, 0), pick[...], preferred_element_type=F32)
        columns = term if columns is None else columns + term
    high, low = columns[:rank], columns[rank:]

    total = None
    for place in range(count):
        domain = domain_at(place)
        for k in range(slots):
            hit = atoms == slot_ref[domain, k]
            rows = slice(k * rank, (k + 1) * rank)
            high_ref[rows, :] = jnp.where(hit, high, 0.0).astype(BF16)
            low_ref[rows, :] = jnp.where(hit, low, 0.0).astype(BF16)
        block = loads[place][:width, :]
        term = jnp.dot(block, high_ref[...], preferred_element_type=F32)
        term += jnp.dot(block, low_ref[...], preferred_element_type=F32)
        total = term if total is None else total + term
    out_ref[...] = total.astype(BF16)


def couple(slot_atom, loads, width, owned):
    flat = loads[0].shape[1]
    slots = slot_atom.shape[1]
    return call(
        functools.partial(couple_kernel, len(loads), slots, owned),
        "couple",
        [((width, flat), BF16)],
        [slot_atom, *loads],
        [
            pltpu.VMEM((owned * (flat // slots), flat), BF16),
            pltpu.VMEM((flat, flat), BF16),
            pltpu.VMEM((flat, flat), BF16),
        ],
        first=SMEM,
        cost=pl.CostEstimate(flops=2 * 10**9, bytes_accessed=0, transcendentals=0),
    )[0]


def choose_kernel(even_ref, odd_ref, pass_ref, passed_ref, *out_refs):
    tile = out_refs[0].shape[1]
    for i, out_ref in enumerate(out_refs):
        part = slice(i * tile, (i + 1) * tile)

        @pl.when(on_even())
        def _():
            out_ref[...] = even_ref[:, part]

        @pl.when(jnp.logical_not(on_even()))
        def _():
            out_ref[...] = odd_ref[:, part]

    passed_ref[...] = pass_ref[...]


def choose(for_even, for_odd, passed, pieces=1):
    width, points = for_even.shape
    outs = [(passed.shape, passed.dtype)]
    outs += [((width, points // pieces), for_even.dtype)] * pieces
    passed, *chosen = call(choose_kernel, "choose", outs, [for_even, for_odd, passed])
    return chosen, passed


def by_distance(rot_ref, width):
    tiles = [rot_ref[:, s * width : (s + 1) * width] for s in range(4)]
    even = on_even()
    one, three = tiles[1].astype(F32), tiles[3].astype(F32)
    by_swap = jnp.where(even, one, three).astype(BF16)
    by_ring = jnp.where(even, three, one).astype(BF16)
    return [tiles[0], by_swap, tiles[2], by_ring]


def apply_kernel(rot_ref, mine, one, two, three, proj_ref, out_ref):
    width, flat = mine.shape
    points = proj_ref.shape[1]
    mixed = None
    blocks = [mine, one, two, three]
    for s, block in enumerate(blocks):
        term = jnp.dot(
            rot_ref[:, s * width : (s + 1) * width], block[...], preferred_element_type=F32
        )
        mixed = term if mixed is None else mixed + term
    mixed = mixed.astype(BF16)
    tile = tile_of(points, 1024)
    for at in range(0, points, tile):
        out_ref[:, at : at + tile] = jnp.dot(
            mixed, proj_ref[:, at : at + tile], preferred_element_type=F32
        )


def finish_kernel(pieces, rot_ref, own, *refs):
    swaps, twos = refs[:pieces], refs[pieces : 2 * pieces]
    ring, applied, out_ref, stack = refs[2 * pieces :]
    width, points = own.shape
    tile = points // pieces
    turn = jnp.concatenate(by_distance(rot_ref, width), axis=1)
    for i in range(pieces):

        @pl.when(pl.program_id(0) == i)
        def _():
            part = slice(i * tile, (i + 1) * tile)
            blocks = (own[:, part], swaps[i][...], twos[i][...], ring[:, part])
            for s, block in enumerate(blocks):
                stack[s * width : (s + 1) * width, :] = block
            rotated = jnp.dot(turn, stack[...], preferred_element_type=F32)
            added = rotated.astype(BF16).astype(F32) + applied[:, part]
            out_ref[...] = added.astype(out_ref.dtype)


def finish(rotation, own, swaps, twos, ring, applied):
    width, points = own.shape
    pieces = len(swaps)
    tile = points // pieces
    args = [rotation, own, *swaps, *twos, ring, applied]
    return pl.pallas_call(
        functools.partial(finish_kernel, pieces),
        grid=(pieces,),
        in_specs=[VMEM] * len(args),
        out_specs=pl.BlockSpec((width, tile), lambda g: (0, g)),
        out_shape=jax.ShapeDtypeStruct((width, points), BF16),
        scratch_shapes=[pltpu.VMEM((4 * width, tile), BF16)],
        compiler_params=ROOM,
        cost_estimate=SMALL,
        name="finish",
    )(*args)


def on_device(orbitals, rotation, projectors, coupling, slot_atom):
    width, points = orbitals.shape
    slot_count, rank, _ = projectors.shape
    owned = coupling.shape[0]
    proj = projectors.reshape(slot_count * rank, points)

    two_odd = along_bands(orbitals, 2, (1,))
    load, own = project(orbitals, proj, coupling.reshape(owned * rank, rank))
    loads = from_all_domains(load)
    two_even = along_bands(own, 2, (0,))
    mine = couple(slot_atom, loads, width, owned)
    chosen, mine = choose(own, two_odd, mine)
    ring = along_bands(chosen[0], 1)
    mine_two = along_bands(mine, 2)
    mine_three = along_bands(mine_two, 1)
    mine_one = swapped(choose(mine, mine_two, mine)[0][0])
    applied = call(
        apply_kernel,
        "apply",
        [((width, points), F32)],
        [rotation, mine, mine_one, mine_two, mine_three, proj],
    )[0]
    twos, applied = choose(two_even, two_odd, applied, PIECES)
    swaps = [swapped(two) for two in twos]
    return finish(rotation, own, swaps, twos, ring, applied)


def solution(mesh):
    in_specs = (P("band", "dom"), P("band", None), P(None, None, "dom"), P("dom", None, None), P())
    out_specs = P("band", "dom")
    return jax.shard_map(
        on_device, mesh=mesh, in_specs=in_specs, out_specs=out_specs, check_vma=False
    )
```

```python
import functools

import jax
import jax.numpy as jnp
from jax import lax
from jax.experimental import pallas as pl
from jax.experimental.pallas import tpu as pltpu
from jax.sharding import PartitionSpec as P

F32 = jnp.float32
BF16 = jnp.bfloat16
SMALL = pl.CostEstimate(flops=0, bytes_accessed=0, transcendentals=0)
ROOM = pltpu.CompilerParams(vmem_limit_bytes=8 * 2**20)
NT = (((1,), (1,)), ((), ()))
VMEM = pl.BlockSpec(memory_space=pltpu.VMEM)
SMEM = pl.BlockSpec(memory_space=pltpu.SMEM)


def call(kernel, name, outs, args, scratch=(), first=VMEM, cost=SMALL):
    shapes = [jax.ShapeDtypeStruct(*o) for o in outs]
    return pl.pallas_call(
        kernel,
        in_specs=[first] + [VMEM] * (len(args) - 1),
        out_specs=[VMEM] * len(outs),
        out_shape=shapes,
        scratch_shapes=list(scratch),
        compiler_params=ROOM,
        cost_estimate=cost,
        name=name,
    )(*args)


def along_bands(block, distance, senders=(0, 1)):
    count = lax.axis_size("band")
    route = [(i, (i + distance) % count) for i in range(count) if i % 2 in senders]
    return lax.ppermute(block, "band", route)


def swapped(block):
    count = lax.axis_size("band")
    return lax.ppermute(block, "band", [(i, i ^ 1) for i in range(count)])


def on_even():
    return lax.axis_index("band") % 2 == 0


def by_permutes():
    count = lax.axis_size("dom")
    return count <= 8 and count & (count - 1) == 0


def from_all_domains(block):
    count = lax.axis_size("dom")
    if by_permutes():
        routes = [[(i, i ^ mask) for i in range(count)] for mask in range(1, count)]
        return [block] + [lax.ppermute(block, "dom", route) for route in routes]
    whole = lax.all_gather(block, "dom")
    return [whole[d] for d in range(count)]


def domain_at(place):
    return lax.axis_index("dom") ^ place if by_permutes() else place


def tile_of(extent, most):
    return max(w for w in range(128, most + 1, 128) if extent % w == 0)


def parts_of(points):
    part = points // 3
    return (points - part, part) if part % 128 == 0 else (points // 2, points // 2)


def project_kernel(pieces, orb_hbm, proj_hbm, coupling_ref, out_ref, *refs):
    own_refs, (orb_ref, proj_ref, orb_sem, sems) = refs[:-4], refs[-4:]
    width, points = orb_ref.shape
    flat = proj_ref.shape[0]
    owned, rank = coupling_ref.shape
    tall = flat // pieces
    fetch_orb = pltpu.make_async_copy(orb_hbm, orb_ref, orb_sem)
    fetch_orb.start()
    fetches = []
    for i in range(pieces):
        rows = pl.ds(i * tall, tall)
        fetches.append(pltpu.make_async_copy(proj_hbm.at[rows], proj_ref.at[rows], sems.at[i]))
        fetches[-1].start()

    whole = coupling_ref[...]
    high = whole.astype(BF16)
    unit = lax.broadcasted_iota(jnp.int32, (rank, rank), 0) == lax.broadcasted_iota(
        jnp.int32, (rank, rank), 1
    )
    unit = jnp.where(unit, 1.0, 0.0).astype(BF16)
    for i, piece in enumerate((high, (whole - high.astype(F32)).astype(BF16))):
        turned = lax.dot_general(unit, piece, NT, preferred_element_type=F32)
        out_ref[width:, i * owned : (i + 1) * owned] = turned.astype(BF16)

    fetch_orb.wait()
    at = 0
    for own_ref in own_refs:
        own_ref[...] = orb_ref[:, at : at + own_ref.shape[1]]
        at += own_ref.shape[1]
    for i, fetch in enumerate(fetches):
        fetch.wait()
        rows = slice(i * tall, (i + 1) * tall)
        part = lax.dot_general(proj_ref[rows, :], orb_ref[...], NT, preferred_element_type=F32)
        out_ref[:width, rows] = part.T.astype(BF16)


def project(orbitals, proj, coupling):
    width, points = orbitals.shape
    flat = proj.shape[0]
    rank = coupling.shape[1]
    pieces = 4 if flat % 512 == 0 else 1
    shapes = [((width + rank, flat), BF16)]
    shapes += [((width, extent), BF16) for extent in parts_of(points)]
    return pl.pallas_call(
        functools.partial(project_kernel, pieces),
        in_specs=[pl.BlockSpec(memory_space=pl.ANY)] * 2 + [VMEM],
        out_specs=[VMEM] * len(shapes),
        out_shape=[jax.ShapeDtypeStruct(*shape) for shape in shapes],
        scratch_shapes=[
            pltpu.VMEM(orbitals.shape, BF16),
            pltpu.VMEM(proj.shape, BF16),
            pltpu.SemaphoreType.DMA,
            pltpu.SemaphoreType.DMA((pieces,)),
        ],
        compiler_params=pltpu.CompilerParams(vmem_limit_bytes=52 * 2**20),
        cost_estimate=SMALL,
        name="project",
    )(orbitals, proj, coupling)


def couple_kernel(count, slots, owned, slot_ref, *refs):
    loads, pass_ref = refs[:count], refs[count]
    out_ref, passed_ref, pick, high_ref, low_ref = refs[count + 1 :]
    passed_ref[...] = pass_ref[...]
    width, flat = out_ref.shape
    rank = flat // slots
    me = lax.axis_index("dom")
    lanes = lax.broadcasted_iota(jnp.int32, (rank, flat), 1)
    unit = lanes % rank == lax.broadcasted_iota(jnp.int32, (rank, flat), 0)
    lane_slot = lanes // rank

    atoms = jnp.zeros((rank, flat), jnp.int32)
    for k in range(slots):
        atoms = jnp.where(lane_slot == k, slot_ref[me, k], atoms)

    columns = None
    for place in range(count):
        owner = domain_at(place)
        for a in range(owned):
            hit = unit & (atoms == owner * owned + a)
            pick[a * rank : (a + 1) * rank, :] = jnp.where(hit, 1.0, 0.0).astype(BF16)
        parts = [loads[place][width:, i * owned * rank : (i + 1) * owned * rank] for i in (0, 1)]
        term = jnp.dot(jnp.concatenate(parts, 0), pick[...], preferred_element_type=F32)
        columns = term if columns is None else columns + term
    high, low = columns[:rank], columns[rank:]

    total = None
    for place in range(count):
        domain = domain_at(place)
        for k in range(slots):
            hit = atoms == slot_ref[domain, k]
            rows = slice(k * rank, (k + 1) * rank)
            high_ref[rows, :] = jnp.where(hit, high, 0.0).astype(BF16)
            low_ref[rows, :] = jnp.where(hit, low, 0.0).astype(BF16)
        block = loads[place][:width, :]
        term = jnp.dot(block, high_ref[...], preferred_element_type=F32)
        term += jnp.dot(block, low_ref[...], preferred_element_type=F32)
        total = term if total is None else total + term
    out_ref[...] = total.astype(BF16)


def couple(slot_atom, loads, width, owned, passed):
    flat = loads[0].shape[1]
    slots = slot_atom.shape[1]
    return call(
        functools.partial(couple_kernel, len(loads), slots, owned),
        "couple",
        [((width, flat), BF16), (passed.shape, passed.dtype)],
        [slot_atom, *loads, passed],
        [
            pltpu.VMEM((owned * (flat // slots), flat), BF16),
            pltpu.VMEM((flat, flat), BF16),
            pltpu.VMEM((flat, flat), BF16),
        ],
        first=SMEM,
        cost=pl.CostEstimate(flops=2 * 10**9, bytes_accessed=0, transcendentals=0),
    )


def choose_kernel(pairs, *refs):
    outs = refs[-len(pairs) :]
    for out_ref, (i, j, place) in zip(outs, pairs):
        part = slice(place, place + out_ref.shape[1])

        @pl.when(on_even())
        def _():
            out_ref[...] = refs[i][...]

        @pl.when(jnp.logical_not(on_even()))
        def _():
            out_ref[...] = refs[j][:, part]


def choose(evens, odd, *after):
    starts = [sum(x.shape[1] for x in evens[:i]) for i in range(len(evens))]
    pairs = [(i, len(evens), start) for i, start in enumerate(starts)]
    outs = [(x.shape, x.dtype) for x in evens]
    return call(
        functools.partial(choose_kernel, pairs), "choose", outs, [*evens, odd, *after]
    )


def by_distance(rot_ref, width):
    tiles = [rot_ref[:, s * width : (s + 1) * width] for s in range(4)]
    even = on_even()
    one, three = tiles[1].astype(F32), tiles[3].astype(F32)
    by_swap = jnp.where(even, one, three).astype(BF16)
    by_ring = jnp.where(even, three, one).astype(BF16)
    return [tiles[0], by_swap, tiles[2], by_ring]


def apply_kernel(rot_ref, mine, one, two, three, proj_ref, out_ref):
    width, flat = mine.shape
    points = proj_ref.shape[1]
    mixed = None
    blocks = [mine, one, two, three]
    for s, block in enumerate(blocks):
        term = jnp.dot(
            rot_ref[:, s * width : (s + 1) * width], block[...], preferred_element_type=F32
        )
        mixed = term if mixed is None else mixed + term
    mixed = mixed.astype(BF16)
    tile = tile_of(points, 1024)
    for at in range(0, points, tile):
        out_ref[:, at : at + tile] = jnp.dot(
            mixed, proj_ref[:, at : at + tile], preferred_element_type=F32
        )


def finish_kernel(start, rot_ref, own, swap, two, ring, applied, *rest):
    out_ref, stack = rest[-2:]
    width, tile = out_ref.shape
    at = pl.multiple_of(pl.program_id(0) * tile, tile)
    here = pl.ds(at, tile)
    for s, ref in enumerate((own, swap, two, ring)):
        stack[s * width : (s + 1) * width, :] = ref[:, here]
    turn = jnp.concatenate(by_distance(rot_ref, width), axis=1)
    rotated = jnp.dot(turn, stack[...], preferred_element_type=F32)
    there = pl.ds(pl.multiple_of(start + at, tile), tile)
    added = rotated.astype(BF16).astype(F32) + applied[:, there]
    out_ref[...] = added.astype(out_ref.dtype)


def finish(rotation, own, swap, two, ring, applied, start, so_far):
    width, points = applied.shape
    tile = tile_of(own.shape[1], 1024)
    args = [rotation, own, swap, two, ring, applied]
    specs = [VMEM] * len(args)
    alias = {}
    if so_far is not None:
        alias = {len(args): 0}
        args.append(so_far)
        specs.append(pl.BlockSpec(memory_space=pl.ANY))
    return pl.pallas_call(
        functools.partial(finish_kernel, start),
        grid=(own.shape[1] // tile,),
        in_specs=specs,
        out_specs=pl.BlockSpec((width, tile), lambda g: (0, start // tile + g)),
        out_shape=jax.ShapeDtypeStruct((width, points), BF16),
        scratch_shapes=[pltpu.VMEM((4 * width, tile), BF16)],
        input_output_aliases=alias,
        compiler_params=ROOM,
        cost_estimate=SMALL,
        name="finish",
    )(*args)


def on_device(orbitals, rotation, projectors, coupling, slot_atom):
    width, points = orbitals.shape
    slot_count, rank, _ = projectors.shape
    owned = coupling.shape[0]
    proj = projectors.reshape(slot_count * rank, points)

    two_odd = along_bands(orbitals, 2, (1,))
    load, *own = project(orbitals, proj, coupling.reshape(owned * rank, rank))
    loads = from_all_domains(load)
    two_even = [along_bands(own[0], 2, (0,))]
    mine, own[1] = couple(slot_atom, loads, width, owned, own[1])
    mine_two = along_bands(mine, 2)
    two_even.append(along_bands(own[1], 2, (0,)))
    chosen = choose(own, two_odd, mine)
    ring = [along_bands(block, 1) for block in chosen]
    mine_three = along_bands(mine_two, 1)
    mine_one = swapped(choose([mine], mine_two, chosen[0])[0])
    applied = call(
        apply_kernel,
        "apply",
        [((width, points), F32)],
        [rotation, mine, mine_one, mine_two, mine_three, proj],
        cost=pl.CostEstimate(flops=2 * 10**9, bytes_accessed=0, transcendentals=0),
    )[0]
    two = choose(two_even, two_odd, applied)
    swap = [swapped(block) for block in two]
    out, start = None, 0
    for i in range(len(own)):
        out = finish(rotation, own[i], swap[i], two[i], ring[i], applied, start, out)
        start += own[i].shape[1]
    return out


def solution(mesh):
    in_specs = (P("band", "dom"), P("band", None), P(None, None, "dom"), P("dom", None, None), P())
    out_specs = P("band", "dom")
    return jax.shard_map(
        on_device, mesh=mesh, in_specs=in_specs, out_specs=out_specs, check_vma=False
    )
```

```python
import functools

import jax
import jax.numpy as jnp
from jax import lax
from jax.experimental import pallas as pl
from jax.experimental.pallas import tpu as pltpu
from jax.sharding import PartitionSpec as P

TURN = 3 * 10**9
F32 = jnp.float32
BF16 = jnp.bfloat16
ROOM = pltpu.CompilerParams(vmem_limit_bytes=8 * 2**20)
NT = (((1,), (1,)), ((), ()))
VMEM = pl.BlockSpec(memory_space=pltpu.VMEM)
SMEM = pl.BlockSpec(memory_space=pltpu.SMEM)


def flops(count):
    return pl.CostEstimate(flops=count, bytes_accessed=0, transcendentals=0)


def call(kernel, name, outs, args, scratch=(), first=VMEM, cost=0):
    shapes = [jax.ShapeDtypeStruct(*o) for o in outs]
    return pl.pallas_call(
        kernel,
        in_specs=[first] + [VMEM] * (len(args) - 1),
        out_specs=[VMEM] * len(outs),
        out_shape=shapes,
        scratch_shapes=list(scratch),
        compiler_params=ROOM,
        cost_estimate=flops(cost),
        name=name,
    )(*args)


def along_bands(block, distance, senders=(0, 1)):
    count = lax.axis_size("band")
    route = [(i, (i + distance) % count) for i in range(count) if i % 2 in senders]
    return lax.ppermute(block, "band", route)


def swapped(block):
    count = lax.axis_size("band")
    return lax.ppermute(block, "band", [(i, i ^ 1) for i in range(count)])


def on_even():
    return lax.axis_index("band") % 2 == 0


def by_permutes():
    count = lax.axis_size("dom")
    return count <= 8 and count & (count - 1) == 0


def from_all_domains(block):
    count = lax.axis_size("dom")
    if by_permutes():
        routes = [[(i, i ^ mask) for i in range(count)] for mask in range(1, count)]
        return [block] + [lax.ppermute(block, "dom", route) for route in routes]
    whole = lax.all_gather(block, "dom")
    return [whole[d] for d in range(count)]


def domain_at(place):
    return lax.axis_index("dom") ^ place if by_permutes() else place


def tile_of(extent, most):
    return max(w for w in range(128, most + 1, 128) if extent % w == 0)


def parts_of(points):
    part = points // 3
    return (points - part, part) if part % 128 == 0 else (points // 2, points // 2)


def turn_kernel(coupling_ref, out_ref):
    owned, rank = coupling_ref.shape
    whole = coupling_ref[...]
    high = whole.astype(BF16)
    unit = lax.broadcasted_iota(jnp.int32, (rank, rank), 0) == lax.broadcasted_iota(
        jnp.int32, (rank, rank), 1
    )
    unit = jnp.where(unit, 1.0, 0.0).astype(BF16)
    for i, piece in enumerate((high, (whole - high.astype(F32)).astype(BF16))):
        turned = lax.dot_general(unit, piece, NT, preferred_element_type=F32)
        out_ref[:, i * owned : (i + 1) * owned] = turned.astype(BF16)


def project_kernel(orb_ref, proj_ref, turned_ref, out_ref, *own_refs):
    width, points = orb_ref.shape
    out_ref[width:, : turned_ref.shape[1]] = turned_ref[...]
    at = 0
    for own_ref in own_refs:
        own_ref[...] = orb_ref[:, at : at + own_ref.shape[1]]
        at += own_ref.shape[1]
    tile = tile_of(points, 1024)
    total = None
    for at in range(0, points, tile):
        term = lax.dot_general(
            proj_ref[:, at : at + tile], orb_ref[:, at : at + tile], NT, preferred_element_type=F32
        )
        total = term if total is None else total + term
    out_ref[:width, :] = total.T.astype(BF16)


def project(orbitals, proj, coupling):
    width, points = orbitals.shape
    owned, rank = coupling.shape
    turned = call(
        turn_kernel, "turn", [((rank, 2 * owned), BF16)], [coupling], cost=TURN
    )[0]
    outs = [((width + rank, proj.shape[0]), BF16)]
    outs += [((width, extent), BF16) for extent in parts_of(points)]
    return call(project_kernel, "project", outs, [orbitals, proj, turned])


def couple_kernel(count, slots, owned, slot_ref, *refs):
    loads, pass_ref = refs[:count], refs[count]
    out_ref, passed_ref, pick, high_ref, low_ref = refs[count + 1 :]
    passed_ref[...] = pass_ref[...]
    width, flat = out_ref.shape
    rank = flat // slots
    me = lax.axis_index("dom")
    lanes = lax.broadcasted_iota(jnp.int32, (rank, flat), 1)
    unit = lanes % rank == lax.broadcasted_iota(jnp.int32, (rank, flat), 0)
    lane_slot = lanes // rank

    atoms = jnp.zeros((rank, flat), jnp.int32)
    for k in range(slots):
        atoms = jnp.where(lane_slot == k, slot_ref[me, k], atoms)

    columns = None
    for place in range(count):
        owner = domain_at(place)
        for a in range(owned):
            hit = unit & (atoms == owner * owned + a)
            pick[a * rank : (a + 1) * rank, :] = jnp.where(hit, 1.0, 0.0).astype(BF16)
        parts = [loads[place][width:, i * owned * rank : (i + 1) * owned * rank] for i in (0, 1)]
        term = jnp.dot(jnp.concatenate(parts, 0), pick[...], preferred_element_type=F32)
        columns = term if columns is None else columns + term
    high, low = columns[:rank], columns[rank:]

    total = None
    for place in range(count):
        domain = domain_at(place)
        for k in range(slots):
            hit = atoms == slot_ref[domain, k]
            rows = slice(k * rank, (k + 1) * rank)
            high_ref[rows, :] = jnp.where(hit, high, 0.0).astype(BF16)
            low_ref[rows, :] = jnp.where(hit, low, 0.0).astype(BF16)
        block = loads[place][:width, :]
        term = jnp.dot(block, high_ref[...], preferred_element_type=F32)
        term += jnp.dot(block, low_ref[...], preferred_element_type=F32)
        total = term if total is None else total + term
    out_ref[...] = total.astype(BF16)


def couple(slot_atom, loads, width, owned, passed):
    flat = loads[0].shape[1]
    slots = slot_atom.shape[1]
    return call(
        functools.partial(couple_kernel, len(loads), slots, owned),
        "couple",
        [((width, flat), BF16), (passed.shape, passed.dtype)],
        [slot_atom, *loads, passed],
        [
            pltpu.VMEM((owned * (flat // slots), flat), BF16),
            pltpu.VMEM((flat, flat), BF16),
            pltpu.VMEM((flat, flat), BF16),
        ],
        first=SMEM,
        cost=2 * 10**9,
    )


def choose_kernel(pairs, *refs):
    outs = refs[-len(pairs) :]
    for out_ref, (i, j, place) in zip(outs, pairs):
        part = slice(place, place + out_ref.shape[1])

        @pl.when(on_even())
        def _():
            out_ref[...] = refs[i][...]

        @pl.when(jnp.logical_not(on_even()))
        def _():
            out_ref[...] = refs[j][:, part]


def choose(evens, odd, *after):
    starts = [sum(x.shape[1] for x in evens[:i]) for i in range(len(evens))]
    pairs = [(i, len(evens), start) for i, start in enumerate(starts)]
    outs = [(x.shape, x.dtype) for x in evens]
    return call(
        functools.partial(choose_kernel, pairs), "choose", outs, [*evens, odd, *after]
    )


def by_distance(rot_ref, width):
    tiles = [rot_ref[:, s * width : (s + 1) * width] for s in range(4)]
    even = on_even()
    one, three = tiles[1].astype(F32), tiles[3].astype(F32)
    by_swap = jnp.where(even, one, three).astype(BF16)
    by_ring = jnp.where(even, three, one).astype(BF16)
    return [tiles[0], by_swap, tiles[2], by_ring]


def apply_kernel(rot_ref, mine, one, two, three, proj_ref, out_ref):
    width, flat = mine.shape
    points = proj_ref.shape[1]
    mixed = None
    blocks = [mine, one, two, three]
    for s, block in enumerate(blocks):
        term = jnp.dot(
            rot_ref[:, s * width : (s + 1) * width], block[...], preferred_element_type=F32
        )
        mixed = term if mixed is None else mixed + term
    mixed = mixed.astype(BF16)
    tile = tile_of(points, 1024)
    for at in range(0, points, tile):
        out_ref[:, at : at + tile] = jnp.dot(
            mixed, proj_ref[:, at : at + tile], preferred_element_type=F32
        )


def finish_kernel(start, rot_ref, own, swap, two, ring, applied, *rest):
    out_ref, stack = rest[-2:]
    width, tile = out_ref.shape
    at = pl.multiple_of(pl.program_id(0) * tile, tile)
    here = pl.ds(at, tile)
    for s, ref in enumerate((own, swap, two, ring)):
        stack[s * width : (s + 1) * width, :] = ref[:, here]
    turn = jnp.concatenate(by_distance(rot_ref, width), axis=1)
    rotated = jnp.dot(turn, stack[...], preferred_element_type=F32)
    there = pl.ds(pl.multiple_of(start + at, tile), tile)
    added = rotated.astype(BF16).astype(F32) + applied[:, there]
    out_ref[...] = added.astype(out_ref.dtype)


def finish(rotation, own, swap, two, ring, applied, start, so_far):
    width, points = applied.shape
    tile = tile_of(own.shape[1], 1024)
    args = [rotation, own, swap, two, ring, applied]
    specs = [VMEM] * len(args)
    alias = {}
    if so_far is not None:
        alias = {len(args): 0}
        args.append(so_far)
        specs.append(pl.BlockSpec(memory_space=pl.ANY))
    return pl.pallas_call(
        functools.partial(finish_kernel, start),
        grid=(own.shape[1] // tile,),
        in_specs=specs,
        out_specs=pl.BlockSpec((width, tile), lambda g: (0, start // tile + g)),
        out_shape=jax.ShapeDtypeStruct((width, points), BF16),
        scratch_shapes=[pltpu.VMEM((4 * width, tile), BF16)],
        input_output_aliases=alias,
        compiler_params=ROOM,
        cost_estimate=flops(0),
        name="finish",
    )(*args)


def on_device(orbitals, rotation, projectors, coupling, slot_atom):
    width, points = orbitals.shape
    slot_count, rank, _ = projectors.shape
    owned = coupling.shape[0]
    proj = projectors.reshape(slot_count * rank, points)

    two_odd = along_bands(orbitals, 2, (1,))
    load, *own = project(orbitals, proj, coupling.reshape(owned * rank, rank))
    loads = from_all_domains(load)
    two_even = [along_bands(own[0], 2, (0,))]
    mine, own[1] = couple(slot_atom, loads, width, owned, own[1])
    mine_two = along_bands(mine, 2)
    two_even.append(along_bands(own[1], 2, (0,)))
    chosen = choose(own, two_odd, mine)
    ring = [along_bands(block, 1) for block in chosen]
    mine_three = along_bands(mine_two, 1)
    mine_one = swapped(choose([mine], mine_two, chosen[0])[0])
    applied = call(
        apply_kernel,
        "apply",
        [((width, points), F32)],
        [rotation, mine, mine_one, mine_two, mine_three, proj],
        cost=2 * 10**9,
    )[0]
    two = choose(two_even, two_odd, applied)
    swap = [swapped(block) for block in two]
    out, start = None, 0
    for i in range(len(own)):
        out = finish(rotation, own[i], swap[i], two[i], ring[i], applied, start, out)
        start += own[i].shape[1]
    return out


def solution(mesh):
    in_specs = (P("band", "dom"), P("band", None), P(None, None, "dom"), P("dom", None, None), P())
    out_specs = P("band", "dom")
    return jax.shard_map(
        on_device, mesh=mesh, in_specs=in_specs, out_specs=out_specs, check_vma=False
    )
```

```python
import functools

import jax
import jax.numpy as jnp
from jax import lax
from jax.experimental import pallas as pl
from jax.experimental.pallas import tpu as pltpu
from jax.sharding import PartitionSpec as P

TURN = 3 * 10**9
COUPLE = 2 * 10**9
APPLY = 4 * 10**9
F32 = jnp.float32
BF16 = jnp.bfloat16
ROOM = pltpu.CompilerParams(vmem_limit_bytes=8 * 2**20)
NT = (((1,), (1,)), ((), ()))
VMEM = pl.BlockSpec(memory_space=pltpu.VMEM)
SMEM = pl.BlockSpec(memory_space=pltpu.SMEM)


def flops(count):
    return pl.CostEstimate(flops=count, bytes_accessed=0, transcendentals=0)


def call(kernel, name, outs, args, scratch=(), first=VMEM, cost=0):
    shapes = [jax.ShapeDtypeStruct(*o) for o in outs]
    return pl.pallas_call(
        kernel,
        in_specs=[first] + [VMEM] * (len(args) - 1),
        out_specs=[VMEM] * len(outs),
        out_shape=shapes,
        scratch_shapes=list(scratch),
        compiler_params=ROOM,
        cost_estimate=flops(cost),
        name=name,
    )(*args)


def along_bands(block, distance):
    count = lax.axis_size("band")
    return lax.ppermute(block, "band", [(i, (i + distance) % count) for i in range(count)])


def swapped(block):
    count = lax.axis_size("band")
    return lax.ppermute(block, "band", [(i, i ^ 1) for i in range(count)])


def on_even():
    return lax.axis_index("band") % 2 == 0


def by_permutes():
    count = lax.axis_size("dom")
    return count <= 8 and count & (count - 1) == 0


def from_all_domains(block):
    count = lax.axis_size("dom")
    if by_permutes():
        routes = [[(i, i ^ mask) for i in range(count)] for mask in range(1, count)]
        return [block] + [lax.ppermute(block, "dom", route) for route in routes]
    whole = lax.all_gather(block, "dom")
    return [whole[d] for d in range(count)]


def domain_at(place):
    return lax.axis_index("dom") ^ place if by_permutes() else place


def tile_of(extent, most):
    return max(w for w in range(128, most + 1, 128) if extent % w == 0)


def parts_of(points):
    part = points // 3
    return (points - part, part) if part % 128 == 0 else (points // 2, points // 2)


def turn_kernel(coupling_ref, out_ref):
    owned, rank = coupling_ref.shape
    whole = coupling_ref[...]
    high = whole.astype(BF16)
    unit = lax.broadcasted_iota(jnp.int32, (rank, rank), 0) == lax.broadcasted_iota(
        jnp.int32, (rank, rank), 1
    )
    unit = jnp.where(unit, 1.0, 0.0).astype(BF16)
    for i, piece in enumerate((high, (whole - high.astype(F32)).astype(BF16))):
        turned = lax.dot_general(unit, piece, NT, preferred_element_type=F32)
        out_ref[:, i * owned : (i + 1) * owned] = turned.astype(BF16)


def project_kernel(orb_ref, proj_ref, turned_ref, out_ref):
    width, points = orb_ref.shape
    out_ref[width:, : turned_ref.shape[1]] = turned_ref[...]
    tile = tile_of(points, 1024)
    total = None
    for at in range(0, points, tile):
        term = lax.dot_general(
            proj_ref[:, at : at + tile], orb_ref[:, at : at + tile], NT, preferred_element_type=F32
        )
        total = term if total is None else total + term
    out_ref[:width, :] = total.T.astype(BF16)


def project(orbitals, proj, coupling):
    width, points = orbitals.shape
    owned, rank = coupling.shape
    turned = call(
        turn_kernel, "turn", [((rank, 2 * owned), BF16)], [coupling], cost=TURN
    )[0]
    outs = [((width + rank, proj.shape[0]), BF16)]
    return call(project_kernel, "project", outs, [orbitals, proj, turned])[0]


def couple_kernel(count, slots, owned, slot_ref, *refs):
    loads = refs[:count]
    out_ref, pick, high_ref, low_ref = refs[count:]
    width, flat = out_ref.shape
    rank = flat // slots
    me = lax.axis_index("dom")
    lanes = lax.broadcasted_iota(jnp.int32, (rank, flat), 1)
    unit = lanes % rank == lax.broadcasted_iota(jnp.int32, (rank, flat), 0)
    lane_slot = lanes // rank

    atoms = jnp.zeros((rank, flat), jnp.int32)
    for k in range(slots):
        atoms = jnp.where(lane_slot == k, slot_ref[me, k], atoms)

    columns = None
    for place in range(count):
        owner = domain_at(place)
        for a in range(owned):
            hit = unit & (atoms == owner * owned + a)
            pick[a * rank : (a + 1) * rank, :] = jnp.where(hit, 1.0, 0.0).astype(BF16)
        parts = [loads[place][width:, i * owned * rank : (i + 1) * owned * rank] for i in (0, 1)]
        term = jnp.dot(jnp.concatenate(parts, 0), pick[...], preferred_element_type=F32)
        columns = term if columns is None else columns + term
    high, low = columns[:rank], columns[rank:]

    total = None
    for place in range(count):
        domain = domain_at(place)
        for k in range(slots):
            hit = atoms == slot_ref[domain, k]
            rows = slice(k * rank, (k + 1) * rank)
            high_ref[rows, :] = jnp.where(hit, high, 0.0).astype(BF16)
            low_ref[rows, :] = jnp.where(hit, low, 0.0).astype(BF16)
        block = loads[place][:width, :]
        term = jnp.dot(block, high_ref[...], preferred_element_type=F32)
        term += jnp.dot(block, low_ref[...], preferred_element_type=F32)
        total = term if total is None else total + term
    out_ref[...] = total.astype(BF16)


def couple(slot_atom, loads, width, owned):
    flat = loads[0].shape[1]
    slots = slot_atom.shape[1]
    return call(
        functools.partial(couple_kernel, len(loads), slots, owned),
        "couple",
        [((width, flat), BF16)],
        [slot_atom, *loads],
        [
            pltpu.VMEM((owned * (flat // slots), flat), BF16),
            pltpu.VMEM((flat, flat), BF16),
            pltpu.VMEM((flat, flat), BF16),
        ],
        first=SMEM,
        cost=COUPLE,
    )[0]


def choose_kernel(even_ref, odd_ref, after_ref, out_ref, *part_refs):
    @pl.when(on_even())
    def _():
        out_ref[...] = even_ref[...]

    @pl.when(jnp.logical_not(on_even()))
    def _():
        out_ref[...] = odd_ref[...]

    at = 0
    for part_ref in part_refs:
        part_ref[...] = odd_ref[:, at : at + part_ref.shape[1]]
        at += part_ref.shape[1]


def choose(for_even, for_odd, after, extents=()):
    width = for_even.shape[0]
    outs = [(for_even.shape, BF16)] + [((width, extent), BF16) for extent in extents]
    chosen, *parts = call(choose_kernel, "choose", outs, [for_even, for_odd, after])
    return chosen, parts


def apply_kernel(rot_ref, mine, one, two, three, proj_ref, out_ref):
    width, flat = mine.shape
    points = proj_ref.shape[1]
    mixed = None
    blocks = [mine, one, two, three]
    for s, block in enumerate(blocks):
        term = jnp.dot(
            rot_ref[:, s * width : (s + 1) * width], block[...], preferred_element_type=F32
        )
        mixed = term if mixed is None else mixed + term
    mixed = mixed.astype(BF16)
    tile = tile_of(points, 1024)
    for at in range(0, points, tile):
        out_ref[:, at : at + tile] = jnp.dot(
            mixed, proj_ref[:, at : at + tile], preferred_element_type=F32
        )


def finish_kernel(start, rot_ref, own, one, two, three, applied, *rest):
    out_ref, stack = rest[-2:]
    width, tile = out_ref.shape
    at = pl.multiple_of(pl.program_id(0) * tile, tile)
    there = pl.ds(pl.multiple_of(start + at, tile), tile)
    for s, ref in enumerate((own, one, two)):
        stack[s * width : (s + 1) * width, :] = ref[:, there]
    stack[3 * width :, :] = three[:, pl.ds(at, tile)]
    rotated = jnp.dot(rot_ref[...], stack[...], preferred_element_type=F32)
    added = rotated.astype(BF16).astype(F32) + applied[:, there]
    out_ref[...] = added.astype(out_ref.dtype)


def finish(rotation, own, one, two, three, applied, start, so_far):
    width, points = applied.shape
    extent = three.shape[1]
    tile = tile_of(extent, 1024)
    args = [rotation, own, one, two, three, applied]
    specs = [VMEM] * len(args)
    alias = {}
    if so_far is not None:
        alias = {len(args): 0}
        args.append(so_far)
        specs.append(pl.BlockSpec(memory_space=pl.ANY))
    return pl.pallas_call(
        functools.partial(finish_kernel, start),
        grid=(extent // tile,),
        in_specs=specs,
        out_specs=pl.BlockSpec((width, tile), lambda g: (0, start // tile + g)),
        out_shape=jax.ShapeDtypeStruct((width, points), BF16),
        scratch_shapes=[pltpu.VMEM((4 * width, tile), BF16)],
        input_output_aliases=alias,
        compiler_params=ROOM,
        cost_estimate=flops(0),
        name="finish",
    )(*args)


def on_device(orbitals, rotation, projectors, coupling, slot_atom):
    width, points = orbitals.shape
    slot_count, rank, _ = projectors.shape
    owned = coupling.shape[0]
    proj = projectors.reshape(slot_count * rank, points)

    two = along_bands(orbitals, 2)
    loads = from_all_domains(project(orbitals, proj, coupling.reshape(owned * rank, rank)))
    mine = couple(slot_atom, loads, width, owned)
    mine_two = along_bands(mine, 2)
    chosen, parts = choose(orbitals, two, mine_two, parts_of(points))
    one = swapped(chosen)
    three = [along_bands(part, 1) for part in parts]
    mine_three = along_bands(mine_two, 1)
    mine_one = swapped(choose(mine, mine_two, mine)[0])
    applied = call(
        apply_kernel,
        "apply",
        [((width, points), F32)],
        [rotation, mine, mine_one, mine_two, mine_three, proj],
        cost=APPLY,
    )[0]
    out, start = None, 0
    for part in three:
        out = finish(rotation, orbitals, one, two, part, applied, start, out)
        start += part.shape[1]
    return out


def solution(mesh):
    in_specs = (P("band", "dom"), P("band", None), P(None, None, "dom"), P("dom", None, None), P())
    out_specs = P("band", "dom")
    return jax.shard_map(
        on_device, mesh=mesh, in_specs=in_specs, out_specs=out_specs, check_vma=False
    )
```

```python
import functools

import jax
import jax.numpy as jnp
from jax import lax
from jax.experimental import pallas as pl
from jax.experimental.pallas import tpu as pltpu
from jax.sharding import PartitionSpec as P

TURN = 3 * 10**9
COUPLE = 2 * 10**9
APPLY = 2 * 10**9
F32 = jnp.float32
BF16 = jnp.bfloat16
ROOM = pltpu.CompilerParams(vmem_limit_bytes=8 * 2**20)
NT = (((1,), (1,)), ((), ()))
VMEM = pl.BlockSpec(memory_space=pltpu.VMEM)
SMEM = pl.BlockSpec(memory_space=pltpu.SMEM)


def flops(count):
    return pl.CostEstimate(flops=count, bytes_accessed=0, transcendentals=0)


def call(kernel, name, outs, args, scratch=(), first=VMEM, cost=0):
    shapes = [jax.ShapeDtypeStruct(*o) for o in outs]
    return pl.pallas_call(
        kernel,
        in_specs=[first] + [VMEM] * (len(args) - 1),
        out_specs=[VMEM] * len(outs),
        out_shape=shapes,
        scratch_shapes=list(scratch),
        compiler_params=ROOM,
        cost_estimate=flops(cost),
        name=name,
    )(*args)


def along_bands(block, distance, senders=(0, 1)):
    count = lax.axis_size("band")
    route = [(i, (i + distance) % count if i % 2 in senders else i) for i in range(count)]
    return lax.ppermute(block, "band", route)


def swapped(block):
    count = lax.axis_size("band")
    return lax.ppermute(block, "band", [(i, i ^ 1) for i in range(count)])


def on_even():
    return lax.axis_index("band") % 2 == 0


def by_permutes():
    count = lax.axis_size("dom")
    return count <= 8 and count & (count - 1) == 0


def from_all_domains(block):
    count = lax.axis_size("dom")
    if by_permutes():
        routes = [[(i, i ^ mask) for i in range(count)] for mask in range(1, count)]
        return [block] + [lax.ppermute(block, "dom", route) for route in routes]
    whole = lax.all_gather(block, "dom")
    return [whole[d] for d in range(count)]


def domain_at(place):
    return lax.axis_index("dom") ^ place if by_permutes() else place


def tile_of(extent, most):
    return max(w for w in range(128, most + 1, 128) if extent % w == 0)


def parts_of(points):
    part = points // 3
    return (points - part, part) if part % 128 == 0 else (points // 2, points // 2)


def turn_kernel(coupling_ref, out_ref):
    owned, rank = coupling_ref.shape
    whole = coupling_ref[...]
    high = whole.astype(BF16)
    unit = lax.broadcasted_iota(jnp.int32, (rank, rank), 0) == lax.broadcasted_iota(
        jnp.int32, (rank, rank), 1
    )
    unit = jnp.where(unit, 1.0, 0.0).astype(BF16)
    for i, piece in enumerate((high, (whole - high.astype(F32)).astype(BF16))):
        turned = lax.dot_general(unit, piece, NT, preferred_element_type=F32)
        out_ref[:, i * owned : (i + 1) * owned] = turned.astype(BF16)


def project_kernel(orb_ref, proj_ref, turned_ref, out_ref, *own_refs):
    width, points = orb_ref.shape
    out_ref[width:, : turned_ref.shape[1]] = turned_ref[...]
    at = 0
    for own_ref in own_refs:
        own_ref[...] = orb_ref[:, at : at + own_ref.shape[1]]
        at += own_ref.shape[1]
    tile = tile_of(points, 1024)
    total = None
    for at in range(0, points, tile):
        term = lax.dot_general(
            proj_ref[:, at : at + tile], orb_ref[:, at : at + tile], NT, preferred_element_type=F32
        )
        total = term if total is None else total + term
    out_ref[:width, :] = total.T.astype(BF16)


def project(orbitals, proj, coupling):
    width, points = orbitals.shape
    owned, rank = coupling.shape
    turned = call(
        turn_kernel, "turn", [((rank, 2 * owned), BF16)], [coupling], cost=TURN
    )[0]
    outs = [((width + rank, proj.shape[0]), BF16)]
    outs += [((width, extent), BF16) for extent in parts_of(points)]
    return call(project_kernel, "project", outs, [orbitals, proj, turned])


def couple_kernel(count, slots, owned, slot_ref, *refs):
    loads, pass_ref = refs[:count], refs[count]
    out_ref, passed_ref, pick, high_ref, low_ref = refs[count + 1 :]
    passed_ref[...] = pass_ref[...]
    width, flat = out_ref.shape
    rank = flat // slots
    me = lax.axis_index("dom")
    lanes = lax.broadcasted_iota(jnp.int32, (rank, flat), 1)
    unit = lanes % rank == lax.broadcasted_iota(jnp.int32, (rank, flat), 0)
    lane_slot = lanes // rank

    atoms = jnp.zeros((rank, flat), jnp.int32)
    for k in range(slots):
        atoms = jnp.where(lane_slot == k, slot_ref[me, k], atoms)

    columns = None
    for place in range(count):
        owner = domain_at(place)
        for a in range(owned):
            hit = unit & (atoms == owner * owned + a)
            pick[a * rank : (a + 1) * rank, :] = jnp.where(hit, 1.0, 0.0).astype(BF16)
        parts = [loads[place][width:, i * owned * rank : (i + 1) * owned * rank] for i in (0, 1)]
        term = jnp.dot(jnp.concatenate(parts, 0), pick[...], preferred_element_type=F32)
        columns = term if columns is None else columns + term
    high, low = columns[:rank], columns[rank:]

    total = None
    for place in range(count):
        domain = domain_at(place)
        for k in range(slots):
            hit = atoms == slot_ref[domain, k]
            rows = slice(k * rank, (k + 1) * rank)
            high_ref[rows, :] = jnp.where(hit, high, 0.0).astype(BF16)
            low_ref[rows, :] = jnp.where(hit, low, 0.0).astype(BF16)
        block = loads[place][:width, :]
        term = jnp.dot(block, high_ref[...], preferred_element_type=F32)
        term += jnp.dot(block, low_ref[...], preferred_element_type=F32)
        total = term if total is None else total + term
    out_ref[...] = total.astype(BF16)


def couple(slot_atom, loads, width, owned, passed):
    flat = loads[0].shape[1]
    slots = slot_atom.shape[1]
    return call(
        functools.partial(couple_kernel, len(loads), slots, owned),
        "couple",
        [((width, flat), BF16), (passed.shape, passed.dtype)],
        [slot_atom, *loads, passed],
        [
            pltpu.VMEM((owned * (flat // slots), flat), BF16),
            pltpu.VMEM((flat, flat), BF16),
            pltpu.VMEM((flat, flat), BF16),
        ],
        first=SMEM,
        cost=COUPLE,
    )


def choose_kernel(count, *refs):
    evens, odd_ref, out_ref = refs[:count], refs[count], refs[-1]

    @pl.when(on_even())
    def _():
        at = 0
        for even_ref in evens:
            out_ref[:, at : at + even_ref.shape[1]] = even_ref[...]
            at += even_ref.shape[1]

    @pl.when(jnp.logical_not(on_even()))
    def _():
        out_ref[...] = odd_ref[...]


def choose(evens, odd, *after):
    outs = [(odd.shape, odd.dtype)]
    return call(
        functools.partial(choose_kernel, len(evens)), "choose", outs, [*evens, odd, *after]
    )[0]


def by_distance(rot_ref, width):
    tiles = [rot_ref[:, s * width : (s + 1) * width] for s in range(4)]
    even = on_even()
    one, three = tiles[1].astype(F32), tiles[3].astype(F32)
    by_swap = jnp.where(even, one, three).astype(BF16)
    by_ring = jnp.where(even, three, one).astype(BF16)
    return [tiles[0], by_swap, tiles[2], by_ring]


def apply_kernel(rot_ref, mine, one, two, three, proj_ref, out_ref):
    width, flat = mine.shape
    points = proj_ref.shape[1]
    mixed = None
    blocks = [mine, one, two, three]
    for s, block in enumerate(blocks):
        term = jnp.dot(
            rot_ref[:, s * width : (s + 1) * width], block[...], preferred_element_type=F32
        )
        mixed = term if mixed is None else mixed + term
    mixed = mixed.astype(BF16)
    tile = tile_of(points, 1024)
    for at in range(0, points, tile):
        out_ref[:, at : at + tile] = jnp.dot(
            mixed, proj_ref[:, at : at + tile], preferred_element_type=F32
        )


def finish_kernel(rot_ref, own, swap, two, ring, applied, out_hbm, stack, out_ref, sems):
    width, points = own.shape
    turn = jnp.concatenate(by_distance(rot_ref, width), axis=1)
    pieces = sems.shape[0]
    tile = points // pieces
    copies = []
    for i in range(pieces):
        here = slice(i * tile, (i + 1) * tile)
        for s, ref in enumerate((own, swap, two, ring)):
            stack[s * width : (s + 1) * width, here] = ref[:, here]
        rotated = jnp.dot(turn, stack[:, here], preferred_element_type=F32)
        added = rotated.astype(BF16).astype(F32) + applied[:, here]
        out_ref[:, here] = added.astype(out_ref.dtype)
        part = (slice(None), pl.ds(i * tile, tile))
        copies.append(pltpu.make_async_copy(out_ref.at[part], out_hbm.at[part], sems.at[i]))
        copies[-1].start()
    for copy in copies:
        copy.wait()


def finish(*args):
    width, points = args[-1].shape
    pieces = points // tile_of(points, 1024)
    return pl.pallas_call(
        finish_kernel,
        in_specs=[VMEM] * len(args),
        out_specs=pl.BlockSpec(memory_space=pl.ANY),
        out_shape=jax.ShapeDtypeStruct((width, points), BF16),
        scratch_shapes=[
            pltpu.VMEM((4 * width, points), BF16),
            pltpu.VMEM((width, points), BF16),
            pltpu.SemaphoreType.DMA((pieces,)),
        ],
        compiler_params=ROOM,
        cost_estimate=flops(0),
        name="finish",
    )(*args)


def on_device(orbitals, rotation, projectors, coupling, slot_atom):
    width, points = orbitals.shape
    slot_count, rank, _ = projectors.shape
    owned = coupling.shape[0]
    proj = projectors.reshape(slot_count * rank, points)

    mixed = along_bands(orbitals, 2, (1,))
    load, *own = project(orbitals, proj, coupling.reshape(owned * rank, rank))
    loads = from_all_domains(load)
    two_even = [along_bands(own[0], 2, (0,))]
    mine, own[1] = couple(slot_atom, loads, width, owned, own[1])
    mine_two = along_bands(mine, 2)
    two_even.append(along_bands(own[1], 2, (0,)))
    mixed = choose([mixed], mixed, mine)
    ring = along_bands(mixed, 1)
    mine_three = along_bands(mine_two, 1)
    mine_one = swapped(choose([mine], mine_two, mixed))
    applied = call(
        apply_kernel,
        "apply",
        [((width, points), F32)],
        [rotation, mine, mine_one, mine_two, mine_three, proj],
        cost=APPLY,
    )[0]
    two = choose(two_even, mixed, applied)
    swap = swapped(two)
    return finish(rotation, orbitals, swap, two, ring, applied)


def solution(mesh):
    in_specs = (P("band", "dom"), P("band", None), P(None, None, "dom"), P("dom", None, None), P())
    out_specs = P("band", "dom")
    return jax.shard_map(
        on_device, mesh=mesh, in_specs=in_specs, out_specs=out_specs, check_vma=False
    )
```

```python
import functools

import jax
import jax.numpy as jnp
from jax import lax
from jax.experimental import pallas as pl
from jax.experimental.pallas import tpu as pltpu
from jax.sharding import PartitionSpec as P

TURN = 3 * 10**9
COUPLE = 2 * 10**9
APPLY = 5 * 10**9
F32 = jnp.float32
BF16 = jnp.bfloat16
ROOM = pltpu.CompilerParams(vmem_limit_bytes=8 * 2**20)
NT = (((1,), (1,)), ((), ()))
VMEM = pl.BlockSpec(memory_space=pltpu.VMEM)
SMEM = pl.BlockSpec(memory_space=pltpu.SMEM)


def flops(count):
    return pl.CostEstimate(flops=count, bytes_accessed=0, transcendentals=0)


def call(kernel, name, outs, args, scratch=(), first=VMEM, cost=0):
    shapes = [jax.ShapeDtypeStruct(*o) for o in outs]
    return pl.pallas_call(
        kernel,
        in_specs=[first] + [VMEM] * (len(args) - 1),
        out_specs=[VMEM] * len(outs),
        out_shape=shapes,
        scratch_shapes=list(scratch),
        compiler_params=ROOM,
        cost_estimate=flops(cost),
        name=name,
    )(*args)


def along_bands(block, distance):
    count = lax.axis_size("band")
    return lax.ppermute(block, "band", [(i, (i + distance) % count) for i in range(count)])


def swapped(block):
    count = lax.axis_size("band")
    return lax.ppermute(block, "band", [(i, i ^ 1) for i in range(count)])


def on_even():
    return lax.axis_index("band") % 2 == 0


def by_permutes():
    count = lax.axis_size("dom")
    return count <= 8 and count & (count - 1) == 0


def from_all_domains(block):
    count = lax.axis_size("dom")
    if by_permutes():
        routes = [[(i, i ^ mask) for i in range(count)] for mask in range(1, count)]
        return [block] + [lax.ppermute(block, "dom", route) for route in routes]
    whole = lax.all_gather(block, "dom")
    return [whole[d] for d in range(count)]


def domain_at(place):
    return lax.axis_index("dom") ^ place if by_permutes() else place


def tile_of(extent, most):
    return max(w for w in range(128, most + 1, 128) if extent % w == 0)


def turn_kernel(coupling_ref, out_ref):
    owned, rank = coupling_ref.shape
    whole = coupling_ref[...]
    high = whole.astype(BF16)
    unit = lax.broadcasted_iota(jnp.int32, (rank, rank), 0) == lax.broadcasted_iota(
        jnp.int32, (rank, rank), 1
    )
    unit = jnp.where(unit, 1.0, 0.0).astype(BF16)
    for i, piece in enumerate((high, (whole - high.astype(F32)).astype(BF16))):
        turned = lax.dot_general(unit, piece, NT, preferred_element_type=F32)
        out_ref[:, i * owned : (i + 1) * owned] = turned.astype(BF16)


def project_kernel(orb_ref, proj_ref, turned_ref, out_ref):
    width, points = orb_ref.shape
    out_ref[width:, : turned_ref.shape[1]] = turned_ref[...]
    tile = tile_of(points, 1024)
    total = None
    for at in range(0, points, tile):
        term = lax.dot_general(
            proj_ref[:, at : at + tile], orb_ref[:, at : at + tile], NT, preferred_element_type=F32
        )
        total = term if total is None else total + term
    out_ref[:width, :] = total.T.astype(BF16)


def project(orbitals, proj, coupling):
    width, points = orbitals.shape
    owned, rank = coupling.shape
    turned = call(
        turn_kernel, "turn", [((rank, 2 * owned), BF16)], [coupling], cost=TURN
    )[0]
    outs = [((width + rank, proj.shape[0]), BF16)]
    return call(project_kernel, "project", outs, [orbitals, proj, turned])[0]


def couple_kernel(count, slots, owned, slot_ref, *refs):
    loads = refs[:count]
    out_ref, pick, high_ref, low_ref = refs[count:]
    width, flat = out_ref.shape
    rank = flat // slots
    me = lax.axis_index("dom")
    lanes = lax.broadcasted_iota(jnp.int32, (rank, flat), 1)
    unit = lanes % rank == lax.broadcasted_iota(jnp.int32, (rank, flat), 0)
    lane_slot = lanes // rank

    atoms = jnp.zeros((rank, flat), jnp.int32)
    for k in range(slots):
        atoms = jnp.where(lane_slot == k, slot_ref[me, k], atoms)

    columns = None
    for place in range(count):
        owner = domain_at(place)
        for a in range(owned):
            hit = unit & (atoms == owner * owned + a)
            pick[a * rank : (a + 1) * rank, :] = jnp.where(hit, 1.0, 0.0).astype(BF16)
        parts = [loads[place][width:, i * owned * rank : (i + 1) * owned * rank] for i in (0, 1)]
        term = jnp.dot(jnp.concatenate(parts, 0), pick[...], preferred_element_type=F32)
        columns = term if columns is None else columns + term
    high, low = columns[:rank], columns[rank:]

    total = None
    for place in range(count):
        domain = domain_at(place)
        for k in range(slots):
            hit = atoms == slot_ref[domain, k]
            rows = slice(k * rank, (k + 1) * rank)
            high_ref[rows, :] = jnp.where(hit, high, 0.0).astype(BF16)
            low_ref[rows, :] = jnp.where(hit, low, 0.0).astype(BF16)
        block = loads[place][:width, :]
        term = jnp.dot(block, high_ref[...], preferred_element_type=F32)
        term += jnp.dot(block, low_ref[...], preferred_element_type=F32)
        total = term if total is None else total + term
    out_ref[...] = total.astype(BF16)


def couple(slot_atom, loads, width, owned):
    flat = loads[0].shape[1]
    slots = slot_atom.shape[1]
    return call(
        functools.partial(couple_kernel, len(loads), slots, owned),
        "couple",
        [((width, flat), BF16)],
        [slot_atom, *loads],
        [
            pltpu.VMEM((owned * (flat // slots), flat), BF16),
            pltpu.VMEM((flat, flat), BF16),
            pltpu.VMEM((flat, flat), BF16),
        ],
        first=SMEM,
        cost=COUPLE,
    )[0]


def hold_kernel(block_ref, after_ref, out_ref):
    out_ref[...] = block_ref[...]


def hold(block, after):
    return call(hold_kernel, "hold", [(block.shape, block.dtype)], [block, after])[0]


def choose_kernel(mine, mine_two, own, two_a, two_b, coef_ref, upper_ref, lower_ref, held_ref):
    cut, half = two_a.shape[0], upper_ref.shape[0]

    @pl.when(on_even())
    def _():
        coef_ref[...] = mine[...]
        upper_ref[...] = own[:half, :]
        lower_ref[...] = own[half:, :]

    @pl.when(jnp.logical_not(on_even()))
    def _():
        coef_ref[...] = mine_two[...]
        upper_ref[...] = two_a[:half, :]
        lower_ref[: cut - half, :] = two_a[half:, :]
        lower_ref[cut - half :, :] = two_b[...]

    held_ref[...] = two_b[...]


def choose(mine, mine_two, own, two_a, two_b):
    args = [mine, mine_two, own, two_a, two_b]
    half = ((own.shape[0] // 2, own.shape[1]), own.dtype)
    outs = [(mine.shape, mine.dtype), half, half, (two_b.shape, two_b.dtype)]
    return call(choose_kernel, "choose", outs, args)


def apply_kernel(rot_ref, mine, one, two, three, proj_ref, out_ref):
    width, flat = mine.shape
    points = proj_ref.shape[1]
    mixed = None
    blocks = [mine, one, two, three]
    for s, block in enumerate(blocks):
        term = jnp.dot(
            rot_ref[:, s * width : (s + 1) * width], block[...], preferred_element_type=F32
        )
        mixed = term if mixed is None else mixed + term
    mixed = mixed.astype(BF16)
    tile = tile_of(points, 1024)
    for at in range(0, points, tile):
        out_ref[:, at : at + tile] = jnp.dot(
            mixed, proj_ref[:, at : at + tile], preferred_element_type=F32
        )


def finish_kernel(
    rot_ref, own, one_a, one_b, two_a, two_b, three_a, three_b, applied, out_hbm, stack, out_ref, sems
):
    width, points = own.shape
    pieces = sems.shape[0]
    tile = points // pieces
    copies = []
    for i in range(pieces):
        here = slice(i * tile, (i + 1) * tile)
        at = 0
        for ref in (own, one_a, one_b, two_a, two_b, three_a, three_b):
            stack[at : at + ref.shape[0], here] = ref[:, here]
            at += ref.shape[0]
        rotated = jnp.dot(rot_ref[...], stack[:, here], preferred_element_type=F32)
        added = rotated.astype(BF16).astype(F32) + applied[:, here]
        out_ref[:, here] = added.astype(out_ref.dtype)
        part = (slice(None), pl.ds(i * tile, tile))
        copies.append(pltpu.make_async_copy(out_ref.at[part], out_hbm.at[part], sems.at[i]))
        copies[-1].start()
    for copy in copies:
        copy.wait()


def finish(*args):
    width, points = args[-1].shape
    pieces = points // tile_of(points, 1024)
    return pl.pallas_call(
        finish_kernel,
        in_specs=[VMEM] * len(args),
        out_specs=pl.BlockSpec(memory_space=pl.ANY),
        out_shape=jax.ShapeDtypeStruct((width, points), BF16),
        scratch_shapes=[
            pltpu.VMEM((4 * width, points), BF16),
            pltpu.VMEM((width, points), BF16),
            pltpu.SemaphoreType.DMA((pieces,)),
        ],
        compiler_params=ROOM,
        cost_estimate=flops(0),
        name="finish",
    )(*args)


def on_device(orbitals, rotation, projectors, coupling, slot_atom):
    width, points = orbitals.shape
    slot_count, rank, _ = projectors.shape
    owned = coupling.shape[0]
    proj = projectors.reshape(slot_count * rank, points)

    cut = width * 3 // 4
    two_a = along_bands(orbitals[:cut], 2)
    two_b = along_bands(orbitals[cut:], 2)
    loads = from_all_domains(project(orbitals, proj, coupling.reshape(owned * rank, rank)))
    mine = couple(slot_atom, loads, width, owned)
    mine_two = along_bands(mine, 2)
    three_a = along_bands(hold(two_a, mine), 1)
    other, upper, lower, held = choose(mine, mine_two, orbitals, two_a, two_b)
    mine_three = along_bands(mine_two, 1)
    mine_one = swapped(other)
    three_b = along_bands(held, 1)
    one_a, one_b = swapped(upper), swapped(lower)
    applied = call(
        apply_kernel,
        "apply",
        [((width, points), F32)],
        [rotation, mine, mine_one, mine_two, mine_three, proj],
        cost=APPLY,
    )[0]
    return finish(rotation, orbitals, one_a, one_b, two_a, two_b, three_a, three_b, applied)


def solution(mesh):
    in_specs = (P("band", "dom"), P("band", None), P(None, None, "dom"), P("dom", None, None), P())
    out_specs = P("band", "dom")
    return jax.shard_map(
        on_device, mesh=mesh, in_specs=in_specs, out_specs=out_specs, check_vma=False
    )
```

```python
import functools

import jax
import jax.numpy as jnp
from jax import lax
from jax.experimental import pallas as pl
from jax.experimental.pallas import tpu as pltpu
from jax.sharding import PartitionSpec as P

TURN = 5 * 10**9
COUPLE = 2 * 10**9
APPLY = 5 * 10**9
F32 = jnp.float32
BF16 = jnp.bfloat16
ROOM = pltpu.CompilerParams(vmem_limit_bytes=8 * 2**20)
NT = (((1,), (1,)), ((), ()))
VMEM = pl.BlockSpec(memory_space=pltpu.VMEM)
SMEM = pl.BlockSpec(memory_space=pltpu.SMEM)


def flops(count):
    return pl.CostEstimate(flops=count, bytes_accessed=0, transcendentals=0)


def call(kernel, name, outs, args, scratch=(), first=VMEM, cost=0):
    shapes = [jax.ShapeDtypeStruct(*o) for o in outs]
    return pl.pallas_call(
        kernel,
        in_specs=[first] + [VMEM] * (len(args) - 1),
        out_specs=[VMEM] * len(outs),
        out_shape=shapes,
        scratch_shapes=list(scratch),
        compiler_params=ROOM,
        cost_estimate=flops(cost),
        name=name,
    )(*args)


def along_bands(block, distance):
    count = lax.axis_size("band")
    return lax.ppermute(block, "band", [(i, (i + distance) % count) for i in range(count)])


def swapped(block):
    count = lax.axis_size("band")
    return lax.ppermute(block, "band", [(i, i ^ 1) for i in range(count)])


def on_even():
    return lax.axis_index("band") % 2 == 0


def by_permutes():
    count = lax.axis_size("dom")
    return count <= 8 and count & (count - 1) == 0


def from_all_domains(block):
    count = lax.axis_size("dom")
    if by_permutes():
        routes = [[(i, i ^ mask) for i in range(count)] for mask in range(1, count)]
        return [block] + [lax.ppermute(block, "dom", route) for route in routes]
    whole = lax.all_gather(block, "dom")
    return [whole[d] for d in range(count)]


def domain_at(place):
    return lax.axis_index("dom") ^ place if by_permutes() else place


def tile_of(extent, most):
    return max(w for w in range(128, most + 1, 128) if extent % w == 0)


def turn_kernel(coupling_ref, out_ref):
    owned, rank = coupling_ref.shape
    whole = coupling_ref[...]
    high = whole.astype(BF16)
    unit = lax.broadcasted_iota(jnp.int32, (rank, rank), 0) == lax.broadcasted_iota(
        jnp.int32, (rank, rank), 1
    )
    unit = jnp.where(unit, 1.0, 0.0).astype(BF16)
    for i, piece in enumerate((high, (whole - high.astype(F32)).astype(BF16))):
        turned = lax.dot_general(unit, piece, NT, preferred_element_type=F32)
        out_ref[:, i * owned : (i + 1) * owned] = turned.astype(BF16)


def project_kernel(orb_ref, proj_ref, turned_ref, out_ref):
    width, points = orb_ref.shape
    out_ref[width:, : turned_ref.shape[1]] = turned_ref[...]
    tile = tile_of(points, 1024)
    total = None
    for at in range(0, points, tile):
        term = lax.dot_general(
            proj_ref[:, at : at + tile], orb_ref[:, at : at + tile], NT, preferred_element_type=F32
        )
        total = term if total is None else total + term
    out_ref[:width, :] = total.T.astype(BF16)


def project(orbitals, proj, coupling):
    width, points = orbitals.shape
    owned, rank = coupling.shape
    turned = call(
        turn_kernel, "turn", [((rank, 2 * owned), BF16)], [coupling], cost=TURN
    )[0]
    outs = [((width + rank, proj.shape[0]), BF16)]
    return call(project_kernel, "project", outs, [orbitals, proj, turned])[0]


def couple_kernel(count, slots, owned, slot_ref, *refs):
    loads = refs[:count]
    out_ref, pick, high_ref, low_ref = refs[count:]
    width, flat = out_ref.shape
    rank = flat // slots
    me = lax.axis_index("dom")
    lanes = lax.broadcasted_iota(jnp.int32, (rank, flat), 1)
    unit = lanes % rank == lax.broadcasted_iota(jnp.int32, (rank, flat), 0)
    lane_slot = lanes // rank

    atoms = jnp.zeros((rank, flat), jnp.int32)
    for k in range(slots):
        atoms = jnp.where(lane_slot == k, slot_ref[me, k], atoms)

    columns = None
    for place in range(count):
        owner = domain_at(place)
        for a in range(owned):
            hit = unit & (atoms == owner * owned + a)
            pick[a * rank : (a + 1) * rank, :] = jnp.where(hit, 1.0, 0.0).astype(BF16)
        parts = [loads[place][width:, i * owned * rank : (i + 1) * owned * rank] for i in (0, 1)]
        term = jnp.dot(jnp.concatenate(parts, 0), pick[...], preferred_element_type=F32)
        columns = term if columns is None else columns + term
    high, low = columns[:rank], columns[rank:]

    total = None
    for place in range(count):
        domain = domain_at(place)
        for k in range(slots):
            hit = atoms == slot_ref[domain, k]
            rows = slice(k * rank, (k + 1) * rank)
            high_ref[rows, :] = jnp.where(hit, high, 0.0).astype(BF16)
            low_ref[rows, :] = jnp.where(hit, low, 0.0).astype(BF16)
        block = loads[place][:width, :]
        term = jnp.dot(block, high_ref[...], preferred_element_type=F32)
        term += jnp.dot(block, low_ref[...], preferred_element_type=F32)
        total = term if total is None else total + term
    out_ref[...] = total.astype(BF16)


def couple(slot_atom, loads, width, owned):
    flat = loads[0].shape[1]
    slots = slot_atom.shape[1]
    return call(
        functools.partial(couple_kernel, len(loads), slots, owned),
        "couple",
        [((width, flat), BF16)],
        [slot_atom, *loads],
        [
            pltpu.VMEM((owned * (flat // slots), flat), BF16),
            pltpu.VMEM((flat, flat), BF16),
            pltpu.VMEM((flat, flat), BF16),
        ],
        first=SMEM,
        cost=COUPLE,
    )[0]


def hold_kernel(block_ref, after_ref, out_ref):
    out_ref[...] = block_ref[...]


def hold(block, after):
    return call(hold_kernel, "hold", [(block.shape, block.dtype)], [block, after])[0]


def choose_kernel(mine, mine_two, own, two_a, two_b, coef_ref, upper_ref, lower_ref, held_ref):
    cut, half = two_a.shape[0], upper_ref.shape[0]

    @pl.when(on_even())
    def _():
        coef_ref[...] = mine[...]
        upper_ref[...] = own[:half, :]
        lower_ref[...] = own[half:, :]

    @pl.when(jnp.logical_not(on_even()))
    def _():
        coef_ref[...] = mine_two[...]
        upper_ref[...] = two_a[:half, :]
        lower_ref[: cut - half, :] = two_a[half:, :]
        lower_ref[cut - half :, :] = two_b[...]

    held_ref[...] = two_b[...]


def choose(mine, mine_two, own, two_a, two_b):
    args = [mine, mine_two, own, two_a, two_b]
    half = ((own.shape[0] // 2, own.shape[1]), own.dtype)
    outs = [(mine.shape, mine.dtype), half, half, (two_b.shape, two_b.dtype)]
    return call(choose_kernel, "choose", outs, args)


def apply_kernel(rot_ref, mine, one, two, three, proj_ref, out_ref):
    width, flat = mine.shape
    points = proj_ref.shape[1]
    mixed = None
    blocks = [mine, one, two, three]
    for s, block in enumerate(blocks):
        term = jnp.dot(
            rot_ref[:, s * width : (s + 1) * width], block[...], preferred_element_type=F32
        )
        mixed = term if mixed is None else mixed + term
    mixed = mixed.astype(BF16)
    tile = tile_of(points, 1024)
    for at in range(0, points, tile):
        out_ref[:, at : at + tile] = jnp.dot(
            mixed, proj_ref[:, at : at + tile], preferred_element_type=F32
        )


def gather_kernel(rot_ref, *refs):
    blocks, (out_ref, stack) = refs[:-2], refs[-2:]
    depth, points = stack.shape
    tile = tile_of(points, 1024)
    for i in range(points // tile):
        here = slice(i * tile, (i + 1) * tile)
        at = 0
        for ref in blocks:
            stack[at : at + ref.shape[0], here] = ref[:, here]
            at += ref.shape[0]
        out_ref[:, here] = jnp.dot(rot_ref[:, :depth], stack[:, here], preferred_element_type=F32)


def gather(rotation, *blocks):
    width, points = blocks[0].shape
    depth = sum(block.shape[0] for block in blocks)
    scratch = [pltpu.VMEM((depth, points), BF16)]
    return call(
        gather_kernel, "gather", [((width, points), F32)], [rotation, *blocks], scratch
    )[0]


def finish_kernel(rot_ref, partial_ref, last_ref, applied, out_hbm, out_ref, sems):
    points = out_ref.shape[1]
    rows = last_ref.shape[0]
    pieces = sems.shape[0]
    tile = points // pieces
    turn = rot_ref[:, rot_ref.shape[1] - rows :]
    copies = []
    for i in range(pieces):
        here = slice(i * tile, (i + 1) * tile)
        rotated = partial_ref[:, here] + jnp.dot(
            turn, last_ref[:, here], preferred_element_type=F32
        )
        added = rotated.astype(BF16).astype(F32) + applied[:, here]
        out_ref[:, here] = added.astype(out_ref.dtype)
        part = (slice(None), pl.ds(i * tile, tile))
        copies.append(pltpu.make_async_copy(out_ref.at[part], out_hbm.at[part], sems.at[i]))
        copies[-1].start()
    for copy in copies:
        copy.wait()


def finish(*args):
    width, points = args[-1].shape
    pieces = points // tile_of(points, 1024)
    return pl.pallas_call(
        finish_kernel,
        in_specs=[VMEM] * len(args),
        out_specs=pl.BlockSpec(memory_space=pl.ANY),
        out_shape=jax.ShapeDtypeStruct((width, points), BF16),
        scratch_shapes=[pltpu.VMEM((width, points), BF16), pltpu.SemaphoreType.DMA((pieces,))],
        compiler_params=ROOM,
        cost_estimate=flops(0),
        name="finish",
    )(*args)


def on_device(orbitals, rotation, projectors, coupling, slot_atom):
    width, points = orbitals.shape
    slot_count, rank, _ = projectors.shape
    owned = coupling.shape[0]
    proj = projectors.reshape(slot_count * rank, points)

    cut = width * 3 // 4
    two_a = along_bands(orbitals[:cut], 2)
    two_b = along_bands(orbitals[cut:], 2)
    loads = from_all_domains(project(orbitals, proj, coupling.reshape(owned * rank, rank)))
    mine = couple(slot_atom, loads, width, owned)
    mine_two = along_bands(mine, 2)
    three_a = along_bands(hold(two_a, mine), 1)
    other, upper, lower, held = choose(mine, mine_two, orbitals, two_a, two_b)
    mine_three = along_bands(mine_two, 1)
    mine_one = swapped(other)
    three_b = along_bands(held, 1)
    one_a, one_b = swapped(upper), swapped(lower)
    applied = call(
        apply_kernel,
        "apply",
        [((width, points), F32)],
        [rotation, mine, mine_one, mine_two, mine_three, proj],
        cost=APPLY,
    )[0]
    partial = gather(rotation, orbitals, one_a, one_b, two_a, two_b, three_a)
    return finish(rotation, partial, three_b, applied)


def solution(mesh):
    in_specs = (P("band", "dom"), P("band", None), P(None, None, "dom"), P("dom", None, None), P())
    out_specs = P("band", "dom")
    return jax.shard_map(
        on_device, mesh=mesh, in_specs=in_specs, out_specs=out_specs, check_vma=False
    )
```

```python
import functools

import jax
import jax.numpy as jnp
from jax import lax
from jax.experimental import pallas as pl
from jax.experimental.pallas import tpu as pltpu
from jax.sharding import PartitionSpec as P

TURN = 3 * 10**9
COUPLE = 2 * 10**9
APPLY = 5 * 10**9
CUT_ROOM = 60 * 2**20
F32 = jnp.float32
BF16 = jnp.bfloat16
ROOM = pltpu.CompilerParams(vmem_limit_bytes=8 * 2**20)
NT = (((1,), (1,)), ((), ()))
VMEM = pl.BlockSpec(memory_space=pltpu.VMEM)
SMEM = pl.BlockSpec(memory_space=pltpu.SMEM)


def flops(count):
    return pl.CostEstimate(flops=count, bytes_accessed=0, transcendentals=0)


def call(kernel, name, outs, args, scratch=(), first=VMEM, cost=0):
    shapes = [jax.ShapeDtypeStruct(*o) for o in outs]
    return pl.pallas_call(
        kernel,
        in_specs=[first] + [VMEM] * (len(args) - 1),
        out_specs=[VMEM] * len(outs),
        out_shape=shapes,
        scratch_shapes=list(scratch),
        compiler_params=ROOM,
        cost_estimate=flops(cost),
        name=name,
    )(*args)


def along_bands(block, distance):
    count = lax.axis_size("band")
    return lax.ppermute(block, "band", [(i, (i + distance) % count) for i in range(count)])


def swapped(block):
    count = lax.axis_size("band")
    return lax.ppermute(block, "band", [(i, i ^ 1) for i in range(count)])


def on_even():
    return lax.axis_index("band") % 2 == 0


def by_permutes():
    count = lax.axis_size("dom")
    return count <= 8 and count & (count - 1) == 0


def from_all_domains(block):
    count = lax.axis_size("dom")
    if by_permutes():
        routes = [[(i, i ^ mask) for i in range(count)] for mask in range(1, count)]
        return [block] + [lax.ppermute(block, "dom", route) for route in routes]
    whole = lax.all_gather(block, "dom")
    return [whole[d] for d in range(count)]


def domain_at(place):
    return lax.axis_index("dom") ^ place if by_permutes() else place


def tile_of(extent, most):
    return max(w for w in range(128, most + 1, 128) if extent % w == 0)


def turn_kernel(coupling_ref, out_ref):
    owned, rank = coupling_ref.shape
    whole = coupling_ref[...]
    high = whole.astype(BF16)
    unit = lax.broadcasted_iota(jnp.int32, (rank, rank), 0) == lax.broadcasted_iota(
        jnp.int32, (rank, rank), 1
    )
    unit = jnp.where(unit, 1.0, 0.0).astype(BF16)
    for i, piece in enumerate((high, (whole - high.astype(F32)).astype(BF16))):
        turned = lax.dot_general(unit, piece, NT, preferred_element_type=F32)
        out_ref[:, i * owned : (i + 1) * owned] = turned.astype(BF16)


def project_kernel(orb_ref, proj_ref, turned_ref, out_ref):
    width, points = orb_ref.shape
    out_ref[width:, : turned_ref.shape[1]] = turned_ref[...]
    tile = tile_of(points, 1024)
    total = None
    for at in range(0, points, tile):
        term = lax.dot_general(
            proj_ref[:, at : at + tile], orb_ref[:, at : at + tile], NT, preferred_element_type=F32
        )
        total = term if total is None else total + term
    out_ref[:width, :] = total.T.astype(BF16)


def project(orbitals, proj, coupling):
    width, points = orbitals.shape
    owned, rank = coupling.shape
    turned = call(
        turn_kernel, "turn", [((rank, 2 * owned), BF16)], [coupling], cost=TURN
    )[0]
    outs = [((width + rank, proj.shape[0]), BF16)]
    return call(project_kernel, "project", outs, [orbitals, proj, turned])[0]


def couple_kernel(count, slots, owned, slot_ref, *refs):
    loads = refs[:count]
    out_ref, pick, high_ref, low_ref = refs[count:]
    width, flat = out_ref.shape
    rank = flat // slots
    me = lax.axis_index("dom")
    lanes = lax.broadcasted_iota(jnp.int32, (rank, flat), 1)
    unit = lanes % rank == lax.broadcasted_iota(jnp.int32, (rank, flat), 0)
    lane_slot = lanes // rank

    atoms = jnp.zeros((rank, flat), jnp.int32)
    for k in range(slots):
        atoms = jnp.where(lane_slot == k, slot_ref[me, k], atoms)

    columns = None
    for place in range(count):
        owner = domain_at(place)
        for a in range(owned):
            hit = unit & (atoms == owner * owned + a)
            pick[a * rank : (a + 1) * rank, :] = jnp.where(hit, 1.0, 0.0).astype(BF16)
        parts = [loads[place][width:, i * owned * rank : (i + 1) * owned * rank] for i in (0, 1)]
        term = jnp.dot(jnp.concatenate(parts, 0), pick[...], preferred_element_type=F32)
        columns = term if columns is None else columns + term
    high, low = columns[:rank], columns[rank:]

    total = None
    for place in range(count):
        domain = domain_at(place)
        for k in range(slots):
            hit = atoms == slot_ref[domain, k]
            rows = slice(k * rank, (k + 1) * rank)
            high_ref[rows, :] = jnp.where(hit, high, 0.0).astype(BF16)
            low_ref[rows, :] = jnp.where(hit, low, 0.0).astype(BF16)
        block = loads[place][:width, :]
        term = jnp.dot(block, high_ref[...], preferred_element_type=F32)
        term += jnp.dot(block, low_ref[...], preferred_element_type=F32)
        total = term if total is None else total + term
    out_ref[...] = total.astype(BF16)


def couple(slot_atom, loads, width, owned):
    flat = loads[0].shape[1]
    slots = slot_atom.shape[1]
    return call(
        functools.partial(couple_kernel, len(loads), slots, owned),
        "couple",
        [((width, flat), BF16)],
        [slot_atom, *loads],
        [
            pltpu.VMEM((owned * (flat // slots), flat), BF16),
            pltpu.VMEM((flat, flat), BF16),
            pltpu.VMEM((flat, flat), BF16),
        ],
        first=SMEM,
        cost=COUPLE,
    )[0]


def cut_kernel(block_hbm, upper_ref, lower_ref, sems):
    rows = upper_ref.shape[0]
    upper = pltpu.make_async_copy(block_hbm.at[pl.ds(0, rows)], upper_ref, sems.at[0])
    lower = pltpu.make_async_copy(
        block_hbm.at[pl.ds(rows, lower_ref.shape[0])], lower_ref, sems.at[1]
    )
    upper.start()
    lower.start()
    upper.wait()
    lower.wait()


def cut(block, rows):
    width, points = block.shape
    shapes = [(rows, points), (width - rows, points)]
    return pl.pallas_call(
        cut_kernel,
        in_specs=[pl.BlockSpec(memory_space=pl.ANY)],
        out_specs=[pl.BlockSpec(memory_space=pl.ANY)] * 2,
        out_shape=[jax.ShapeDtypeStruct(shape, block.dtype) for shape in shapes],
        scratch_shapes=[pltpu.SemaphoreType.DMA((2,))],
        compiler_params=pltpu.CompilerParams(vmem_limit_bytes=CUT_ROOM),
        cost_estimate=flops(0),
        name="cut",
    )(block)


def hold_kernel(block_ref, after_ref, out_ref):
    out_ref[...] = block_ref[...]


def hold(block, after):
    return call(hold_kernel, "hold", [(block.shape, block.dtype)], [block, after])[0]


def choose_kernel(mine, mine_two, own, two_a, two_b, coef_ref, upper_ref, lower_ref, held_ref):
    cut, half = two_a.shape[0], upper_ref.shape[0]

    @pl.when(on_even())
    def _():
        coef_ref[...] = mine[...]
        upper_ref[...] = own[:half, :]
        lower_ref[...] = own[half:, :]

    @pl.when(jnp.logical_not(on_even()))
    def _():
        coef_ref[...] = mine_two[...]
        upper_ref[...] = two_a[:half, :]
        lower_ref[: cut - half, :] = two_a[half:, :]
        lower_ref[cut - half :, :] = two_b[...]

    held_ref[...] = two_b[...]


def choose(mine, mine_two, own, two_a, two_b):
    args = [mine, mine_two, own, two_a, two_b]
    half = ((own.shape[0] // 2, own.shape[1]), own.dtype)
    outs = [(mine.shape, mine.dtype), half, half, (two_b.shape, two_b.dtype)]
    return call(choose_kernel, "choose", outs, args)


def apply_kernel(rot_ref, mine, one, two, three, proj_ref, out_ref):
    width, flat = mine.shape
    points = proj_ref.shape[1]
    mixed = None
    blocks = [mine, one, two, three]
    for s, block in enumerate(blocks):
        term = jnp.dot(
            rot_ref[:, s * width : (s + 1) * width], block[...], preferred_element_type=F32
        )
        mixed = term if mixed is None else mixed + term
    mixed = mixed.astype(BF16)
    tile = tile_of(points, 1024)
    for at in range(0, points, tile):
        out_ref[:, at : at + tile] = jnp.dot(
            mixed, proj_ref[:, at : at + tile], preferred_element_type=F32
        )


def finish_kernel(
    rot_ref, own, one_a, one_b, two_a, two_b, three_a, three_b, applied, out_hbm, stack, out_ref, sems
):
    width, points = own.shape
    pieces = sems.shape[0]
    tile = points // pieces
    copies = []
    for i in range(pieces):
        here = slice(i * tile, (i + 1) * tile)
        at = 0
        for ref in (own, one_a, one_b, two_a, two_b, three_a, three_b):
            stack[at : at + ref.shape[0], here] = ref[:, here]
            at += ref.shape[0]
        rotated = jnp.dot(rot_ref[...], stack[:, here], preferred_element_type=F32)
        added = rotated.astype(BF16).astype(F32) + applied[:, here]
        out_ref[:, here] = added.astype(out_ref.dtype)
        part = (slice(None), pl.ds(i * tile, tile))
        copies.append(pltpu.make_async_copy(out_ref.at[part], out_hbm.at[part], sems.at[i]))
        copies[-1].start()
    for copy in copies:
        copy.wait()


def finish(*args):
    width, points = args[-1].shape
    pieces = points // tile_of(points, 512)
    return pl.pallas_call(
        finish_kernel,
        in_specs=[VMEM] * len(args),
        out_specs=pl.BlockSpec(memory_space=pl.ANY),
        out_shape=jax.ShapeDtypeStruct((width, points), BF16),
        scratch_shapes=[
            pltpu.VMEM((4 * width, points), BF16),
            pltpu.VMEM((width, points), BF16),
            pltpu.SemaphoreType.DMA((pieces,)),
        ],
        compiler_params=ROOM,
        cost_estimate=flops(0),
        name="finish",
    )(*args)


def on_device(orbitals, rotation, projectors, coupling, slot_atom):
    width, points = orbitals.shape
    slot_count, rank, _ = projectors.shape
    owned = coupling.shape[0]
    proj = projectors.reshape(slot_count * rank, points)

    own_a, own_b = cut(orbitals, width * 3 // 4)
    two_a = along_bands(own_a, 2)
    two_b = along_bands(own_b, 2)
    loads = from_all_domains(project(orbitals, proj, coupling.reshape(owned * rank, rank)))
    mine = couple(slot_atom, loads, width, owned)
    mine_two = along_bands(mine, 2)
    three_a = along_bands(hold(two_a, mine), 1)
    other, upper, lower, held = choose(mine, mine_two, orbitals, two_a, two_b)
    mine_three = along_bands(mine_two, 1)
    mine_one = swapped(other)
    three_b = along_bands(held, 1)
    one_a, one_b = swapped(upper), swapped(lower)
    applied = call(
        apply_kernel,
        "apply",
        [((width, points), F32)],
        [rotation, mine, mine_one, mine_two, mine_three, proj],
        cost=APPLY,
    )[0]
    return finish(rotation, orbitals, one_a, one_b, two_a, two_b, three_a, three_b, applied)


def solution(mesh):
    in_specs = (P("band", "dom"), P("band", None), P(None, None, "dom"), P("dom", None, None), P())
    out_specs = P("band", "dom")
    return jax.shard_map(
        on_device, mesh=mesh, in_specs=in_specs, out_specs=out_specs, check_vma=False
    )
```

```python
import functools

import jax
import jax.numpy as jnp
from jax import lax
from jax.experimental import pallas as pl
from jax.experimental.pallas import tpu as pltpu
from jax.sharding import PartitionSpec as P

TURN = 1 * 10**9
COUPLE = 2 * 10**9
APPLY = 5 * 10**9
F32 = jnp.float32
BF16 = jnp.bfloat16
ROOM = pltpu.CompilerParams(vmem_limit_bytes=8 * 2**20)
NT = (((1,), (1,)), ((), ()))
VMEM = pl.BlockSpec(memory_space=pltpu.VMEM)
SMEM = pl.BlockSpec(memory_space=pltpu.SMEM)


def flops(count):
    return pl.CostEstimate(flops=count, bytes_accessed=0, transcendentals=0)


def call(kernel, name, outs, args, scratch=(), first=VMEM, cost=0):
    shapes = [jax.ShapeDtypeStruct(*o) for o in outs]
    return pl.pallas_call(
        kernel,
        in_specs=[first] + [VMEM] * (len(args) - 1),
        out_specs=[VMEM] * len(outs),
        out_shape=shapes,
        scratch_shapes=list(scratch),
        compiler_params=ROOM,
        cost_estimate=flops(cost),
        name=name,
    )(*args)


def along_bands(block, distance):
    count = lax.axis_size("band")
    return lax.ppermute(block, "band", [(i, (i + distance) % count) for i in range(count)])


def swapped(block):
    count = lax.axis_size("band")
    return lax.ppermute(block, "band", [(i, i ^ 1) for i in range(count)])


def on_even():
    return lax.axis_index("band") % 2 == 0


def by_permutes():
    count = lax.axis_size("dom")
    return count <= 8 and count & (count - 1) == 0


def from_all_domains(block):
    count = lax.axis_size("dom")
    if by_permutes():
        routes = [[(i, i ^ mask) for i in range(count)] for mask in range(1, count)]
        return [block] + [lax.ppermute(block, "dom", route) for route in routes]
    whole = lax.all_gather(block, "dom")
    return [whole[d] for d in range(count)]


def domain_at(place):
    return lax.axis_index("dom") ^ place if by_permutes() else place


def tile_of(extent, most):
    return max(w for w in range(128, most + 1, 128) if extent % w == 0)


def turn_kernel(coupling_ref, out_ref):
    owned, rank = coupling_ref.shape
    whole = coupling_ref[...]
    high = whole.astype(BF16)
    unit = lax.broadcasted_iota(jnp.int32, (rank, rank), 0) == lax.broadcasted_iota(
        jnp.int32, (rank, rank), 1
    )
    unit = jnp.where(unit, 1.0, 0.0).astype(BF16)
    for i, piece in enumerate((high, (whole - high.astype(F32)).astype(BF16))):
        turned = lax.dot_general(unit, piece, NT, preferred_element_type=F32)
        out_ref[:, i * owned : (i + 1) * owned] = turned.astype(BF16)


def project_kernel(orb_ref, proj_ref, turned_ref, out_ref):
    width, points = orb_ref.shape
    out_ref[width:, : turned_ref.shape[1]] = turned_ref[...]
    tile = tile_of(points, 1024)
    total = None
    for at in range(0, points, tile):
        term = lax.dot_general(
            proj_ref[:, at : at + tile], orb_ref[:, at : at + tile], NT, preferred_element_type=F32
        )
        total = term if total is None else total + term
    out_ref[:width, :] = total.T.astype(BF16)


def project(orbitals, proj, coupling):
    width, points = orbitals.shape
    owned, rank = coupling.shape
    turned = call(
        turn_kernel, "turn", [((rank, 2 * owned), BF16)], [coupling], cost=TURN
    )[0]
    outs = [((width + rank, proj.shape[0]), BF16)]
    return call(project_kernel, "project", outs, [orbitals, proj, turned])[0]


def couple_kernel(count, slots, owned, slot_ref, *refs):
    loads = refs[:count]
    out_ref, pick, high_ref, low_ref = refs[count:]
    width, flat = out_ref.shape
    rank = flat // slots
    me = lax.axis_index("dom")
    lanes = lax.broadcasted_iota(jnp.int32, (rank, flat), 1)
    unit = lanes % rank == lax.broadcasted_iota(jnp.int32, (rank, flat), 0)
    lane_slot = lanes // rank

    atoms = jnp.zeros((rank, flat), jnp.int32)
    for k in range(slots):
        atoms = jnp.where(lane_slot == k, slot_ref[me, k], atoms)

    columns = None
    for place in range(count):
        owner = domain_at(place)
        for a in range(owned):
            hit = unit & (atoms == owner * owned + a)
            pick[a * rank : (a + 1) * rank, :] = jnp.where(hit, 1.0, 0.0).astype(BF16)
        parts = [loads[place][width:, i * owned * rank : (i + 1) * owned * rank] for i in (0, 1)]
        term = jnp.dot(jnp.concatenate(parts, 0), pick[...], preferred_element_type=F32)
        columns = term if columns is None else columns + term
    high, low = columns[:rank], columns[rank:]

    total = None
    for place in range(count):
        domain = domain_at(place)
        for k in range(slots):
            hit = atoms == slot_ref[domain, k]
            rows = slice(k * rank, (k + 1) * rank)
            high_ref[rows, :] = jnp.where(hit, high, 0.0).astype(BF16)
            low_ref[rows, :] = jnp.where(hit, low, 0.0).astype(BF16)
        block = loads[place][:width, :]
        term = jnp.dot(block, high_ref[...], preferred_element_type=F32)
        term += jnp.dot(block, low_ref[...], preferred_element_type=F32)
        total = term if total is None else total + term
    out_ref[...] = total.astype(BF16)


def couple(slot_atom, loads, width, owned):
    flat = loads[0].shape[1]
    slots = slot_atom.shape[1]
    return call(
        functools.partial(couple_kernel, len(loads), slots, owned),
        "couple",
        [((width, flat), BF16)],
        [slot_atom, *loads],
        [
            pltpu.VMEM((owned * (flat // slots), flat), BF16),
            pltpu.VMEM((flat, flat), BF16),
            pltpu.VMEM((flat, flat), BF16),
        ],
        first=SMEM,
        cost=COUPLE,
    )[0]


def hold_kernel(block_ref, after_ref, out_ref):
    out_ref[...] = block_ref[...]


def hold(block, after):
    return call(hold_kernel, "hold", [(block.shape, block.dtype)], [block, after])[0]


def choose_kernel(mine, mine_two, own, two_a, two_b, coef_ref, upper_ref, lower_ref, held_ref):
    cut, half = two_a.shape[0], upper_ref.shape[0]

    @pl.when(on_even())
    def _():
        coef_ref[...] = mine[...]
        upper_ref[...] = own[:half, :]
        lower_ref[...] = own[half:, :]

    @pl.when(jnp.logical_not(on_even()))
    def _():
        coef_ref[...] = mine_two[...]
        upper_ref[...] = two_a[:half, :]
        lower_ref[: cut - half, :] = two_a[half:, :]
        lower_ref[cut - half :, :] = two_b[...]

    held_ref[...] = two_b[...]


def choose(mine, mine_two, own, two_a, two_b):
    args = [mine, mine_two, own, two_a, two_b]
    half = ((own.shape[0] // 2, own.shape[1]), own.dtype)
    outs = [(mine.shape, mine.dtype), half, half, (two_b.shape, two_b.dtype)]
    return call(choose_kernel, "choose", outs, args)


def apply_kernel(rot_ref, mine, one, two, three, proj_ref, out_ref):
    width, flat = mine.shape
    points = proj_ref.shape[1]
    mixed = None
    blocks = [mine, one, two, three]
    for s, block in enumerate(blocks):
        term = jnp.dot(
            rot_ref[:, s * width : (s + 1) * width], block[...], preferred_element_type=F32
        )
        mixed = term if mixed is None else mixed + term
    mixed = mixed.astype(BF16)
    tile = tile_of(points, 1024)
    for at in range(0, points, tile):
        out_ref[:, at : at + tile] = jnp.dot(
            mixed, proj_ref[:, at : at + tile], preferred_element_type=F32
        )


def gather_kernel(rot_ref, own, one_a, two_a, two_b, three_a, out_ref, stack):
    width, points = own.shape
    first, second = width + one_a.shape[0], 2 * width
    turn = jnp.concatenate(
        [rot_ref[:, :first], rot_ref[:, second : second + stack.shape[0] - first]], axis=1
    )
    tile = tile_of(points, 1024)
    for i in range(points // tile):
        here = slice(i * tile, (i + 1) * tile)
        at = 0
        for ref in (own, one_a, two_a, two_b, three_a):
            stack[at : at + ref.shape[0], here] = ref[:, here]
            at += ref.shape[0]
        out_ref[:, here] = jnp.dot(turn, stack[:, here], preferred_element_type=F32)


def gather(rotation, *blocks):
    width, points = blocks[0].shape
    depth = sum(block.shape[0] for block in blocks)
    scratch = [pltpu.VMEM((depth, points), BF16)]
    return call(
        gather_kernel, "gather", [((width, points), F32)], [rotation, *blocks], scratch
    )[0]


def finish_kernel(rot_ref, partial_ref, one_b, three_b, applied, out_hbm, out_ref, sems):
    width, points = out_ref.shape
    pieces = sems.shape[0]
    tile = points // pieces
    turn = jnp.concatenate(
        [
            rot_ref[:, 2 * width - one_b.shape[0] : 2 * width],
            rot_ref[:, 4 * width - three_b.shape[0] :],
        ],
        axis=1,
    )
    copies = []
    for i in range(pieces):
        here = slice(i * tile, (i + 1) * tile)
        last = jnp.concatenate([one_b[:, here], three_b[:, here]], axis=0)
        rotated = partial_ref[:, here] + jnp.dot(turn, last, preferred_element_type=F32)
        added = rotated.astype(BF16).astype(F32) + applied[:, here]
        out_ref[:, here] = added.astype(out_ref.dtype)
        part = (slice(None), pl.ds(i * tile, tile))
        copies.append(pltpu.make_async_copy(out_ref.at[part], out_hbm.at[part], sems.at[i]))
        copies[-1].start()
    for copy in copies:
        copy.wait()


def finish(*args):
    width, points = args[-1].shape
    pieces = points // tile_of(points, 1024)
    return pl.pallas_call(
        finish_kernel,
        in_specs=[VMEM] * len(args),
        out_specs=pl.BlockSpec(memory_space=pl.ANY),
        out_shape=jax.ShapeDtypeStruct((width, points), BF16),
        scratch_shapes=[pltpu.VMEM((width, points), BF16), pltpu.SemaphoreType.DMA((pieces,))],
        compiler_params=ROOM,
        cost_estimate=flops(0),
        name="finish",
    )(*args)


def on_device(orbitals, rotation, projectors, coupling, slot_atom):
    width, points = orbitals.shape
    slot_count, rank, _ = projectors.shape
    owned = coupling.shape[0]
    proj = projectors.reshape(slot_count * rank, points)

    cut = width * 3 // 4
    two_a = along_bands(orbitals[:cut], 2)
    two_b = along_bands(orbitals[cut:], 2)
    loads = from_all_domains(project(orbitals, proj, coupling.reshape(owned * rank, rank)))
    mine = couple(slot_atom, loads, width, owned)
    mine_two = along_bands(mine, 2)
    three_a = along_bands(hold(two_a, mine), 1)
    other, upper, lower, held = choose(mine, mine_two, orbitals, two_a, two_b)
    mine_three = along_bands(mine_two, 1)
    mine_one = swapped(other)
    three_b = along_bands(held, 1)
    one_a, one_b = swapped(upper), swapped(lower)
    applied = call(
        apply_kernel,
        "apply",
        [((width, points), F32)],
        [rotation, mine, mine_one, mine_two, mine_three, proj],
        cost=APPLY,
    )[0]
    partial = gather(rotation, orbitals, one_a, two_a, two_b, three_a)
    return finish(rotation, partial, one_b, three_b, applied)


def solution(mesh):
    in_specs = (P("band", "dom"), P("band", None), P(None, None, "dom"), P("dom", None, None), P())
    out_specs = P("band", "dom")
    return jax.shard_map(
        on_device, mesh=mesh, in_specs=in_specs, out_specs=out_specs, check_vma=False
    )
```

```python
import functools

import jax
import jax.numpy as jnp
from jax import lax
from jax.experimental import pallas as pl
from jax.experimental.pallas import tpu as pltpu
from jax.sharding import PartitionSpec as P

TURN = 3 * 10**9
COUPLE = 2 * 10**9
APPLY = 60 * 10**8
SELECT = 20 * 10**8
F32 = jnp.float32
BF16 = jnp.bfloat16
ROOM = pltpu.CompilerParams(vmem_limit_bytes=8 * 2**20)
NT = (((1,), (1,)), ((), ()))
VMEM = pl.BlockSpec(memory_space=pltpu.VMEM)
SMEM = pl.BlockSpec(memory_space=pltpu.SMEM)


def flops(count):
    return pl.CostEstimate(flops=count, bytes_accessed=0, transcendentals=0)


def call(kernel, name, outs, args, scratch=(), first=VMEM, cost=0):
    shapes = [jax.ShapeDtypeStruct(*o) for o in outs]
    return pl.pallas_call(
        kernel,
        in_specs=[first] + [VMEM] * (len(args) - 1),
        out_specs=[VMEM] * len(outs),
        out_shape=shapes,
        scratch_shapes=list(scratch),
        compiler_params=ROOM,
        cost_estimate=flops(cost),
        name=name,
    )(*args)


def along_bands(block, distance):
    count = lax.axis_size("band")
    return lax.ppermute(block, "band", [(i, (i + distance) % count) for i in range(count)])


def swapped(block):
    count = lax.axis_size("band")
    return lax.ppermute(block, "band", [(i, i ^ 1) for i in range(count)])


def on_even():
    return lax.axis_index("band") % 2 == 0


def by_permutes():
    count = lax.axis_size("dom")
    return count <= 8 and count & (count - 1) == 0


def from_all_domains(block):
    count = lax.axis_size("dom")
    if by_permutes():
        routes = [[(i, i ^ mask) for i in range(count)] for mask in range(1, count)]
        return [block] + [lax.ppermute(block, "dom", route) for route in routes]
    whole = lax.all_gather(block, "dom")
    return [whole[d] for d in range(count)]


def domain_at(place):
    return lax.axis_index("dom") ^ place if by_permutes() else place


def tile_of(extent, most):
    return max(w for w in range(128, most + 1, 128) if extent % w == 0)


def turn_kernel(coupling_ref, out_ref):
    owned, rank = coupling_ref.shape
    whole = coupling_ref[...]
    high = whole.astype(BF16)
    unit = lax.broadcasted_iota(jnp.int32, (rank, rank), 0) == lax.broadcasted_iota(
        jnp.int32, (rank, rank), 1
    )
    unit = jnp.where(unit, 1.0, 0.0).astype(BF16)
    for i, piece in enumerate((high, (whole - high.astype(F32)).astype(BF16))):
        turned = lax.dot_general(unit, piece, NT, preferred_element_type=F32)
        out_ref[:, i * owned : (i + 1) * owned] = turned.astype(BF16)


def project_kernel(orb_ref, proj_ref, turned_ref, out_ref):
    width, points = orb_ref.shape
    out_ref[width:, : turned_ref.shape[1]] = turned_ref[...]
    tile = tile_of(points, 1024)
    total = None
    for at in range(0, points, tile):
        term = lax.dot_general(
            proj_ref[:, at : at + tile], orb_ref[:, at : at + tile], NT, preferred_element_type=F32
        )
        total = term if total is None else total + term
    out_ref[:width, :] = total.T.astype(BF16)


def project(orbitals, proj, coupling):
    width, points = orbitals.shape
    owned, rank = coupling.shape
    turned = call(
        turn_kernel, "turn", [((rank, 2 * owned), BF16)], [coupling], cost=TURN
    )[0]
    outs = [((width + rank, proj.shape[0]), BF16)]
    return call(project_kernel, "project", outs, [orbitals, proj, turned])[0]


def couple_kernel(count, slots, owned, slot_ref, *refs):
    loads, pass_ref = refs[:count], refs[count]
    out_ref, passed_ref, pick, high_ref, low_ref = refs[count + 1 :]
    passed_ref[...] = pass_ref[...]
    width, flat = out_ref.shape
    rank = flat // slots
    me = lax.axis_index("dom")
    lanes = lax.broadcasted_iota(jnp.int32, (rank, flat), 1)
    unit = lanes % rank == lax.broadcasted_iota(jnp.int32, (rank, flat), 0)
    lane_slot = lanes // rank

    atoms = jnp.zeros((rank, flat), jnp.int32)
    for k in range(slots):
        atoms = jnp.where(lane_slot == k, slot_ref[me, k], atoms)

    columns = None
    for place in range(count):
        owner = domain_at(place)
        for a in range(owned):
            hit = unit & (atoms == owner * owned + a)
            pick[a * rank : (a + 1) * rank, :] = jnp.where(hit, 1.0, 0.0).astype(BF16)
        parts = [loads[place][width:, i * owned * rank : (i + 1) * owned * rank] for i in (0, 1)]
        term = jnp.dot(jnp.concatenate(parts, 0), pick[...], preferred_element_type=F32)
        columns = term if columns is None else columns + term
    high, low = columns[:rank], columns[rank:]

    total = None
    for place in range(count):
        domain = domain_at(place)
        for k in range(slots):
            hit = atoms == slot_ref[domain, k]
            rows = slice(k * rank, (k + 1) * rank)
            high_ref[rows, :] = jnp.where(hit, high, 0.0).astype(BF16)
            low_ref[rows, :] = jnp.where(hit, low, 0.0).astype(BF16)
        block = loads[place][:width, :]
        term = jnp.dot(block, high_ref[...], preferred_element_type=F32)
        term += jnp.dot(block, low_ref[...], preferred_element_type=F32)
        total = term if total is None else total + term
    out_ref[...] = total.astype(BF16)


def couple(slot_atom, loads, width, owned, passed):
    flat = loads[0].shape[1]
    slots = slot_atom.shape[1]
    return call(
        functools.partial(couple_kernel, len(loads), slots, owned),
        "couple",
        [((width, flat), BF16), (passed.shape, passed.dtype)],
        [slot_atom, *loads, passed],
        [
            pltpu.VMEM((owned * (flat // slots), flat), BF16),
            pltpu.VMEM((flat, flat), BF16),
            pltpu.VMEM((flat, flat), BF16),
        ],
        first=SMEM,
        cost=COUPLE,
    )


def hold_kernel(block_ref, after_ref, out_ref):
    out_ref[...] = block_ref[...]


def hold(block, after):
    return call(hold_kernel, "hold", [(block.shape, block.dtype)], [block, after])[0]


def select_kernel(even_ref, odd_ref, out_ref, odd_again_ref):
    odd_again_ref[...] = odd_ref[...]

    @pl.when(on_even())
    def _():
        out_ref[...] = even_ref[...]

    @pl.when(jnp.logical_not(on_even()))
    def _():
        out_ref[...] = odd_ref[...]


def select(for_even, for_odd):
    outs = [(for_even.shape, for_even.dtype)] * 2
    return call(select_kernel, "select", outs, [for_even, for_odd], cost=SELECT)


def choose_kernel(own, two_a, two_b, after_ref, upper_ref, lower_ref, held_ref):
    cut, half = two_a.shape[0], upper_ref.shape[0]

    @pl.when(on_even())
    def _():
        upper_ref[...] = own[:half, :]
        lower_ref[...] = own[half:, :]

    @pl.when(jnp.logical_not(on_even()))
    def _():
        upper_ref[...] = two_a[:half, :]
        lower_ref[: cut - half, :] = two_a[half:, :]
        lower_ref[cut - half :, :] = two_b[...]

    held_ref[...] = two_b[...]


def choose(own, two_a, two_b, after):
    half = ((own.shape[0] // 2, own.shape[1]), own.dtype)
    outs = [half, half, (two_b.shape, two_b.dtype)]
    return call(choose_kernel, "choose", outs, [own, two_a, two_b, after])


def apply_kernel(rot_ref, mine, one, two, three, proj_ref, out_ref):
    width, flat = mine.shape
    points = proj_ref.shape[1]
    mixed = None
    blocks = [mine, one, two, three]
    for s, block in enumerate(blocks):
        term = jnp.dot(
            rot_ref[:, s * width : (s + 1) * width], block[...], preferred_element_type=F32
        )
        mixed = term if mixed is None else mixed + term
    mixed = mixed.astype(BF16)
    tile = tile_of(points, 1024)
    for at in range(0, points, tile):
        out_ref[:, at : at + tile] = jnp.dot(
            mixed, proj_ref[:, at : at + tile], preferred_element_type=F32
        )


def gather_kernel(rot_ref, own, one_a, two_a, two_b, three_a, out_ref, stack):
    width, points = own.shape
    first, second = width + one_a.shape[0], 2 * width
    turn = jnp.concatenate(
        [rot_ref[:, :first], rot_ref[:, second : second + stack.shape[0] - first]], axis=1
    )
    tile = tile_of(points, 1024)
    for i in range(points // tile):
        here = slice(i * tile, (i + 1) * tile)
        at = 0
        for ref in (own, one_a, two_a, two_b, three_a):
            stack[at : at + ref.shape[0], here] = ref[:, here]
            at += ref.shape[0]
        out_ref[:, here] = jnp.dot(turn, stack[:, here], preferred_element_type=F32)


def gather(rotation, *blocks):
    width, points = blocks[0].shape
    depth = sum(block.shape[0] for block in blocks)
    scratch = [pltpu.VMEM((depth, points), BF16)]
    return call(
        gather_kernel, "gather", [((width, points), F32)], [rotation, *blocks], scratch
    )[0]


def finish_kernel(rot_ref, partial_ref, one_b, three_b, applied, out_hbm, out_ref, sems):
    width, points = out_ref.shape
    pieces = sems.shape[0]
    tile = points // pieces
    turn = jnp.concatenate(
        [
            rot_ref[:, 2 * width - one_b.shape[0] : 2 * width],
            rot_ref[:, 4 * width - three_b.shape[0] :],
        ],
        axis=1,
    )
    copies = []
    for i in range(pieces):
        here = slice(i * tile, (i + 1) * tile)
        last = jnp.concatenate([one_b[:, here], three_b[:, here]], axis=0)
        rotated = partial_ref[:, here] + jnp.dot(turn, last, preferred_element_type=F32)
        added = rotated.astype(BF16).astype(F32) + applied[:, here]
        out_ref[:, here] = added.astype(out_ref.dtype)
        part = (slice(None), pl.ds(i * tile, tile))
        copies.append(pltpu.make_async_copy(out_ref.at[part], out_hbm.at[part], sems.at[i]))
        copies[-1].start()
    for copy in copies:
        copy.wait()


def finish(*args):
    width, points = args[-1].shape
    pieces = points // tile_of(points, 1024)
    return pl.pallas_call(
        finish_kernel,
        in_specs=[VMEM] * len(args),
        out_specs=pl.BlockSpec(memory_space=pl.ANY),
        out_shape=jax.ShapeDtypeStruct((width, points), BF16),
        scratch_shapes=[pltpu.VMEM((width, points), BF16), pltpu.SemaphoreType.DMA((pieces,))],
        compiler_params=ROOM,
        cost_estimate=flops(0),
        name="finish",
    )(*args)


def on_device(orbitals, rotation, projectors, coupling, slot_atom):
    width, points = orbitals.shape
    slot_count, rank, _ = projectors.shape
    owned = coupling.shape[0]
    proj = projectors.reshape(slot_count * rank, points)

    cut = width * 3 // 4
    two_a = along_bands(orbitals[:cut], 2)
    loads = from_all_domains(project(orbitals, proj, coupling.reshape(owned * rank, rank)))
    mine, own_b = couple(slot_atom, loads, width, owned, orbitals[cut:])
    mine_two = along_bands(mine, 2)
    two_b = along_bands(own_b, 2)
    other, mine_two = select(mine, mine_two)
    mine_three = along_bands(mine_two, 1)
    mine_one = swapped(other)
    three_a = along_bands(hold(two_a, other), 1)
    upper, lower, held = choose(orbitals, two_a, two_b, other)
    three_b = along_bands(held, 1)
    one_a, one_b = swapped(upper), swapped(lower)
    applied = call(
        apply_kernel,
        "apply",
        [((width, points), F32)],
        [rotation, mine, mine_one, mine_two, mine_three, proj],
        cost=APPLY,
    )[0]
    partial = gather(rotation, orbitals, one_a, two_a, two_b, three_a)
    return finish(rotation, partial, one_b, three_b, applied)


def solution(mesh):
    in_specs = (P("band", "dom"), P("band", None), P(None, None, "dom"), P("dom", None, None), P())
    out_specs = P("band", "dom")
    return jax.shard_map(
        on_device, mesh=mesh, in_specs=in_specs, out_specs=out_specs, check_vma=False
    )
```

```python
import functools

import jax
import jax.numpy as jnp
from jax import lax
from jax.experimental import pallas as pl
from jax.experimental.pallas import tpu as pltpu
from jax.sharding import PartitionSpec as P

TURN = 3 * 10**9
COUPLE = 2 * 10**9
APPLY = 50 * 10**8
GATHER = 45 * 10**8

F32 = jnp.float32
BF16 = jnp.bfloat16
ROOM = pltpu.CompilerParams(vmem_limit_bytes=8 * 2**20)
NT = (((1,), (1,)), ((), ()))
VMEM = pl.BlockSpec(memory_space=pltpu.VMEM)
SMEM = pl.BlockSpec(memory_space=pltpu.SMEM)


def flops(count):
    return pl.CostEstimate(flops=count, bytes_accessed=0, transcendentals=0)


def call(kernel, name, outs, args, scratch=(), first=VMEM, cost=0):
    shapes = [jax.ShapeDtypeStruct(*o) for o in outs]
    return pl.pallas_call(
        kernel,
        in_specs=[first] + [VMEM] * (len(args) - 1),
        out_specs=[VMEM] * len(outs),
        out_shape=shapes,
        scratch_shapes=list(scratch),
        compiler_params=ROOM,
        cost_estimate=flops(cost),
        name=name,
    )(*args)


def along_bands(block, distance):
    count = lax.axis_size("band")
    return lax.ppermute(block, "band", [(i, (i + distance) % count) for i in range(count)])


def swapped(block):
    count = lax.axis_size("band")
    return lax.ppermute(block, "band", [(i, i ^ 1) for i in range(count)])


def on_even():
    return lax.axis_index("band") % 2 == 0


def by_permutes():
    count = lax.axis_size("dom")
    return count <= 8 and count & (count - 1) == 0


def from_all_domains(block):
    count = lax.axis_size("dom")
    if by_permutes():
        routes = [[(i, i ^ mask) for i in range(count)] for mask in range(1, count)]
        return [block] + [lax.ppermute(block, "dom", route) for route in routes]
    whole = lax.all_gather(block, "dom")
    return [whole[d] for d in range(count)]


def domain_at(place):
    return lax.axis_index("dom") ^ place if by_permutes() else place


def tile_of(extent, most):
    return max(w for w in range(128, most + 1, 128) if extent % w == 0)


def turn_kernel(coupling_ref, out_ref):
    owned, rank = coupling_ref.shape
    whole = coupling_ref[...]
    high = whole.astype(BF16)
    unit = lax.broadcasted_iota(jnp.int32, (rank, rank), 0) == lax.broadcasted_iota(
        jnp.int32, (rank, rank), 1
    )
    unit = jnp.where(unit, 1.0, 0.0).astype(BF16)
    for i, piece in enumerate((high, (whole - high.astype(F32)).astype(BF16))):
        turned = lax.dot_general(unit, piece, NT, preferred_element_type=F32)
        out_ref[:, i * owned : (i + 1) * owned] = turned.astype(BF16)


def project_kernel(orb_ref, proj_ref, turned_ref, out_ref):
    width, points = orb_ref.shape
    out_ref[width:, : turned_ref.shape[1]] = turned_ref[...]
    tile = tile_of(points, 1024)
    total = None
    for at in range(0, points, tile):
        term = lax.dot_general(
            proj_ref[:, at : at + tile], orb_ref[:, at : at + tile], NT, preferred_element_type=F32
        )
        total = term if total is None else total + term
    out_ref[:width, :] = total.T.astype(BF16)


def project(orbitals, proj, coupling):
    width, points = orbitals.shape
    owned, rank = coupling.shape
    turned = call(
        turn_kernel, "turn", [((rank, 2 * owned), BF16)], [coupling], cost=TURN
    )[0]
    outs = [((width + rank, proj.shape[0]), BF16)]
    return call(project_kernel, "project", outs, [orbitals, proj, turned])[0]


def couple_kernel(count, slots, owned, slot_ref, *refs):
    loads = refs[:count]
    out_ref, pick, high_ref, low_ref = refs[count:]
    width, flat = out_ref.shape
    rank = flat // slots
    me = lax.axis_index("dom")
    lanes = lax.broadcasted_iota(jnp.int32, (rank, flat), 1)
    unit = lanes % rank == lax.broadcasted_iota(jnp.int32, (rank, flat), 0)
    lane_slot = lanes // rank

    atoms = jnp.zeros((rank, flat), jnp.int32)
    for k in range(slots):
        atoms = jnp.where(lane_slot == k, slot_ref[me, k], atoms)

    columns = None
    for place in range(count):
        owner = domain_at(place)
        for a in range(owned):
            hit = unit & (atoms == owner * owned + a)
            pick[a * rank : (a + 1) * rank, :] = jnp.where(hit, 1.0, 0.0).astype(BF16)
        parts = [loads[place][width:, i * owned * rank : (i + 1) * owned * rank] for i in (0, 1)]
        term = jnp.dot(jnp.concatenate(parts, 0), pick[...], preferred_element_type=F32)
        columns = term if columns is None else columns + term
    high, low = columns[:rank], columns[rank:]

    total = None
    for place in range(count):
        domain = domain_at(place)
        for k in range(slots):
            hit = atoms == slot_ref[domain, k]
            rows = slice(k * rank, (k + 1) * rank)
            high_ref[rows, :] = jnp.where(hit, high, 0.0).astype(BF16)
            low_ref[rows, :] = jnp.where(hit, low, 0.0).astype(BF16)
        block = loads[place][:width, :]
        term = jnp.dot(block, high_ref[...], preferred_element_type=F32)
        term += jnp.dot(block, low_ref[...], preferred_element_type=F32)
        total = term if total is None else total + term
    out_ref[...] = total.astype(BF16)


def couple(slot_atom, loads, width, owned):
    flat = loads[0].shape[1]
    slots = slot_atom.shape[1]
    return call(
        functools.partial(couple_kernel, len(loads), slots, owned),
        "couple",
        [((width, flat), BF16)],
        [slot_atom, *loads],
        [
            pltpu.VMEM((owned * (flat // slots), flat), BF16),
            pltpu.VMEM((flat, flat), BF16),
            pltpu.VMEM((flat, flat), BF16),
        ],
        first=SMEM,
        cost=COUPLE,
    )[0]


def hold_kernel(block_ref, after_ref, out_ref):
    out_ref[...] = block_ref[...]


def hold(block, after):
    return call(hold_kernel, "hold", [(block.shape, block.dtype)], [block, after])[0]


def packed(coef_shape, rows):
    width, flat = coef_shape
    return [
        (slice(i * flat, (i + 1) * flat), slice(i * rows, (i + 1) * rows))
        for i in range(width // rows)
    ]


def choose_kernel(mine, mine_two, own, two_a, two_b, swap_ref, *held_refs):
    width, cut = own.shape[0], two_a.shape[0]
    parts = packed(mine.shape, two_b.shape[0])

    @pl.when(on_even())
    def _():
        swap_ref[:width, :] = own[...]
        for columns, rows in parts:
            swap_ref[width:, columns] = mine[rows, :]

    @pl.when(jnp.logical_not(on_even()))
    def _():
        swap_ref[:cut, :] = two_a[...]
        swap_ref[cut:width, :] = two_b[...]
        for columns, rows in parts:
            swap_ref[width:, columns] = mine_two[rows, :]

    at = 0
    for ref in held_refs:
        ref[...] = two_b[:, at : at + ref.shape[1]]
        at += ref.shape[1]


def choose(mine, mine_two, own, two_a, two_b):
    args = [mine, mine_two, own, two_a, two_b]
    rows, points = two_b.shape
    last = points * 7 // 12 // 128 * 128
    outs = [((own.shape[0] + rows, points), own.dtype)]
    outs += [((rows, extent), own.dtype) for extent in (points - last, last)]
    return call(choose_kernel, "choose", outs, args)


def gather_kernel(rot_ref, own, two_a, two_b, three_a, out_ref, stack):
    width, points = own.shape
    depth = stack.shape[0]
    turn = jnp.concatenate([rot_ref[:, :width], rot_ref[:, 2 * width : width + depth]], axis=1)
    tile = tile_of(points, 1024)
    for i in range(points // tile):
        here = slice(i * tile, (i + 1) * tile)
        at = 0
        for ref in (own, two_a, two_b, three_a):
            stack[at : at + ref.shape[0], here] = ref[:, here]
            at += ref.shape[0]
        out_ref[:, here] = jnp.dot(turn, stack[:, here], preferred_element_type=F32)


def gather(rotation, *blocks):
    width, points = blocks[0].shape
    depth = sum(block.shape[0] for block in blocks)
    scratch = [pltpu.VMEM((depth, points), BF16)]
    return call(
        gather_kernel, "gather", [((width, points), F32)], [rotation, *blocks], scratch, cost=GATHER
    )[0]


def apply_kernel(rot_ref, mine, swap_ref, two, three, proj_ref, after_ref, out_ref):
    width, flat = mine.shape
    points = proj_ref.shape[1]
    one = [swap_ref[width:, columns] for columns, _ in packed(mine.shape, swap_ref.shape[0] - width)]
    blocks = (mine[...], jnp.concatenate(one, axis=0), two[...], three[...])
    mixed = sum(
        jnp.dot(rot_ref[:, s * width : (s + 1) * width], block, preferred_element_type=F32)
        for s, block in enumerate(blocks)
    )
    mixed = mixed.astype(BF16)
    tile = tile_of(points, 1024)
    for at in range(0, points, tile):
        out_ref[:, at : at + tile] = jnp.dot(
            mixed, proj_ref[:, at : at + tile], preferred_element_type=F32
        )


def finish_kernel(start, rot_ref, partial_ref, swap_ref, last_ref, applied, *refs):
    out_hbm, out_ref, sems = refs[-3:]
    width, extent = out_ref.shape
    rows = last_ref.shape[0]
    pieces = sems.shape[0]
    tile = extent // pieces
    turn = jnp.concatenate(
        [rot_ref[:, width : 2 * width], rot_ref[:, rot_ref.shape[1] - rows :]], axis=1
    )
    copies = []
    for i in range(pieces):
        here = slice(i * tile, (i + 1) * tile)
        there = slice(start + i * tile, start + (i + 1) * tile)
        last = jnp.concatenate([swap_ref[:width, there], last_ref[:, here]], axis=0)
        rotated = partial_ref[:, there] + jnp.dot(turn, last, preferred_element_type=F32)
        added = rotated.astype(BF16).astype(F32) + applied[:, there]
        out_ref[:, here] = added.astype(out_ref.dtype)
        copies.append(
            pltpu.make_async_copy(
                out_ref.at[:, pl.ds(i * tile, tile)],
                out_hbm.at[:, pl.ds(start + i * tile, tile)],
                sems.at[i],
            )
        )
        copies[-1].start()
    for copy in copies:
        copy.wait()


def finish(start, rotation, partial, swap, last, applied, so_far):
    width, points = applied.shape
    extent = last.shape[1]
    pieces = extent // tile_of(extent, 1024)
    args = [rotation, partial, swap, last, applied]
    specs = [VMEM] * len(args)
    alias = {}
    if so_far is not None:
        alias = {len(args): 0}
        args.append(so_far)
        specs.append(pl.BlockSpec(memory_space=pl.ANY))
    return pl.pallas_call(
        functools.partial(finish_kernel, start),
        in_specs=specs,
        out_specs=pl.BlockSpec(memory_space=pl.ANY),
        out_shape=jax.ShapeDtypeStruct((width, points), BF16),
        scratch_shapes=[pltpu.VMEM((width, extent), BF16), pltpu.SemaphoreType.DMA((pieces,))],
        input_output_aliases=alias,
        compiler_params=ROOM,
        cost_estimate=flops(0),
        name="finish",
    )(*args)


def on_device(orbitals, rotation, projectors, coupling, slot_atom):
    width, points = orbitals.shape
    slot_count, rank, _ = projectors.shape
    owned = coupling.shape[0]
    proj = projectors.reshape(slot_count * rank, points)

    cut = width * 3 // 4
    two_a = along_bands(orbitals[:cut], 2)
    two_b = along_bands(orbitals[cut:], 2)
    loads = from_all_domains(project(orbitals, proj, coupling.reshape(owned * rank, rank)))
    mine = couple(slot_atom, loads, width, owned)
    mine_two = along_bands(mine, 2)
    three_a = along_bands(hold(two_a, mine), 1)
    swap, *held = choose(mine, mine_two, orbitals, two_a, two_b)
    mine_three = along_bands(mine_two, 1)
    swap = swapped(swap)
    three_b = [along_bands(block, 1) for block in held]
    partial = gather(rotation, orbitals, two_a, two_b, three_a)
    applied = call(
        apply_kernel,
        "apply",
        [((width, points), F32)],
        [rotation, mine, swap, mine_two, mine_three, proj, partial],
        cost=APPLY,
    )[0]
    out, start = None, 0
    for last in three_b:
        out = finish(start, rotation, partial, swap, last, applied, out)
        start += last.shape[1]
    return out


def solution(mesh):
    in_specs = (P("band", "dom"), P("band", None), P(None, None, "dom"), P("dom", None, None), P())
    out_specs = P("band", "dom")
    return jax.shard_map(
        on_device, mesh=mesh, in_specs=in_specs, out_specs=out_specs, check_vma=False
    )
```

```python
import functools

import jax
import jax.numpy as jnp
from jax import lax
from jax.experimental import pallas as pl
from jax.experimental.pallas import tpu as pltpu
from jax.sharding import PartitionSpec as P

TURN = 3 * 10**9
COUPLE = 2 * 10**9
APPLY = 50 * 10**8
GATHER = 66 * 10**8

F32 = jnp.float32
BF16 = jnp.bfloat16
ROOM = pltpu.CompilerParams(vmem_limit_bytes=8 * 2**20)
NT = (((1,), (1,)), ((), ()))
VMEM = pl.BlockSpec(memory_space=pltpu.VMEM)
SMEM = pl.BlockSpec(memory_space=pltpu.SMEM)


def flops(count):
    return pl.CostEstimate(flops=count, bytes_accessed=0, transcendentals=0)


def call(kernel, name, outs, args, scratch=(), first=VMEM, cost=0):
    shapes = [jax.ShapeDtypeStruct(*o) for o in outs]
    return pl.pallas_call(
        kernel,
        in_specs=[first] + [VMEM] * (len(args) - 1),
        out_specs=[VMEM] * len(outs),
        out_shape=shapes,
        scratch_shapes=list(scratch),
        compiler_params=ROOM,
        cost_estimate=flops(cost),
        name=name,
    )(*args)


def along_bands(block, distance):
    count = lax.axis_size("band")
    return lax.ppermute(block, "band", [(i, (i + distance) % count) for i in range(count)])


def swapped(block):
    count = lax.axis_size("band")
    return lax.ppermute(block, "band", [(i, i ^ 1) for i in range(count)])


def on_even():
    return lax.axis_index("band") % 2 == 0


def by_permutes():
    count = lax.axis_size("dom")
    return count <= 8 and count & (count - 1) == 0


def from_all_domains(block):
    count = lax.axis_size("dom")
    if by_permutes():
        routes = [[(i, i ^ mask) for i in range(count)] for mask in range(1, count)]
        return [block] + [lax.ppermute(block, "dom", route) for route in routes]
    whole = lax.all_gather(block, "dom")
    return [whole[d] for d in range(count)]


def domain_at(place):
    return lax.axis_index("dom") ^ place if by_permutes() else place


def tile_of(extent, most):
    return max(w for w in range(128, most + 1, 128) if extent % w == 0)


def turn_kernel(coupling_ref, out_ref):
    owned, rank = coupling_ref.shape
    whole = coupling_ref[...]
    high = whole.astype(BF16)
    unit = lax.broadcasted_iota(jnp.int32, (rank, rank), 0) == lax.broadcasted_iota(
        jnp.int32, (rank, rank), 1
    )
    unit = jnp.where(unit, 1.0, 0.0).astype(BF16)
    for i, piece in enumerate((high, (whole - high.astype(F32)).astype(BF16))):
        turned = lax.dot_general(unit, piece, NT, preferred_element_type=F32)
        out_ref[:, i * owned : (i + 1) * owned] = turned.astype(BF16)


def project_kernel(orb_ref, proj_ref, turned_ref, out_ref):
    width, points = orb_ref.shape
    out_ref[width:, : turned_ref.shape[1]] = turned_ref[...]
    tile = tile_of(points, 1024)
    total = None
    for at in range(0, points, tile):
        term = lax.dot_general(
            proj_ref[:, at : at + tile], orb_ref[:, at : at + tile], NT, preferred_element_type=F32
        )
        total = term if total is None else total + term
    out_ref[:width, :] = total.T.astype(BF16)


def project(orbitals, proj, coupling):
    width, points = orbitals.shape
    owned, rank = coupling.shape
    turned = call(
        turn_kernel, "turn", [((rank, 2 * owned), BF16)], [coupling], cost=TURN
    )[0]
    outs = [((width + rank, proj.shape[0]), BF16)]
    return call(project_kernel, "project", outs, [orbitals, proj, turned])[0]


def couple_kernel(count, slots, owned, slot_ref, *refs):
    loads = refs[:count]
    out_ref, pick, high_ref, low_ref = refs[count:]
    width, flat = out_ref.shape
    rank = flat // slots
    me = lax.axis_index("dom")
    lanes = lax.broadcasted_iota(jnp.int32, (rank, flat), 1)
    unit = lanes % rank == lax.broadcasted_iota(jnp.int32, (rank, flat), 0)
    lane_slot = lanes // rank

    atoms = jnp.zeros((rank, flat), jnp.int32)
    for k in range(slots):
        atoms = jnp.where(lane_slot == k, slot_ref[me, k], atoms)

    columns = None
    for place in range(count):
        owner = domain_at(place)
        for a in range(owned):
            hit = unit & (atoms == owner * owned + a)
            pick[a * rank : (a + 1) * rank, :] = jnp.where(hit, 1.0, 0.0).astype(BF16)
        parts = [loads[place][width:, i * owned * rank : (i + 1) * owned * rank] for i in (0, 1)]
        term = jnp.dot(jnp.concatenate(parts, 0), pick[...], preferred_element_type=F32)
        columns = term if columns is None else columns + term
    high, low = columns[:rank], columns[rank:]

    total = None
    for place in range(count):
        domain = domain_at(place)
        for k in range(slots):
            hit = atoms == slot_ref[domain, k]
            rows = slice(k * rank, (k + 1) * rank)
            high_ref[rows, :] = jnp.where(hit, high, 0.0).astype(BF16)
            low_ref[rows, :] = jnp.where(hit, low, 0.0).astype(BF16)
        block = loads[place][:width, :]
        term = jnp.dot(block, high_ref[...], preferred_element_type=F32)
        term += jnp.dot(block, low_ref[...], preferred_element_type=F32)
        total = term if total is None else total + term
    out_ref[...] = total.astype(BF16)


def couple(slot_atom, loads, width, owned):
    flat = loads[0].shape[1]
    slots = slot_atom.shape[1]
    return call(
        functools.partial(couple_kernel, len(loads), slots, owned),
        "couple",
        [((width, flat), BF16)],
        [slot_atom, *loads],
        [
            pltpu.VMEM((owned * (flat // slots), flat), BF16),
            pltpu.VMEM((flat, flat), BF16),
            pltpu.VMEM((flat, flat), BF16),
        ],
        first=SMEM,
        cost=COUPLE,
    )[0]


def lower_kernel(block_ref, out_ref):
    out_ref[...] = block_ref[block_ref.shape[0] - out_ref.shape[0] :, :]


def lower(block, rows):
    return call(lower_kernel, "lower", [((rows, block.shape[1]), block.dtype)], [block])[0]


def hold_kernel(block_ref, after_ref, out_ref):
    out_ref[...] = block_ref[...]


def hold(block, after):
    return call(hold_kernel, "hold", [(block.shape, block.dtype)], [block, after])[0]


def packed(coef_shape, rows):
    width, flat = coef_shape
    return [
        (slice(i * flat, (i + 1) * flat), slice(i * rows, (i + 1) * rows))
        for i in range(width // rows)
    ]


def choose_kernel(mine, mine_two, own, two_a, two_b, swap_ref, held_ref):
    width, cut = own.shape[0], two_a.shape[0]
    parts = packed(mine.shape, swap_ref.shape[0] - width)

    @pl.when(on_even())
    def _():
        swap_ref[:width, :] = own[...]
        for columns, rows in parts:
            swap_ref[width:, columns] = mine[rows, :]

    @pl.when(jnp.logical_not(on_even()))
    def _():
        swap_ref[:cut, :] = two_a[...]
        swap_ref[cut:width, :] = two_b[...]
        for columns, rows in parts:
            swap_ref[width:, columns] = mine_two[rows, :]

    held_ref[...] = two_b[...]


def choose(mine, mine_two, own, two_a, two_b):
    args = [mine, mine_two, own, two_a, two_b]
    width, points = own.shape
    outs = [((width + width // 4, points), own.dtype), (two_b.shape, own.dtype)]
    return call(choose_kernel, "choose", outs, args)


def gather_kernel(rot_ref, own, two_a, two_b, three_a, out_ref, stack):
    width, points = own.shape
    depth = stack.shape[0]
    turn = jnp.concatenate([rot_ref[:, :width], rot_ref[:, 2 * width : width + depth]], axis=1)
    tile = tile_of(points, 1024)
    for i in range(points // tile):
        here = slice(i * tile, (i + 1) * tile)
        at = 0
        for ref in (own, two_a, two_b, three_a):
            stack[at : at + ref.shape[0], here] = ref[:, here]
            at += ref.shape[0]
        out_ref[:, here] = jnp.dot(turn, stack[:, here], preferred_element_type=F32)


def gather(rotation, *blocks):
    width, points = blocks[0].shape
    depth = sum(block.shape[0] for block in blocks)
    scratch = [pltpu.VMEM((depth, points), BF16)]
    return call(
        gather_kernel, "gather", [((width, points), F32)], [rotation, *blocks], scratch, cost=GATHER
    )[0]


def apply_kernel(rot_ref, mine, swap_ref, two, three, proj_ref, after_ref, out_ref):
    width, flat = mine.shape
    points = proj_ref.shape[1]
    one = [swap_ref[width:, columns] for columns, _ in packed(mine.shape, swap_ref.shape[0] - width)]
    blocks = (mine[...], jnp.concatenate(one, axis=0), two[...], three[...])
    mixed = sum(
        jnp.dot(rot_ref[:, s * width : (s + 1) * width], block, preferred_element_type=F32)
        for s, block in enumerate(blocks)
    )
    mixed = mixed.astype(BF16)
    tile = tile_of(points, 1024)
    for at in range(0, points, tile):
        out_ref[:, at : at + tile] = jnp.dot(
            mixed, proj_ref[:, at : at + tile], preferred_element_type=F32
        )


def finish_kernel(
    rot_ref, partial_ref, swap_ref, last_ref, applied, out_hbm, out_ref, sems
):
    width, points = out_ref.shape
    rows = last_ref.shape[0]
    pieces = sems.shape[0]
    tile = points // pieces
    turn = jnp.concatenate(
        [rot_ref[:, width : 2 * width], rot_ref[:, rot_ref.shape[1] - rows :]], axis=1
    )
    copies = []
    for i in range(pieces):
        here = slice(i * tile, (i + 1) * tile)
        last = jnp.concatenate([swap_ref[:width, here], last_ref[:, here]], axis=0)
        rotated = partial_ref[:, here] + jnp.dot(turn, last, preferred_element_type=F32)
        added = rotated.astype(BF16).astype(F32) + applied[:, here]
        out_ref[:, here] = added.astype(out_ref.dtype)
        part = (slice(None), pl.ds(i * tile, tile))
        copies.append(pltpu.make_async_copy(out_ref.at[part], out_hbm.at[part], sems.at[i]))
        copies[-1].start()
    for copy in copies:
        copy.wait()


def finish(*args):
    width, points = args[-1].shape
    pieces = points // tile_of(points, 1024)
    return pl.pallas_call(
        finish_kernel,
        in_specs=[VMEM] * len(args),
        out_specs=pl.BlockSpec(memory_space=pl.ANY),
        out_shape=jax.ShapeDtypeStruct((width, points), BF16),
        scratch_shapes=[pltpu.VMEM((width, points), BF16), pltpu.SemaphoreType.DMA((pieces,))],
        compiler_params=ROOM,
        cost_estimate=flops(0),
        name="finish",
    )(*args)


def on_device(orbitals, rotation, projectors, coupling, slot_atom):
    width, points = orbitals.shape
    slot_count, rank, _ = projectors.shape
    owned = coupling.shape[0]
    proj = projectors.reshape(slot_count * rank, points)

    cut = width // 2
    two_a = along_bands(orbitals[:cut], 2)
    two_b = along_bands(lower(orbitals, width - cut), 2)
    loads = from_all_domains(project(orbitals, proj, coupling.reshape(owned * rank, rank)))
    mine = couple(slot_atom, loads, width, owned)
    mine_two = along_bands(mine, 2)
    three_a = along_bands(hold(two_a, mine), 1)
    swap, held = choose(mine, mine_two, orbitals, two_a, two_b)
    mine_three = along_bands(mine_two, 1)
    swap = swapped(swap)
    three_b = along_bands(held, 1)
    partial = gather(rotation, orbitals, two_a, two_b, three_a)
    applied = call(
        apply_kernel,
        "apply",
        [((width, points), F32)],
        [rotation, mine, swap, mine_two, mine_three, proj, partial],
        cost=APPLY,
    )[0]
    return finish(rotation, partial, swap, three_b, applied)


def solution(mesh):
    in_specs = (P("band", "dom"), P("band", None), P(None, None, "dom"), P("dom", None, None), P())
    out_specs = P("band", "dom")
    return jax.shard_map(
        on_device, mesh=mesh, in_specs=in_specs, out_specs=out_specs, check_vma=False
    )
```

```python
import functools

import jax
import jax.numpy as jnp
from jax import lax
from jax.experimental import pallas as pl
from jax.experimental.pallas import tpu as pltpu
from jax.sharding import PartitionSpec as P

TURN = 3 * 10**9
COUPLE = 2 * 10**9
APPLY = 50 * 10**8
GATHER = 45 * 10**8

F32 = jnp.float32
BF16 = jnp.bfloat16
ROOM = pltpu.CompilerParams(vmem_limit_bytes=8 * 2**20)
NT = (((1,), (1,)), ((), ()))
VMEM = pl.BlockSpec(memory_space=pltpu.VMEM)
SMEM = pl.BlockSpec(memory_space=pltpu.SMEM)


def flops(count):
    return pl.CostEstimate(flops=count, bytes_accessed=0, transcendentals=0)


def call(kernel, name, outs, args, scratch=(), first=VMEM, cost=0):
    shapes = [jax.ShapeDtypeStruct(*o) for o in outs]
    return pl.pallas_call(
        kernel,
        in_specs=[first] + [VMEM] * (len(args) - 1),
        out_specs=[VMEM] * len(outs),
        out_shape=shapes,
        scratch_shapes=list(scratch),
        compiler_params=ROOM,
        cost_estimate=flops(cost),
        name=name,
    )(*args)


def along_bands(block, distance):
    count = lax.axis_size("band")
    return lax.ppermute(block, "band", [(i, (i + distance) % count) for i in range(count)])


def swapped(block):
    count = lax.axis_size("band")
    return lax.ppermute(block, "band", [(i, i ^ 1) for i in range(count)])


def on_even():
    return lax.axis_index("band") % 2 == 0


def by_permutes():
    count = lax.axis_size("dom")
    return count <= 8 and count & (count - 1) == 0


def from_all_domains(block):
    count = lax.axis_size("dom")
    if by_permutes():
        routes = [[(i, i ^ mask) for i in range(count)] for mask in range(1, count)]
        return [block] + [lax.ppermute(block, "dom", route) for route in routes]
    whole = lax.all_gather(block, "dom")
    return [whole[d] for d in range(count)]


def domain_at(place):
    return lax.axis_index("dom") ^ place if by_permutes() else place


def tile_of(extent, most):
    return max(w for w in range(128, most + 1, 128) if extent % w == 0)


def turn_kernel(coupling_ref, out_ref):
    owned, rank = coupling_ref.shape
    whole = coupling_ref[...]
    high = whole.astype(BF16)
    unit = lax.broadcasted_iota(jnp.int32, (rank, rank), 0) == lax.broadcasted_iota(
        jnp.int32, (rank, rank), 1
    )
    unit = jnp.where(unit, 1.0, 0.0).astype(BF16)
    for i, piece in enumerate((high, (whole - high.astype(F32)).astype(BF16))):
        turned = lax.dot_general(unit, piece, NT, preferred_element_type=F32)
        out_ref[:, i * owned : (i + 1) * owned] = turned.astype(BF16)


def project_kernel(orb_ref, proj_ref, turned_ref, out_ref):
    width, points = orb_ref.shape
    out_ref[width:, : turned_ref.shape[1]] = turned_ref[...]
    tile = tile_of(points, 1024)
    total = None
    for at in range(0, points, tile):
        term = lax.dot_general(
            proj_ref[:, at : at + tile], orb_ref[:, at : at + tile], NT, preferred_element_type=F32
        )
        total = term if total is None else total + term
    out_ref[:width, :] = total.T.astype(BF16)


def project(orbitals, proj, coupling):
    width, points = orbitals.shape
    owned, rank = coupling.shape
    turned = call(
        turn_kernel, "turn", [((rank, 2 * owned), BF16)], [coupling], cost=TURN
    )[0]
    outs = [((width + rank, proj.shape[0]), BF16)]
    return call(project_kernel, "project", outs, [orbitals, proj, turned])[0]


def couple_kernel(count, slots, owned, slot_ref, *refs):
    loads = refs[:count]
    out_ref, pick, high_ref, low_ref = refs[count:]
    width, flat = out_ref.shape
    rank = flat // slots
    me = lax.axis_index("dom")
    lanes = lax.broadcasted_iota(jnp.int32, (rank, flat), 1)
    unit = lanes % rank == lax.broadcasted_iota(jnp.int32, (rank, flat), 0)
    lane_slot = lanes // rank

    atoms = jnp.zeros((rank, flat), jnp.int32)
    for k in range(slots):
        atoms = jnp.where(lane_slot == k, slot_ref[me, k], atoms)

    columns = None
    for place in range(count):
        owner = domain_at(place)
        for a in range(owned):
            hit = unit & (atoms == owner * owned + a)
            pick[a * rank : (a + 1) * rank, :] = jnp.where(hit, 1.0, 0.0).astype(BF16)
        parts = [loads[place][width:, i * owned * rank : (i + 1) * owned * rank] for i in (0, 1)]
        term = jnp.dot(jnp.concatenate(parts, 0), pick[...], preferred_element_type=F32)
        columns = term if columns is None else columns + term
    high, low = columns[:rank], columns[rank:]

    total = None
    for place in range(count):
        domain = domain_at(place)
        for k in range(slots):
            hit = atoms == slot_ref[domain, k]
            rows = slice(k * rank, (k + 1) * rank)
            high_ref[rows, :] = jnp.where(hit, high, 0.0).astype(BF16)
            low_ref[rows, :] = jnp.where(hit, low, 0.0).astype(BF16)
        block = loads[place][:width, :]
        term = jnp.dot(block, high_ref[...], preferred_element_type=F32)
        term += jnp.dot(block, low_ref[...], preferred_element_type=F32)
        total = term if total is None else total + term
    out_ref[...] = total.astype(BF16)


def couple(slot_atom, loads, width, owned):
    flat = loads[0].shape[1]
    slots = slot_atom.shape[1]
    return call(
        functools.partial(couple_kernel, len(loads), slots, owned),
        "couple",
        [((width, flat), BF16)],
        [slot_atom, *loads],
        [
            pltpu.VMEM((owned * (flat // slots), flat), BF16),
            pltpu.VMEM((flat, flat), BF16),
            pltpu.VMEM((flat, flat), BF16),
        ],
        first=SMEM,
        cost=COUPLE,
    )[0]


def hold_kernel(block_ref, after_ref, out_ref):
    out_ref[...] = block_ref[...]


def hold(block, after):
    return call(hold_kernel, "hold", [(block.shape, block.dtype)], [block, after])[0]


def packed(coef_shape, rows):
    width, flat = coef_shape
    return [
        (slice(i * flat, (i + 1) * flat), slice(i * rows, (i + 1) * rows))
        for i in range(width // rows)
    ]


def choose_kernel(mine, mine_two, own, two_a, two_b, swap_ref, held_ref):
    width, cut = own.shape[0], two_a.shape[0]
    parts = packed(mine.shape, swap_ref.shape[0] - width)

    @pl.when(on_even())
    def _():
        swap_ref[:width, :] = own[...]
        for columns, rows in parts:
            swap_ref[width:, columns] = mine[rows, :]

    @pl.when(jnp.logical_not(on_even()))
    def _():
        swap_ref[:cut, :] = two_a[...]
        swap_ref[cut:width, :] = two_b[...]
        for columns, rows in parts:
            swap_ref[width:, columns] = mine_two[rows, :]

    held_ref[...] = two_b[...]


def choose(mine, mine_two, own, two_a, two_b):
    args = [mine, mine_two, own, two_a, two_b]
    width, points = own.shape
    outs = [((width + width // 4, points), own.dtype), (two_b.shape, own.dtype)]
    return call(choose_kernel, "choose", outs, args)


def gather_kernel(rot_ref, own, two_a, two_b, three_a, out_ref, stack):
    width, points = own.shape
    depth = stack.shape[0]
    turn = jnp.concatenate([rot_ref[:, :width], rot_ref[:, 2 * width : width + depth]], axis=1)
    tile = tile_of(points, 1024)
    for i in range(points // tile):
        here = slice(i * tile, (i + 1) * tile)
        at = 0
        for ref in (own, two_a, two_b, three_a):
            stack[at : at + ref.shape[0], here] = ref[:, here]
            at += ref.shape[0]
        out_ref[:, here] = jnp.dot(turn, stack[:, here], preferred_element_type=F32)


def gather(rotation, *blocks):
    width, points = blocks[0].shape
    depth = sum(block.shape[0] for block in blocks)
    scratch = [pltpu.VMEM((depth, points), BF16)]
    return call(
        gather_kernel, "gather", [((width, points), F32)], [rotation, *blocks], scratch, cost=GATHER
    )[0]


def apply_kernel(rot_ref, mine, swap_ref, two, three, proj_ref, after_ref, out_ref):
    width, flat = mine.shape
    points = proj_ref.shape[1]
    one = [swap_ref[width:, columns] for columns, _ in packed(mine.shape, swap_ref.shape[0] - width)]
    blocks = (mine[...], jnp.concatenate(one, axis=0), two[...], three[...])
    mixed = sum(
        jnp.dot(rot_ref[:, s * width : (s + 1) * width], block, preferred_element_type=F32)
        for s, block in enumerate(blocks)
    )
    mixed = mixed.astype(BF16)
    tile = tile_of(points, 1024)
    for at in range(0, points, tile):
        out_ref[:, at : at + tile] = jnp.dot(
            mixed, proj_ref[:, at : at + tile], preferred_element_type=F32
        )


def finish_kernel(
    rot_ref, partial_ref, swap_ref, last_ref, applied, out_hbm, out_ref, sems
):
    width, points = out_ref.shape
    rows = last_ref.shape[0]
    pieces = sems.shape[0]
    tile = points // pieces
    turn = jnp.concatenate(
        [rot_ref[:, width : 2 * width], rot_ref[:, rot_ref.shape[1] - rows :]], axis=1
    )
    copies = []
    for i in range(pieces):
        here = slice(i * tile, (i + 1) * tile)
        last = jnp.concatenate([swap_ref[:width, here], last_ref[:, here]], axis=0)
        rotated = partial_ref[:, here] + jnp.dot(turn, last, preferred_element_type=F32)
        added = rotated.astype(BF16).astype(F32) + applied[:, here]
        out_ref[:, here] = added.astype(out_ref.dtype)
        part = (slice(None), pl.ds(i * tile, tile))
        copies.append(pltpu.make_async_copy(out_ref.at[part], out_hbm.at[part], sems.at[i]))
        copies[-1].start()
    for copy in copies:
        copy.wait()


def finish(*args):
    width, points = args[-1].shape
    pieces = points // tile_of(points, 1024)
    return pl.pallas_call(
        finish_kernel,
        in_specs=[VMEM] * len(args),
        out_specs=pl.BlockSpec(memory_space=pl.ANY),
        out_shape=jax.ShapeDtypeStruct((width, points), BF16),
        scratch_shapes=[pltpu.VMEM((width, points), BF16), pltpu.SemaphoreType.DMA((pieces,))],
        compiler_params=ROOM,
        cost_estimate=flops(0),
        name="finish",
    )(*args)


def on_device(orbitals, rotation, projectors, coupling, slot_atom):
    width, points = orbitals.shape
    slot_count, rank, _ = projectors.shape
    owned = coupling.shape[0]
    proj = projectors.reshape(slot_count * rank, points)

    cut = width * 3 // 4
    two_a = along_bands(orbitals[:cut], 2)
    two_b = along_bands(orbitals[cut:], 2)
    loads = from_all_domains(project(orbitals, proj, coupling.reshape(owned * rank, rank)))
    mine = couple(slot_atom, loads, width, owned)
    mine_two = along_bands(mine, 2)
    three_a = along_bands(hold(two_a, mine), 1)
    swap, held = choose(mine, mine_two, orbitals, two_a, two_b)
    mine_three = along_bands(mine_two, 1)
    swap = swapped(swap)
    three_b = along_bands(held, 1)
    partial = gather(rotation, orbitals, two_a, two_b, three_a)
    applied = call(
        apply_kernel,
        "apply",
        [((width, points), F32)],
        [rotation, mine, swap, mine_two, mine_three, proj, partial],
        cost=APPLY,
    )[0]
    return finish(rotation, partial, swap, three_b, applied)


def solution(mesh):
    in_specs = (P("band", "dom"), P("band", None), P(None, None, "dom"), P("dom", None, None), P())
    out_specs = P("band", "dom")
    return jax.shard_map(
        on_device, mesh=mesh, in_specs=in_specs, out_specs=out_specs, check_vma=False
    )
```

```python
import functools

import jax
import jax.numpy as jnp
from jax import lax
from jax.experimental import pallas as pl
from jax.experimental.pallas import tpu as pltpu
from jax.sharding import PartitionSpec as P

TURN = 0 * 10**9
CUT = 30 * 10**8
COUPLE = 2 * 10**9
APPLY = 50 * 10**8
GATHER = 45 * 10**8

F32 = jnp.float32
BF16 = jnp.bfloat16
ROOM = pltpu.CompilerParams(vmem_limit_bytes=8 * 2**20)
NT = (((1,), (1,)), ((), ()))
VMEM = pl.BlockSpec(memory_space=pltpu.VMEM)
SMEM = pl.BlockSpec(memory_space=pltpu.SMEM)


def flops(count):
    return pl.CostEstimate(flops=count, bytes_accessed=0, transcendentals=0)


def call(kernel, name, outs, args, scratch=(), first=VMEM, cost=0):
    shapes = [jax.ShapeDtypeStruct(*o) for o in outs]
    return pl.pallas_call(
        kernel,
        in_specs=[first] + [VMEM] * (len(args) - 1),
        out_specs=[VMEM] * len(outs),
        out_shape=shapes,
        scratch_shapes=list(scratch),
        compiler_params=ROOM,
        cost_estimate=flops(cost),
        name=name,
    )(*args)


def along_bands(block, distance):
    count = lax.axis_size("band")
    return lax.ppermute(block, "band", [(i, (i + distance) % count) for i in range(count)])


def swapped(block):
    count = lax.axis_size("band")
    return lax.ppermute(block, "band", [(i, i ^ 1) for i in range(count)])


def on_even():
    return lax.axis_index("band") % 2 == 0


def by_permutes():
    count = lax.axis_size("dom")
    return count <= 8 and count & (count - 1) == 0


def from_all_domains(block):
    count = lax.axis_size("dom")
    if by_permutes():
        routes = [[(i, i ^ mask) for i in range(count)] for mask in range(1, count)]
        return [block] + [lax.ppermute(block, "dom", route) for route in routes]
    whole = lax.all_gather(block, "dom")
    return [whole[d] for d in range(count)]


def domain_at(place):
    return lax.axis_index("dom") ^ place if by_permutes() else place


def tile_of(extent, most):
    return max(w for w in range(128, most + 1, 128) if extent % w == 0)


def turn_kernel(coupling_ref, out_ref):
    owned, rank = coupling_ref.shape
    whole = coupling_ref[...]
    high = whole.astype(BF16)
    unit = lax.broadcasted_iota(jnp.int32, (rank, rank), 0) == lax.broadcasted_iota(
        jnp.int32, (rank, rank), 1
    )
    unit = jnp.where(unit, 1.0, 0.0).astype(BF16)
    for i, piece in enumerate((high, (whole - high.astype(F32)).astype(BF16))):
        turned = lax.dot_general(unit, piece, NT, preferred_element_type=F32)
        out_ref[:, i * owned : (i + 1) * owned] = turned.astype(BF16)


def project_kernel(orb_ref, proj_ref, turned_ref, out_ref):
    width, points = orb_ref.shape
    out_ref[width:, : turned_ref.shape[1]] = turned_ref[...]
    tile = tile_of(points, 1024)
    total = None
    for at in range(0, points, tile):
        term = lax.dot_general(
            proj_ref[:, at : at + tile], orb_ref[:, at : at + tile], NT, preferred_element_type=F32
        )
        total = term if total is None else total + term
    out_ref[:width, :] = total.T.astype(BF16)


def project(orbitals, proj, coupling):
    width, points = orbitals.shape
    owned, rank = coupling.shape
    turned = call(
        turn_kernel, "turn", [((rank, 2 * owned), BF16)], [coupling], cost=TURN
    )[0]
    outs = [((width + rank, proj.shape[0]), BF16)]
    return call(project_kernel, "project", outs, [orbitals, proj, turned])[0]


def couple_kernel(count, slots, owned, slot_ref, *refs):
    loads = refs[:count]
    out_ref, pick, high_ref, low_ref = refs[count:]
    width, flat = out_ref.shape
    rank = flat // slots
    me = lax.axis_index("dom")
    lanes = lax.broadcasted_iota(jnp.int32, (rank, flat), 1)
    unit = lanes % rank == lax.broadcasted_iota(jnp.int32, (rank, flat), 0)
    lane_slot = lanes // rank

    atoms = jnp.zeros((rank, flat), jnp.int32)
    for k in range(slots):
        atoms = jnp.where(lane_slot == k, slot_ref[me, k], atoms)

    columns = None
    for place in range(count):
        owner = domain_at(place)
        for a in range(owned):
            hit = unit & (atoms == owner * owned + a)
            pick[a * rank : (a + 1) * rank, :] = jnp.where(hit, 1.0, 0.0).astype(BF16)
        parts = [loads[place][width:, i * owned * rank : (i + 1) * owned * rank] for i in (0, 1)]
        term = jnp.dot(jnp.concatenate(parts, 0), pick[...], preferred_element_type=F32)
        columns = term if columns is None else columns + term
    high, low = columns[:rank], columns[rank:]

    total = None
    for place in range(count):
        domain = domain_at(place)
        for k in range(slots):
            hit = atoms == slot_ref[domain, k]
            rows = slice(k * rank, (k + 1) * rank)
            high_ref[rows, :] = jnp.where(hit, high, 0.0).astype(BF16)
            low_ref[rows, :] = jnp.where(hit, low, 0.0).astype(BF16)
        block = loads[place][:width, :]
        term = jnp.dot(block, high_ref[...], preferred_element_type=F32)
        term += jnp.dot(block, low_ref[...], preferred_element_type=F32)
        total = term if total is None else total + term
    out_ref[...] = total.astype(BF16)


def couple(slot_atom, loads, width, owned):
    flat = loads[0].shape[1]
    slots = slot_atom.shape[1]
    return call(
        functools.partial(couple_kernel, len(loads), slots, owned),
        "couple",
        [((width, flat), BF16)],
        [slot_atom, *loads],
        [
            pltpu.VMEM((owned * (flat // slots), flat), BF16),
            pltpu.VMEM((flat, flat), BF16),
            pltpu.VMEM((flat, flat), BF16),
        ],
        first=SMEM,
        cost=COUPLE,
    )[0]


def halves_kernel(block_ref, *refs):
    upper_ref, lower_ref = refs[-2:]
    half = upper_ref.shape[0]
    upper_ref[...] = block_ref[:half, :]
    lower_ref[...] = block_ref[half:, :]


def halves(block, after, cost=0):
    half = ((block.shape[0] // 2, block.shape[1]), block.dtype)
    return call(halves_kernel, "halves", [half, half], [block, *after], cost=cost)


def hold_kernel(upper_ref, lower_ref, after_ref, out_ref):
    rows = upper_ref.shape[0]
    out_ref[:rows, :] = upper_ref[...]
    out_ref[rows:, :] = lower_ref[: out_ref.shape[0] - rows, :]


def hold(upper, lower, rows, after):
    shape = (rows, upper.shape[1])
    return call(hold_kernel, "hold", [(shape, upper.dtype)], [upper, lower, after])[0]


def packed(coef_shape, rows):
    width, flat = coef_shape
    return [
        (slice(i * flat, (i + 1) * flat), slice(i * rows, (i + 1) * rows))
        for i in range(width // rows)
    ]


def choose_kernel(mine, mine_two, two, lower, swap_ref, held_ref):
    width = two.shape[0]
    parts = packed(mine.shape, swap_ref.shape[0] - width)
    swap_ref[:width, :] = two[...]

    @pl.when(on_even())
    def _():
        for columns, rows in parts:
            swap_ref[width:, columns] = mine[rows, :]

    @pl.when(jnp.logical_not(on_even()))
    def _():
        for columns, rows in parts:
            swap_ref[width:, columns] = mine_two[rows, :]

    held_ref[...] = lower[lower.shape[0] - held_ref.shape[0] :, :]


def choose(mine, mine_two, two, lower):
    width, points = two.shape
    part = width // 4
    outs = [((width + part, points), two.dtype), ((part, points), two.dtype)]
    return call(choose_kernel, "choose", outs, [mine, mine_two, two, lower])


def where_even(tile, even):
    here = on_even() if even else jnp.logical_not(on_even())
    return jnp.where(here, tile.astype(F32), 0.0).astype(BF16)


def gather_kernel(rot_ref, own, one, two, upper, lower, three_a, out_ref, stack):
    width, points = own.shape
    depth = stack.shape[0]
    turn = jnp.concatenate(
        [rot_ref[:, : 3 * width], where_even(rot_ref[:, 3 * width : depth], True)], axis=1
    )
    stack[:width, :] = own[...]
    stack[width : 2 * width, :] = one[...]
    stack[3 * width :, :] = three_a[...]

    @pl.when(on_even())
    def _():
        stack[2 * width : 3 * width, :] = two[...]

    @pl.when(jnp.logical_not(on_even()))
    def _():
        stack[2 * width : 2 * width + upper.shape[0], :] = upper[...]
        stack[2 * width + upper.shape[0] : 3 * width, :] = lower[...]

    tile = tile_of(points, 1024)
    for at in range(0, points, tile):
        here = slice(at, at + tile)
        out_ref[:, here] = jnp.dot(turn, stack[:, here], preferred_element_type=F32)


def gather(rotation, *blocks):
    (width, points), rows = blocks[0].shape, blocks[-1].shape[0]
    scratch = [pltpu.VMEM((3 * width + rows, points), BF16)]
    return call(
        gather_kernel, "gather", [((width, points), F32)], [rotation, *blocks], scratch, cost=GATHER
    )[0]


def apply_kernel(rot_ref, mine, swap_ref, two, three, proj_ref, after_ref, out_ref):
    width, flat = mine.shape
    points = proj_ref.shape[1]
    one = [swap_ref[width:, columns] for columns, _ in packed(mine.shape, swap_ref.shape[0] - width)]
    blocks = (mine[...], jnp.concatenate(one, axis=0), two[...], three[...])
    mixed = sum(
        jnp.dot(rot_ref[:, s * width : (s + 1) * width], block, preferred_element_type=F32)
        for s, block in enumerate(blocks)
    )
    mixed = mixed.astype(BF16)
    tile = tile_of(points, 1024)
    for at in range(0, points, tile):
        out_ref[:, at : at + tile] = jnp.dot(
            mixed, proj_ref[:, at : at + tile], preferred_element_type=F32
        )


def finish_kernel(
    rot_ref, partial_ref, swap_ref, last_ref, applied, out_hbm, out_ref, sems
):
    width, points = out_ref.shape
    rows = last_ref.shape[0]
    pieces = sems.shape[0]
    tile = points // pieces
    turn = jnp.concatenate(
        [
            where_even(rot_ref[:, 3 * width : 4 * width], False),
            where_even(rot_ref[:, 4 * width - rows : 4 * width], True),
        ],
        axis=1,
    )
    copies = []
    for i in range(pieces):
        here = slice(i * tile, (i + 1) * tile)
        last = jnp.concatenate([swap_ref[:width, here], last_ref[:, here]], axis=0)
        rotated = partial_ref[:, here] + jnp.dot(turn, last, preferred_element_type=F32)
        added = rotated.astype(BF16).astype(F32) + applied[:, here]
        out_ref[:, here] = added.astype(out_ref.dtype)
        part = (slice(None), pl.ds(i * tile, tile))
        copies.append(pltpu.make_async_copy(out_ref.at[part], out_hbm.at[part], sems.at[i]))
        copies[-1].start()
    for copy in copies:
        copy.wait()


def finish(*args):
    width, points = args[-1].shape
    pieces = points // tile_of(points, 1024)
    return pl.pallas_call(
        finish_kernel,
        in_specs=[VMEM] * len(args),
        out_specs=pl.BlockSpec(memory_space=pl.ANY),
        out_shape=jax.ShapeDtypeStruct((width, points), BF16),
        scratch_shapes=[pltpu.VMEM((width, points), BF16), pltpu.SemaphoreType.DMA((pieces,))],
        compiler_params=ROOM,
        cost_estimate=flops(0),
        name="finish",
    )(*args)


def on_device(orbitals, rotation, projectors, coupling, slot_atom):
    width, points = orbitals.shape
    slot_count, rank, _ = projectors.shape
    owned = coupling.shape[0]
    proj = projectors.reshape(slot_count * rank, points)

    one = along_bands(orbitals, 1)
    upper, lower = [swapped(block) for block in halves(orbitals, [], CUT)]
    two = along_bands(hold(upper, lower, width, upper), 1)
    loads = from_all_domains(project(orbitals, proj, coupling.reshape(owned * rank, rank)))
    upper, lower = [swapped(block) for block in halves(one, loads[1:])]
    mine = couple(slot_atom, loads, width, owned)
    mine_two = along_bands(mine, 2)
    three_a = along_bands(hold(upper, lower, width * 3 // 4, mine), 1)
    swap, held = choose(mine, mine_two, two, lower)
    mine_three = along_bands(mine_two, 1)
    three_b = along_bands(held, 1)
    swap = swapped(swap)
    partial = gather(rotation, orbitals, one, two, upper, lower, three_a)
    applied = call(
        apply_kernel,
        "apply",
        [((width, points), F32)],
        [rotation, mine, swap, mine_two, mine_three, proj, partial],
        cost=APPLY,
    )[0]
    return finish(rotation, partial, swap, three_b, applied)


def solution(mesh):
    in_specs = (P("band", "dom"), P("band", None), P(None, None, "dom"), P("dom", None, None), P())
    out_specs = P("band", "dom")
    return jax.shard_map(
        on_device, mesh=mesh, in_specs=in_specs, out_specs=out_specs, check_vma=False
    )
```

```python
import functools

import jax
import jax.numpy as jnp
from jax import lax
from jax.experimental import pallas as pl
from jax.experimental.pallas import tpu as pltpu
from jax.sharding import PartitionSpec as P

TURN = 0 * 10**9
CUT = 30 * 10**8
COUPLE = 4 * 10**9
APPLY = 50 * 10**8
GATHER = 45 * 10**8

F32 = jnp.float32
BF16 = jnp.bfloat16
ROOM = pltpu.CompilerParams(vmem_limit_bytes=8 * 2**20)
NT = (((1,), (1,)), ((), ()))
VMEM = pl.BlockSpec(memory_space=pltpu.VMEM)
SMEM = pl.BlockSpec(memory_space=pltpu.SMEM)


def flops(count):
    return pl.CostEstimate(flops=count, bytes_accessed=0, transcendentals=0)


def call(kernel, name, outs, args, scratch=(), first=VMEM, cost=0):
    shapes = [jax.ShapeDtypeStruct(*o) for o in outs]
    return pl.pallas_call(
        kernel,
        in_specs=[first] + [VMEM] * (len(args) - 1),
        out_specs=[VMEM] * len(outs),
        out_shape=shapes,
        scratch_shapes=list(scratch),
        compiler_params=ROOM,
        cost_estimate=flops(cost),
        name=name,
    )(*args)


def along_bands(block, distance):
    count = lax.axis_size("band")
    return lax.ppermute(block, "band", [(i, (i + distance) % count) for i in range(count)])


def swapped(block):
    count = lax.axis_size("band")
    return lax.ppermute(block, "band", [(i, i ^ 1) for i in range(count)])


def on_even():
    return lax.axis_index("band") % 2 == 0


def by_permutes():
    count = lax.axis_size("dom")
    return count <= 8 and count & (count - 1) == 0


def from_all_domains(block):
    count = lax.axis_size("dom")
    if by_permutes():
        routes = [[(i, i ^ mask) for i in range(count)] for mask in range(1, count)]
        return [block] + [lax.ppermute(block, "dom", route) for route in routes]
    whole = lax.all_gather(block, "dom")
    return [whole[d] for d in range(count)]


def domain_at(place):
    return lax.axis_index("dom") ^ place if by_permutes() else place


def tile_of(extent, most):
    return max(w for w in range(128, most + 1, 128) if extent % w == 0)


def turn_kernel(coupling_ref, out_ref):
    owned, rank = coupling_ref.shape
    whole = coupling_ref[...]
    high = whole.astype(BF16)
    unit = lax.broadcasted_iota(jnp.int32, (rank, rank), 0) == lax.broadcasted_iota(
        jnp.int32, (rank, rank), 1
    )
    unit = jnp.where(unit, 1.0, 0.0).astype(BF16)
    for i, piece in enumerate((high, (whole - high.astype(F32)).astype(BF16))):
        turned = lax.dot_general(unit, piece, NT, preferred_element_type=F32)
        out_ref[:, i * owned : (i + 1) * owned] = turned.astype(BF16)


def project_kernel(orb_ref, proj_ref, turned_ref, out_ref):
    width, points = orb_ref.shape
    out_ref[width:, : turned_ref.shape[1]] = turned_ref[...]
    tile = tile_of(points, 1024)
    total = None
    for at in range(0, points, tile):
        term = lax.dot_general(
            proj_ref[:, at : at + tile], orb_ref[:, at : at + tile], NT, preferred_element_type=F32
        )
        total = term if total is None else total + term
    out_ref[:width, :] = total.T.astype(BF16)


def project(orbitals, proj, coupling):
    width, points = orbitals.shape
    owned, rank = coupling.shape
    turned = call(
        turn_kernel, "turn", [((rank, 2 * owned), BF16)], [coupling], cost=TURN
    )[0]
    outs = [((width + rank, proj.shape[0]), BF16)]
    return call(project_kernel, "project", outs, [orbitals, proj, turned])[0]


def couple_kernel(count, slots, owned, slot_ref, *refs):
    loads = refs[:count]
    out_ref, pick, high_ref, low_ref = refs[count:]
    width, flat = out_ref.shape
    rank = flat // slots
    me = lax.axis_index("dom")
    lanes = lax.broadcasted_iota(jnp.int32, (rank, flat), 1)
    unit = lanes % rank == lax.broadcasted_iota(jnp.int32, (rank, flat), 0)
    lane_slot = lanes // rank

    atoms = jnp.zeros((rank, flat), jnp.int32)
    for k in range(slots):
        atoms = jnp.where(lane_slot == k, slot_ref[me, k], atoms)

    columns = None
    for place in range(count):
        owner = domain_at(place)
        for a in range(owned):
            hit = unit & (atoms == owner * owned + a)
            pick[a * rank : (a + 1) * rank, :] = jnp.where(hit, 1.0, 0.0).astype(BF16)
        parts = [loads[place][width:, i * owned * rank : (i + 1) * owned * rank] for i in (0, 1)]
        term = jnp.dot(jnp.concatenate(parts, 0), pick[...], preferred_element_type=F32)
        columns = term if columns is None else columns + term
    high, low = columns[:rank], columns[rank:]

    total = None
    for place in range(count):
        domain = domain_at(place)
        for k in range(slots):
            hit = atoms == slot_ref[domain, k]
            rows = slice(k * rank, (k + 1) * rank)
            high_ref[rows, :] = jnp.where(hit, high, 0.0).astype(BF16)
            low_ref[rows, :] = jnp.where(hit, low, 0.0).astype(BF16)
        block = loads[place][:width, :]
        term = jnp.dot(block, high_ref[...], preferred_element_type=F32)
        term += jnp.dot(block, low_ref[...], preferred_element_type=F32)
        total = term if total is None else total + term
    out_ref[...] = total.astype(BF16)


def couple(slot_atom, loads, width, owned):
    flat = loads[0].shape[1]
    slots = slot_atom.shape[1]
    return call(
        functools.partial(couple_kernel, len(loads), slots, owned),
        "couple",
        [((width, flat), BF16)],
        [slot_atom, *loads],
        [
            pltpu.VMEM((owned * (flat // slots), flat), BF16),
            pltpu.VMEM((flat, flat), BF16),
            pltpu.VMEM((flat, flat), BF16),
        ],
        first=SMEM,
        cost=COUPLE,
    )[0]


def halves_kernel(block_ref, *refs):
    upper_ref, lower_ref = refs[-2:]
    half = upper_ref.shape[0]
    upper_ref[...] = block_ref[:half, :]
    lower_ref[...] = block_ref[half:, :]


def halves(block, after, cost=0):
    half = ((block.shape[0] // 2, block.shape[1]), block.dtype)
    return call(halves_kernel, "halves", [half, half], [block, *after], cost=cost)


def hold_kernel(upper_ref, lower_ref, after_ref, out_ref):
    rows = upper_ref.shape[0]
    out_ref[:rows, :] = upper_ref[...]
    out_ref[rows:, :] = lower_ref[: out_ref.shape[0] - rows, :]


def hold(upper, lower, rows, after):
    shape = (rows, upper.shape[1])
    return call(hold_kernel, "hold", [(shape, upper.dtype)], [upper, lower, after])[0]


def packed(coef_shape, rows):
    width, flat = coef_shape
    return [
        (slice(i * flat, (i + 1) * flat), slice(i * rows, (i + 1) * rows))
        for i in range(width // rows)
    ]


def choose_kernel(mine, mine_two, two, lower, swap_ref, held_ref):
    width = two.shape[0]
    parts = packed(mine.shape, swap_ref.shape[0] - width)
    swap_ref[:width, :] = two[...]

    @pl.when(on_even())
    def _():
        for columns, rows in parts:
            swap_ref[width:, columns] = mine[rows, :]

    @pl.when(jnp.logical_not(on_even()))
    def _():
        for columns, rows in parts:
            swap_ref[width:, columns] = mine_two[rows, :]

    held_ref[...] = lower[lower.shape[0] - held_ref.shape[0] :, :]


def choose(mine, mine_two, two, lower):
    width, points = two.shape
    part = width // 4
    outs = [((width + part, points), two.dtype), ((part, points), two.dtype)]
    return call(choose_kernel, "choose", outs, [mine, mine_two, two, lower])


def where_even(tile, even):
    here = on_even() if even else jnp.logical_not(on_even())
    return jnp.where(here, tile.astype(F32), 0.0).astype(BF16)


def gather_kernel(rot_ref, own, one, two, upper, lower, three_a, out_ref, stack):
    width, points = own.shape
    depth = stack.shape[0]
    turn = jnp.concatenate(
        [rot_ref[:, : 3 * width], where_even(rot_ref[:, 3 * width : depth], True)], axis=1
    )
    stack[:width, :] = own[...]
    stack[width : 2 * width, :] = one[...]
    stack[3 * width :, :] = three_a[...]

    @pl.when(on_even())
    def _():
        stack[2 * width : 3 * width, :] = two[...]

    @pl.when(jnp.logical_not(on_even()))
    def _():
        stack[2 * width : 2 * width + upper.shape[0], :] = upper[...]
        stack[2 * width + upper.shape[0] : 3 * width, :] = lower[...]

    tile = tile_of(points, 1024)
    for at in range(0, points, tile):
        here = slice(at, at + tile)
        out_ref[:, here] = jnp.dot(turn, stack[:, here], preferred_element_type=F32)


def gather(rotation, *blocks):
    (width, points), rows = blocks[0].shape, blocks[-1].shape[0]
    scratch = [pltpu.VMEM((3 * width + rows, points), BF16)]
    return call(
        gather_kernel, "gather", [((width, points), F32)], [rotation, *blocks], scratch, cost=GATHER
    )[0]


def apply_kernel(rot_ref, mine, swap_ref, two, three, proj_ref, after_ref, out_ref):
    width, flat = mine.shape
    points = proj_ref.shape[1]
    one = [swap_ref[width:, columns] for columns, _ in packed(mine.shape, swap_ref.shape[0] - width)]
    blocks = (mine[...], jnp.concatenate(one, axis=0), two[...], three[...])
    mixed = sum(
        jnp.dot(rot_ref[:, s * width : (s + 1) * width], block, preferred_element_type=F32)
        for s, block in enumerate(blocks)
    )
    mixed = mixed.astype(BF16)
    tile = tile_of(points, 1024)
    for at in range(0, points, tile):
        out_ref[:, at : at + tile] = jnp.dot(
            mixed, proj_ref[:, at : at + tile], preferred_element_type=F32
        )


def finish_kernel(
    rot_ref, partial_ref, swap_ref, last_ref, applied, out_hbm, out_ref, sems
):
    width, points = out_ref.shape
    rows = last_ref.shape[0]
    pieces = sems.shape[0]
    tile = points // pieces
    turn = jnp.concatenate(
        [
            where_even(rot_ref[:, 3 * width : 4 * width], False),
            where_even(rot_ref[:, 4 * width - rows : 4 * width], True),
        ],
        axis=1,
    )
    copies = []
    for i in range(pieces):
        here = slice(i * tile, (i + 1) * tile)
        last = jnp.concatenate([swap_ref[:width, here], last_ref[:, here]], axis=0)
        rotated = partial_ref[:, here] + jnp.dot(turn, last, preferred_element_type=F32)
        added = rotated.astype(BF16).astype(F32) + applied[:, here]
        out_ref[:, here] = added.astype(out_ref.dtype)
        part = (slice(None), pl.ds(i * tile, tile))
        copies.append(pltpu.make_async_copy(out_ref.at[part], out_hbm.at[part], sems.at[i]))
        copies[-1].start()
    for copy in copies:
        copy.wait()


def finish(*args):
    width, points = args[-1].shape
    pieces = points // tile_of(points, 1024)
    return pl.pallas_call(
        finish_kernel,
        in_specs=[VMEM] * len(args),
        out_specs=pl.BlockSpec(memory_space=pl.ANY),
        out_shape=jax.ShapeDtypeStruct((width, points), BF16),
        scratch_shapes=[pltpu.VMEM((width, points), BF16), pltpu.SemaphoreType.DMA((pieces,))],
        compiler_params=ROOM,
        cost_estimate=flops(0),
        name="finish",
    )(*args)


def on_device(orbitals, rotation, projectors, coupling, slot_atom):
    width, points = orbitals.shape
    slot_count, rank, _ = projectors.shape
    owned = coupling.shape[0]
    proj = projectors.reshape(slot_count * rank, points)

    one = along_bands(orbitals, 1)
    upper, lower = [swapped(block) for block in halves(orbitals, [], CUT)]
    two = along_bands(hold(upper, lower, width, upper), 1)
    loads = from_all_domains(project(orbitals, proj, coupling.reshape(owned * rank, rank)))
    upper, lower = [swapped(block) for block in halves(one, loads[-1:])]
    mine = couple(slot_atom, loads, width, owned)
    mine_two = along_bands(mine, 2)
    three_a = along_bands(hold(upper, lower, width * 3 // 4, mine), 1)
    swap, held = choose(mine, mine_two, two, lower)
    mine_three = along_bands(mine_two, 1)
    three_b = along_bands(held, 1)
    swap = swapped(swap)
    partial = gather(rotation, orbitals, one, two, upper, lower, three_a)
    applied = call(
        apply_kernel,
        "apply",
        [((width, points), F32)],
        [rotation, mine, swap, mine_two, mine_three, proj, partial],
        cost=APPLY,
    )[0]
    return finish(rotation, partial, swap, three_b, applied)


def solution(mesh):
    in_specs = (P("band", "dom"), P("band", None), P(None, None, "dom"), P("dom", None, None), P())
    out_specs = P("band", "dom")
    return jax.shard_map(
        on_device, mesh=mesh, in_specs=in_specs, out_specs=out_specs, check_vma=False
    )
```

```python
import functools

import jax
import jax.numpy as jnp
from jax import lax
from jax.experimental import pallas as pl
from jax.experimental.pallas import tpu as pltpu
from jax.sharding import PartitionSpec as P

TURN = 0 * 10**9
CUT = 30 * 10**8
COUPLE = 4 * 10**9
APPLY = 50 * 10**8
GATHER = 45 * 10**8

F32 = jnp.float32
BF16 = jnp.bfloat16
ROOM = pltpu.CompilerParams(vmem_limit_bytes=8 * 2**20)
NT = (((1,), (1,)), ((), ()))
VMEM = pl.BlockSpec(memory_space=pltpu.VMEM)
SMEM = pl.BlockSpec(memory_space=pltpu.SMEM)


def flops(count):
    return pl.CostEstimate(flops=count, bytes_accessed=0, transcendentals=0)


def call(kernel, name, outs, args, scratch=(), first=VMEM, cost=0):
    shapes = [jax.ShapeDtypeStruct(*o) for o in outs]
    return pl.pallas_call(
        kernel,
        in_specs=[first] + [VMEM] * (len(args) - 1),
        out_specs=[VMEM] * len(outs),
        out_shape=shapes,
        scratch_shapes=list(scratch),
        compiler_params=ROOM,
        cost_estimate=flops(cost),
        name=name,
    )(*args)


def along_bands(block, distance):
    count = lax.axis_size("band")
    return lax.ppermute(block, "band", [(i, (i + distance) % count) for i in range(count)])


def swapped(block):
    count = lax.axis_size("band")
    return lax.ppermute(block, "band", [(i, i ^ 1) for i in range(count)])


def on_even():
    return lax.axis_index("band") % 2 == 0


def by_permutes():
    count = lax.axis_size("dom")
    return count <= 8 and count & (count - 1) == 0


def from_all_domains(block):
    count = lax.axis_size("dom")
    if by_permutes():
        routes = [[(i, i ^ mask) for i in range(count)] for mask in range(1, count)]
        return [block] + [lax.ppermute(block, "dom", route) for route in routes]
    whole = lax.all_gather(block, "dom")
    return [whole[d] for d in range(count)]


def domain_at(place):
    return lax.axis_index("dom") ^ place if by_permutes() else place


def tile_of(extent, most):
    return max(w for w in range(128, most + 1, 128) if extent % w == 0)


def turn_kernel(coupling_ref, out_ref):
    owned, rank = coupling_ref.shape
    whole = coupling_ref[...]
    high = whole.astype(BF16)
    unit = lax.broadcasted_iota(jnp.int32, (rank, rank), 0) == lax.broadcasted_iota(
        jnp.int32, (rank, rank), 1
    )
    unit = jnp.where(unit, 1.0, 0.0).astype(BF16)
    for i, piece in enumerate((high, (whole - high.astype(F32)).astype(BF16))):
        turned = lax.dot_general(unit, piece, NT, preferred_element_type=F32)
        out_ref[:, i * owned : (i + 1) * owned] = turned.astype(BF16)


def project_kernel(orb_ref, proj_ref, turned_ref, out_ref):
    width, points = orb_ref.shape
    out_ref[width:, : turned_ref.shape[1]] = turned_ref[...]
    tile = tile_of(points, 1024)
    total = None
    for at in range(0, points, tile):
        term = lax.dot_general(
            proj_ref[:, at : at + tile], orb_ref[:, at : at + tile], NT, preferred_element_type=F32
        )
        total = term if total is None else total + term
    out_ref[:width, :] = total.T.astype(BF16)


def project(orbitals, proj, coupling):
    width, points = orbitals.shape
    owned, rank = coupling.shape
    turned = call(
        turn_kernel, "turn", [((rank, 2 * owned), BF16)], [coupling], cost=TURN
    )[0]
    outs = [((width + rank, proj.shape[0]), BF16)]
    return call(project_kernel, "project", outs, [orbitals, proj, turned])[0]


def couple_kernel(count, slots, owned, slot_ref, *refs):
    loads = refs[:count]
    out_ref, pick, high_ref, low_ref = refs[count:]
    width, flat = out_ref.shape
    rank = flat // slots
    me = lax.axis_index("dom")
    lanes = lax.broadcasted_iota(jnp.int32, (rank, flat), 1)
    unit = lanes % rank == lax.broadcasted_iota(jnp.int32, (rank, flat), 0)
    lane_slot = lanes // rank

    atoms = jnp.zeros((rank, flat), jnp.int32)
    for k in range(slots):
        atoms = jnp.where(lane_slot == k, slot_ref[me, k], atoms)

    columns = None
    for place in range(count):
        owner = domain_at(place)
        for a in range(owned):
            hit = unit & (atoms == owner * owned + a)
            pick[a * rank : (a + 1) * rank, :] = jnp.where(hit, 1.0, 0.0).astype(BF16)
        parts = [loads[place][width:, i * owned * rank : (i + 1) * owned * rank] for i in (0, 1)]
        term = jnp.dot(jnp.concatenate(parts, 0), pick[...], preferred_element_type=F32)
        columns = term if columns is None else columns + term
    high, low = columns[:rank], columns[rank:]

    total = None
    for place in range(count):
        domain = domain_at(place)
        for k in range(slots):
            hit = atoms == slot_ref[domain, k]
            rows = slice(k * rank, (k + 1) * rank)
            high_ref[rows, :] = jnp.where(hit, high, 0.0).astype(BF16)
            low_ref[rows, :] = jnp.where(hit, low, 0.0).astype(BF16)
        block = loads[place][:width, :]
        term = jnp.dot(block, high_ref[...], preferred_element_type=F32)
        term += jnp.dot(block, low_ref[...], preferred_element_type=F32)
        total = term if total is None else total + term
    out_ref[...] = total.astype(BF16)


def match_kernel(count, slots, owned, slot_ref, *refs):
    picks, matches = refs[:count], refs[count:]
    flat = matches[0].shape[0]
    rank = flat // slots
    me = lax.axis_index("dom")
    lanes = lax.broadcasted_iota(jnp.int32, (rank, flat), 1)
    unit = lanes % rank == lax.broadcasted_iota(jnp.int32, (rank, flat), 0)
    atoms = jnp.zeros((rank, flat), jnp.int32)
    for k in range(slots):
        atoms = jnp.where(lanes // rank == k, slot_ref[me, k], atoms)
    for place in range(count):
        domain = domain_at(place)
        for a in range(owned):
            hit = unit & (atoms == domain * owned + a)
            rows = slice(a * rank, (a + 1) * rank)
            picks[place][rows, :] = jnp.where(hit, 1.0, 0.0).astype(BF16)
        for k in range(slots):
            hit = unit & (atoms == slot_ref[domain, k])
            rows = slice(k * rank, (k + 1) * rank)
            matches[place][rows, :] = jnp.where(hit, 1.0, 0.0).astype(BF16)


def match(slot_atom, owned, rank):
    count, slots = slot_atom.shape
    flat = slots * rank
    outs = [((owned * rank, flat), BF16)] * count + [((flat, flat), BF16)] * count
    kernel = functools.partial(match_kernel, count, slots, owned)
    return call(kernel, "match", outs, [slot_atom], first=SMEM)


def couple_matched_kernel(count, *refs):
    loads, picks, matches = (refs[i * count : (i + 1) * count] for i in range(3))
    out_ref, high_ref, low_ref = refs[3 * count :]
    width, flat = out_ref.shape
    rank = loads[0].shape[0] - width
    size = picks[0].shape[0]

    columns = None
    for load, pick in zip(loads, picks):
        parts = [load[width:, i * size : (i + 1) * size] for i in (0, 1)]
        term = jnp.dot(jnp.concatenate(parts, 0), pick[...], preferred_element_type=F32)
        columns = term if columns is None else columns + term
    lane_slot = lax.broadcasted_iota(jnp.int32, (rank, flat), 1) // rank
    for k in range(flat // rank):
        rows = slice(k * rank, (k + 1) * rank)
        high_ref[rows, :] = jnp.where(lane_slot == k, columns[:rank], 0.0).astype(BF16)
        low_ref[rows, :] = jnp.where(lane_slot == k, columns[rank:], 0.0).astype(BF16)

    total = sum(
        jnp.dot(load[:width, :], x[...], preferred_element_type=F32)
        for load, x in zip(loads, matches)
    )
    high = total.astype(BF16)
    low = (total - high.astype(F32)).astype(BF16)
    terms = ((high, high_ref), (low, high_ref), (high, low_ref))
    coupled = sum(jnp.dot(x, y[...], preferred_element_type=F32) for x, y in terms)
    out_ref[...] = coupled.astype(BF16)


def couple_matched(loads, matched, width):
    flat = loads[0].shape[1]
    return call(
        functools.partial(couple_matched_kernel, len(loads)),
        "couple",
        [((width, flat), BF16)],
        [*loads, *matched],
        [pltpu.VMEM((flat, flat), BF16)] * 2,
        cost=COUPLE,
    )[0]


def couple(slot_atom, loads, width, owned):
    flat = loads[0].shape[1]
    slots = slot_atom.shape[1]
    return call(
        functools.partial(couple_kernel, len(loads), slots, owned),
        "couple",
        [((width, flat), BF16)],
        [slot_atom, *loads],
        [
            pltpu.VMEM((owned * (flat // slots), flat), BF16),
            pltpu.VMEM((flat, flat), BF16),
            pltpu.VMEM((flat, flat), BF16),
        ],
        first=SMEM,
        cost=COUPLE,
    )[0]


def halves_kernel(block_ref, *refs):
    upper_ref, lower_ref = refs[-2:]
    half = upper_ref.shape[0]
    upper_ref[...] = block_ref[:half, :]
    lower_ref[...] = block_ref[half:, :]


def halves(block, after, cost=0):
    half = ((block.shape[0] // 2, block.shape[1]), block.dtype)
    return call(halves_kernel, "halves", [half, half], [block, *after], cost=cost)


def hold_kernel(upper_ref, lower_ref, after_ref, out_ref):
    rows = upper_ref.shape[0]
    out_ref[:rows, :] = upper_ref[...]
    out_ref[rows:, :] = lower_ref[: out_ref.shape[0] - rows, :]


def hold(upper, lower, rows, after):
    shape = (rows, upper.shape[1])
    return call(hold_kernel, "hold", [(shape, upper.dtype)], [upper, lower, after])[0]


def packed(coef_shape, rows):
    width, flat = coef_shape
    return [
        (slice(i * flat, (i + 1) * flat), slice(i * rows, (i + 1) * rows))
        for i in range(width // rows)
    ]


def choose_kernel(mine, mine_two, two, lower, swap_ref, held_ref):
    width = two.shape[0]
    parts = packed(mine.shape, swap_ref.shape[0] - width)
    swap_ref[:width, :] = two[...]

    @pl.when(on_even())
    def _():
        for columns, rows in parts:
            swap_ref[width:, columns] = mine[rows, :]

    @pl.when(jnp.logical_not(on_even()))
    def _():
        for columns, rows in parts:
            swap_ref[width:, columns] = mine_two[rows, :]

    held_ref[...] = lower[lower.shape[0] - held_ref.shape[0] :, :]


def choose(mine, mine_two, two, lower):
    width, points = two.shape
    part = width // 4
    outs = [((width + part, points), two.dtype), ((part, points), two.dtype)]
    return call(choose_kernel, "choose", outs, [mine, mine_two, two, lower])


def where_even(tile, even):
    here = on_even() if even else jnp.logical_not(on_even())
    return jnp.where(here, tile.astype(F32), 0.0).astype(BF16)


def gather_kernel(rot_ref, own, one, two, upper, lower, three_a, out_ref, stack):
    width, points = own.shape
    depth = stack.shape[0]
    turn = jnp.concatenate(
        [rot_ref[:, : 3 * width], where_even(rot_ref[:, 3 * width : depth], True)], axis=1
    )
    stack[:width, :] = own[...]
    stack[width : 2 * width, :] = one[...]
    stack[3 * width :, :] = three_a[...]

    @pl.when(on_even())
    def _():
        stack[2 * width : 3 * width, :] = two[...]

    @pl.when(jnp.logical_not(on_even()))
    def _():
        stack[2 * width : 2 * width + upper.shape[0], :] = upper[...]
        stack[2 * width + upper.shape[0] : 3 * width, :] = lower[...]

    tile = tile_of(points, 1024)
    for at in range(0, points, tile):
        here = slice(at, at + tile)
        out_ref[:, here] = jnp.dot(turn, stack[:, here], preferred_element_type=F32)


def gather(rotation, *blocks):
    (width, points), rows = blocks[0].shape, blocks[-1].shape[0]
    scratch = [pltpu.VMEM((3 * width + rows, points), BF16)]
    return call(
        gather_kernel, "gather", [((width, points), F32)], [rotation, *blocks], scratch, cost=GATHER
    )[0]


def apply_kernel(rot_ref, mine, swap_ref, two, three, proj_ref, after_ref, out_ref):
    width, flat = mine.shape
    points = proj_ref.shape[1]
    one = [swap_ref[width:, columns] for columns, _ in packed(mine.shape, swap_ref.shape[0] - width)]
    blocks = (mine[...], jnp.concatenate(one, axis=0), two[...], three[...])
    mixed = sum(
        jnp.dot(rot_ref[:, s * width : (s + 1) * width], block, preferred_element_type=F32)
        for s, block in enumerate(blocks)
    )
    mixed = mixed.astype(BF16)
    tile = tile_of(points, 1024)
    for at in range(0, points, tile):
        out_ref[:, at : at + tile] = jnp.dot(
            mixed, proj_ref[:, at : at + tile], preferred_element_type=F32
        )


def finish_kernel(
    rot_ref, partial_ref, swap_ref, last_ref, applied, out_hbm, out_ref, sems
):
    width, points = out_ref.shape
    rows = last_ref.shape[0]
    pieces = sems.shape[0]
    tile = points // pieces
    turn = jnp.concatenate(
        [
            where_even(rot_ref[:, 3 * width : 4 * width], False),
            where_even(rot_ref[:, 4 * width - rows : 4 * width], True),
        ],
        axis=1,
    )
    copies = []
    for i in range(pieces):
        here = slice(i * tile, (i + 1) * tile)
        last = jnp.concatenate([swap_ref[:width, here], last_ref[:, here]], axis=0)
        rotated = partial_ref[:, here] + jnp.dot(turn, last, preferred_element_type=F32)
        added = rotated.astype(BF16).astype(F32) + applied[:, here]
        out_ref[:, here] = added.astype(out_ref.dtype)
        part = (slice(None), pl.ds(i * tile, tile))
        copies.append(pltpu.make_async_copy(out_ref.at[part], out_hbm.at[part], sems.at[i]))
        copies[-1].start()
    for copy in copies:
        copy.wait()


def finish(*args):
    width, points = args[-1].shape
    pieces = points // tile_of(points, 1024)
    return pl.pallas_call(
        finish_kernel,
        in_specs=[VMEM] * len(args),
        out_specs=pl.BlockSpec(memory_space=pl.ANY),
        out_shape=jax.ShapeDtypeStruct((width, points), BF16),
        scratch_shapes=[pltpu.VMEM((width, points), BF16), pltpu.SemaphoreType.DMA((pieces,))],
        compiler_params=ROOM,
        cost_estimate=flops(0),
        name="finish",
    )(*args)


def on_device(orbitals, rotation, projectors, coupling, slot_atom):
    width, points = orbitals.shape
    slot_count, rank, _ = projectors.shape
    owned = coupling.shape[0]
    proj = projectors.reshape(slot_count * rank, points)

    one = along_bands(orbitals, 1)
    upper, lower = [swapped(block) for block in halves(orbitals, [], CUT)]
    two = along_bands(hold(upper, lower, width, upper), 1)
    loads = from_all_domains(project(orbitals, proj, coupling.reshape(owned * rank, rank)))
    matched = list(match(slot_atom, owned, rank)) if by_permutes() else []
    upper, lower = [swapped(block) for block in halves(one, loads[-1:] + matched[:1])]
    if by_permutes():
        mine = couple_matched(loads, matched, width)
    else:
        mine = couple(slot_atom, loads, width, owned)
    mine_two = along_bands(mine, 2)
    three_a = along_bands(hold(upper, lower, width * 3 // 4, mine), 1)
    swap, held = choose(mine, mine_two, two, lower)
    mine_three = along_bands(mine_two, 1)
    three_b = along_bands(held, 1)
    swap = swapped(swap)
    partial = gather(rotation, orbitals, one, two, upper, lower, three_a)
    applied = call(
        apply_kernel,
        "apply",
        [((width, points), F32)],
        [rotation, mine, swap, mine_two, mine_three, proj, partial],
        cost=APPLY,
    )[0]
    return finish(rotation, partial, swap, three_b, applied)


def solution(mesh):
    in_specs = (P("band", "dom"), P("band", None), P(None, None, "dom"), P("dom", None, None), P())
    out_specs = P("band", "dom")
    return jax.shard_map(
        on_device, mesh=mesh, in_specs=in_specs, out_specs=out_specs, check_vma=False
    )
```

```python
import functools

import jax
import jax.numpy as jnp
from jax import lax
from jax.experimental import pallas as pl
from jax.experimental.pallas import tpu as pltpu
from jax.sharding import PartitionSpec as P

TURN = 0 * 10**9
CUT = 30 * 10**8
COUPLE = 4 * 10**9
APPLY = 50 * 10**8
GATHER = 45 * 10**8

F32 = jnp.float32
BF16 = jnp.bfloat16
ROOM = pltpu.CompilerParams(vmem_limit_bytes=8 * 2**20)
NT = (((1,), (1,)), ((), ()))
VMEM = pl.BlockSpec(memory_space=pltpu.VMEM)
SMEM = pl.BlockSpec(memory_space=pltpu.SMEM)


def flops(count):
    return pl.CostEstimate(flops=count, bytes_accessed=0, transcendentals=0)


def call(kernel, name, outs, args, scratch=(), first=VMEM, cost=0):
    shapes = [jax.ShapeDtypeStruct(*o) for o in outs]
    return pl.pallas_call(
        kernel,
        in_specs=[first] + [VMEM] * (len(args) - 1),
        out_specs=[VMEM] * len(outs),
        out_shape=shapes,
        scratch_shapes=list(scratch),
        compiler_params=ROOM,
        cost_estimate=flops(cost),
        name=name,
    )(*args)


def along_bands(block, distance):
    count = lax.axis_size("band")
    return lax.ppermute(block, "band", [(i, (i + distance) % count) for i in range(count)])


def swapped(block):
    count = lax.axis_size("band")
    return lax.ppermute(block, "band", [(i, i ^ 1) for i in range(count)])


def on_even():
    return lax.axis_index("band") % 2 == 0


def by_permutes():
    count = lax.axis_size("dom")
    return count <= 8 and count & (count - 1) == 0


def from_all_domains(block):
    count = lax.axis_size("dom")
    if by_permutes():
        routes = [[(i, i ^ mask) for i in range(count)] for mask in range(1, count)]
        return [block] + [lax.ppermute(block, "dom", route) for route in routes]
    whole = lax.all_gather(block, "dom")
    return [whole[d] for d in range(count)]


def domain_at(place):
    return lax.axis_index("dom") ^ place if by_permutes() else place


def tile_of(extent, most):
    return max(w for w in range(128, most + 1, 128) if extent % w == 0)


def turn_kernel(coupling_ref, out_ref):
    owned, rank = coupling_ref.shape
    whole = coupling_ref[...]
    high = whole.astype(BF16)
    unit = lax.broadcasted_iota(jnp.int32, (rank, rank), 0) == lax.broadcasted_iota(
        jnp.int32, (rank, rank), 1
    )
    unit = jnp.where(unit, 1.0, 0.0).astype(BF16)
    for i, piece in enumerate((high, (whole - high.astype(F32)).astype(BF16))):
        turned = lax.dot_general(unit, piece, NT, preferred_element_type=F32)
        out_ref[:, i * owned : (i + 1) * owned] = turned.astype(BF16)


def project_kernel(orb_ref, proj_ref, turned_ref, out_ref):
    width, points = orb_ref.shape
    out_ref[width:, : turned_ref.shape[1]] = turned_ref[...]
    tile = tile_of(points, 1024)
    total = None
    for at in range(0, points, tile):
        term = lax.dot_general(
            proj_ref[:, at : at + tile], orb_ref[:, at : at + tile], NT, preferred_element_type=F32
        )
        total = term if total is None else total + term
    out_ref[:width, :] = total.T.astype(BF16)


def project(orbitals, proj, coupling):
    width, points = orbitals.shape
    owned, rank = coupling.shape
    turned = call(
        turn_kernel, "turn", [((rank, 2 * owned), BF16)], [coupling], cost=TURN
    )[0]
    outs = [((width + rank, proj.shape[0]), BF16)]
    return call(project_kernel, "project", outs, [orbitals, proj, turned])[0]


def couple_kernel(count, slots, owned, slot_ref, *refs):
    loads = refs[:count]
    out_ref, pick, high_ref, low_ref = refs[count:]
    width, flat = out_ref.shape
    rank = flat // slots
    me = lax.axis_index("dom")
    lanes = lax.broadcasted_iota(jnp.int32, (rank, flat), 1)
    unit = lanes % rank == lax.broadcasted_iota(jnp.int32, (rank, flat), 0)
    lane_slot = lanes // rank

    atoms = jnp.zeros((rank, flat), jnp.int32)
    for k in range(slots):
        atoms = jnp.where(lane_slot == k, slot_ref[me, k], atoms)

    columns = None
    for place in range(count):
        owner = domain_at(place)
        for a in range(owned):
            hit = unit & (atoms == owner * owned + a)
            pick[a * rank : (a + 1) * rank, :] = jnp.where(hit, 1.0, 0.0).astype(BF16)
        parts = [loads[place][width:, i * owned * rank : (i + 1) * owned * rank] for i in (0, 1)]
        term = jnp.dot(jnp.concatenate(parts, 0), pick[...], preferred_element_type=F32)
        columns = term if columns is None else columns + term
    high, low = columns[:rank], columns[rank:]

    total = None
    for place in range(count):
        domain = domain_at(place)
        for k in range(slots):
            hit = atoms == slot_ref[domain, k]
            rows = slice(k * rank, (k + 1) * rank)
            high_ref[rows, :] = jnp.where(hit, high, 0.0).astype(BF16)
            low_ref[rows, :] = jnp.where(hit, low, 0.0).astype(BF16)
        block = loads[place][:width, :]
        term = jnp.dot(block, high_ref[...], preferred_element_type=F32)
        term += jnp.dot(block, low_ref[...], preferred_element_type=F32)
        total = term if total is None else total + term
    out_ref[...] = total.astype(BF16)


def match_kernel(count, slots, owned, slot_ref, *refs):
    picks, matches = refs[:count], refs[count:]
    flat = matches[0].shape[0]
    rank = flat // slots
    me = lax.axis_index("dom")
    lanes = lax.broadcasted_iota(jnp.int32, (rank, flat), 1)
    unit = lanes % rank == lax.broadcasted_iota(jnp.int32, (rank, flat), 0)
    atoms = jnp.zeros((rank, flat), jnp.int32)
    for k in range(slots):
        atoms = jnp.where(lanes // rank == k, slot_ref[me, k], atoms)
    for place in range(count):
        domain = domain_at(place)
        for a in range(owned):
            hit = unit & (atoms == domain * owned + a)
            rows = slice(a * rank, (a + 1) * rank)
            picks[place][rows, :] = jnp.where(hit, 1.0, 0.0).astype(BF16)
        for k in range(slots):
            hit = unit & (atoms == slot_ref[domain, k])
            rows = slice(k * rank, (k + 1) * rank)
            matches[place][rows, :] = jnp.where(hit, 1.0, 0.0).astype(BF16)


def match(slot_atom, owned, rank):
    count, slots = slot_atom.shape
    flat = slots * rank
    outs = [((owned * rank, flat), BF16)] * count + [((flat, flat), BF16)] * count
    kernel = functools.partial(match_kernel, count, slots, owned)
    return call(kernel, "match", outs, [slot_atom], first=SMEM)


def couple_matched_kernel(count, *refs):
    loads, picks, matches = (refs[i * count : (i + 1) * count] for i in range(3))
    out_ref, high_ref, low_ref = refs[3 * count :]
    width, flat = out_ref.shape
    rank = loads[0].shape[0] - width
    size = picks[0].shape[0]

    columns = None
    for load, pick in zip(loads, picks):
        parts = [load[width:, i * size : (i + 1) * size] for i in (0, 1)]
        term = jnp.dot(jnp.concatenate(parts, 0), pick[...], preferred_element_type=F32)
        columns = term if columns is None else columns + term
    lane_slot = lax.broadcasted_iota(jnp.int32, (rank, flat), 1) // rank
    for k in range(flat // rank):
        rows = slice(k * rank, (k + 1) * rank)
        high_ref[rows, :] = jnp.where(lane_slot == k, columns[:rank], 0.0).astype(BF16)
        low_ref[rows, :] = jnp.where(lane_slot == k, columns[rank:], 0.0).astype(BF16)

    total = sum(
        jnp.dot(load[:width, :], x[...], preferred_element_type=F32)
        for load, x in zip(loads, matches)
    )
    high = total.astype(BF16)
    low = (total - high.astype(F32)).astype(BF16)
    terms = ((high, high_ref), (low, high_ref), (high, low_ref))
    coupled = sum(jnp.dot(x, y[...], preferred_element_type=F32) for x, y in terms)
    out_ref[...] = coupled.astype(BF16)


def couple_matched(loads, matched, width):
    flat = loads[0].shape[1]
    return call(
        functools.partial(couple_matched_kernel, len(loads)),
        "couple",
        [((width, flat), BF16)],
        [*loads, *matched],
        [pltpu.VMEM((flat, flat), BF16)] * 2,
        cost=COUPLE,
    )[0]


def couple(slot_atom, loads, width, owned):
    flat = loads[0].shape[1]
    slots = slot_atom.shape[1]
    return call(
        functools.partial(couple_kernel, len(loads), slots, owned),
        "couple",
        [((width, flat), BF16)],
        [slot_atom, *loads],
        [
            pltpu.VMEM((owned * (flat // slots), flat), BF16),
            pltpu.VMEM((flat, flat), BF16),
            pltpu.VMEM((flat, flat), BF16),
        ],
        first=SMEM,
        cost=COUPLE,
    )[0]


def halves_kernel(block_ref, *refs):
    upper_ref, lower_ref = refs[-2:]
    half = upper_ref.shape[0]
    upper_ref[...] = block_ref[:half, :]
    lower_ref[...] = block_ref[half:, :]


def halves(block, after, cost=0):
    half = ((block.shape[0] // 2, block.shape[1]), block.dtype)
    return call(halves_kernel, "halves", [half, half], [block, *after], cost=cost)


def hold_kernel(upper_ref, lower_ref, after_ref, out_ref):
    rows = upper_ref.shape[0]
    out_ref[:rows, :] = upper_ref[...]
    out_ref[rows:, :] = lower_ref[: out_ref.shape[0] - rows, :]


def hold(upper, lower, rows, after):
    shape = (rows, upper.shape[1])
    return call(hold_kernel, "hold", [(shape, upper.dtype)], [upper, lower, after])[0]


def packed(coef_shape, rows):
    width, flat = coef_shape
    return [
        (slice(i * flat, (i + 1) * flat), slice(i * rows, (i + 1) * rows))
        for i in range(width // rows)
    ]


def choose_kernel(mine, mine_two, two, lower, swap_ref, held_ref):
    width = two.shape[0]
    parts = packed(mine.shape, swap_ref.shape[0] - width)
    swap_ref[:width, :] = two[...]

    @pl.when(on_even())
    def _():
        for columns, rows in parts:
            swap_ref[width:, columns] = mine[rows, :]

    @pl.when(jnp.logical_not(on_even()))
    def _():
        for columns, rows in parts:
            swap_ref[width:, columns] = mine_two[rows, :]

    held_ref[...] = lower[lower.shape[0] - held_ref.shape[0] :, :]


def choose(mine, mine_two, two, lower):
    width, points = two.shape
    part = width // 4
    outs = [((width + part, points), two.dtype), ((part, points), two.dtype)]
    return call(choose_kernel, "choose", outs, [mine, mine_two, two, lower])


def where_even(tile, even):
    here = on_even() if even else jnp.logical_not(on_even())
    return jnp.where(here, tile.astype(F32), 0.0).astype(BF16)


def gather_kernel(rot_ref, own, one, two, upper, lower, three_a, out_ref, stack):
    width, points = own.shape
    depth = stack.shape[0]
    turn = jnp.concatenate(
        [rot_ref[:, : 3 * width], where_even(rot_ref[:, 3 * width : depth], True)], axis=1
    )
    stack[:width, :] = own[...]
    stack[width : 2 * width, :] = one[...]
    stack[3 * width :, :] = three_a[...]

    @pl.when(on_even())
    def _():
        stack[2 * width : 3 * width, :] = two[...]

    @pl.when(jnp.logical_not(on_even()))
    def _():
        stack[2 * width : 2 * width + upper.shape[0], :] = upper[...]
        stack[2 * width + upper.shape[0] : 3 * width, :] = lower[...]

    tile = tile_of(points, 1024)
    for at in range(0, points, tile):
        here = slice(at, at + tile)
        out_ref[:, here] = jnp.dot(turn, stack[:, here], preferred_element_type=F32)


def gather(rotation, *blocks):
    (width, points), rows = blocks[0].shape, blocks[-1].shape[0]
    scratch = [pltpu.VMEM((3 * width + rows, points), BF16)]
    return call(
        gather_kernel, "gather", [((width, points), F32)], [rotation, *blocks], scratch, cost=GATHER
    )[0]


def apply_kernel(rot_ref, mine, swap_ref, two, three, proj_ref, after_ref, out_ref):
    width, flat = mine.shape
    points = proj_ref.shape[1]
    one = [swap_ref[width:, columns] for columns, _ in packed(mine.shape, swap_ref.shape[0] - width)]
    blocks = (mine[...], jnp.concatenate(one, axis=0), two[...], three[...])
    mixed = sum(
        jnp.dot(rot_ref[:, s * width : (s + 1) * width], block, preferred_element_type=F32)
        for s, block in enumerate(blocks)
    )
    mixed = mixed.astype(BF16)
    tile = tile_of(points, 1024)
    for at in range(0, points, tile):
        out_ref[:, at : at + tile] = jnp.dot(
            mixed, proj_ref[:, at : at + tile], preferred_element_type=F32
        )


def tiles_of(points):
    if points % 1024:
        tile = tile_of(points, 1024)
        return [(at, tile) for at in range(0, points, tile)]
    ends = [0] + list(range(512, points, 1024)) + [points]
    return [(at, end - at) for at, end in zip(ends, ends[1:])]


def finish_kernel(
    rot_ref, partial_ref, swap_ref, last_ref, applied, out_hbm, out_ref, sems
):
    width, points = out_ref.shape
    rows = last_ref.shape[0]
    on_odd = where_even(rot_ref[:, 3 * width : 4 * width], False)
    on_last = where_even(rot_ref[:, 4 * width - rows : 4 * width], True)
    copies = []
    for i, (at, tile) in enumerate(tiles_of(points)):
        here = slice(at, at + tile)
        rotated = partial_ref[:, here]
        rotated += jnp.dot(on_odd, swap_ref[:width, here], preferred_element_type=F32)
        rotated += jnp.dot(on_last, last_ref[:, here], preferred_element_type=F32)
        added = rotated.astype(BF16).astype(F32) + applied[:, here]
        out_ref[:, here] = added.astype(out_ref.dtype)
        part = (slice(None), pl.ds(at, tile))
        copies.append(pltpu.make_async_copy(out_ref.at[part], out_hbm.at[part], sems.at[i]))
        copies[-1].start()
    for copy in copies:
        copy.wait()


def finish(*args):
    width, points = args[-1].shape
    pieces = len(tiles_of(points))
    return pl.pallas_call(
        finish_kernel,
        in_specs=[VMEM] * len(args),
        out_specs=pl.BlockSpec(memory_space=pl.ANY),
        out_shape=jax.ShapeDtypeStruct((width, points), BF16),
        scratch_shapes=[pltpu.VMEM((width, points), BF16), pltpu.SemaphoreType.DMA((pieces,))],
        compiler_params=ROOM,
        cost_estimate=flops(0),
        name="finish",
    )(*args)


def on_device(orbitals, rotation, projectors, coupling, slot_atom):
    width, points = orbitals.shape
    slot_count, rank, _ = projectors.shape
    owned = coupling.shape[0]
    proj = projectors.reshape(slot_count * rank, points)

    one = along_bands(orbitals, 1)
    upper, lower = [swapped(block) for block in halves(orbitals, [], CUT)]
    two = along_bands(hold(upper, lower, width, upper), 1)
    loads = from_all_domains(project(orbitals, proj, coupling.reshape(owned * rank, rank)))
    matched = list(match(slot_atom, owned, rank)) if by_permutes() else []
    upper, lower = [swapped(block) for block in halves(one, loads[-1:] + matched[:1])]
    if by_permutes():
        mine = couple_matched(loads, matched, width)
    else:
        mine = couple(slot_atom, loads, width, owned)
    mine_two = along_bands(mine, 2)
    three_a = along_bands(hold(upper, lower, width * 3 // 4, mine), 1)
    swap, held = choose(mine, mine_two, two, lower)
    mine_three = along_bands(mine_two, 1)
    three_b = along_bands(held, 1)
    swap = swapped(swap)
    partial = gather(rotation, orbitals, one, two, upper, lower, three_a)
    applied = call(
        apply_kernel,
        "apply",
        [((width, points), F32)],
        [rotation, mine, swap, mine_two, mine_three, proj, partial],
        cost=APPLY,
    )[0]
    return finish(rotation, partial, swap, three_b, applied)


def solution(mesh):
    in_specs = (P("band", "dom"), P("band", None), P(None, None, "dom"), P("dom", None, None), P())
    out_specs = P("band", "dom")
    return jax.shard_map(
        on_device, mesh=mesh, in_specs=in_specs, out_specs=out_specs, check_vma=False
    )
```

```python
import functools

import jax
import jax.numpy as jnp
from jax import lax
from jax.experimental import pallas as pl
from jax.experimental.pallas import tpu as pltpu
from jax.sharding import PartitionSpec as P

TURN = 0 * 10**9
CUT = 30 * 10**8
COUPLE = 4 * 10**9
APPLY = 50 * 10**8
GATHER = 45 * 10**8

F32 = jnp.float32
BF16 = jnp.bfloat16
ROOM = pltpu.CompilerParams(vmem_limit_bytes=8 * 2**20)
NT = (((1,), (1,)), ((), ()))
VMEM = pl.BlockSpec(memory_space=pltpu.VMEM)
SMEM = pl.BlockSpec(memory_space=pltpu.SMEM)


def flops(count):
    return pl.CostEstimate(flops=count, bytes_accessed=0, transcendentals=0)


def call(kernel, name, outs, args, scratch=(), first=VMEM, cost=0):
    shapes = [jax.ShapeDtypeStruct(*o) for o in outs]
    return pl.pallas_call(
        kernel,
        in_specs=[first] + [VMEM] * (len(args) - 1),
        out_specs=[VMEM] * len(outs),
        out_shape=shapes,
        scratch_shapes=list(scratch),
        compiler_params=ROOM,
        cost_estimate=flops(cost),
        name=name,
    )(*args)


def along_bands(block, distance):
    count = lax.axis_size("band")
    return lax.ppermute(block, "band", [(i, (i + distance) % count) for i in range(count)])


def swapped(block):
    count = lax.axis_size("band")
    return lax.ppermute(block, "band", [(i, i ^ 1) for i in range(count)])


def on_even():
    return lax.axis_index("band") % 2 == 0


def by_permutes():
    count = lax.axis_size("dom")
    return count <= 8 and count & (count - 1) == 0


def from_all_domains(block):
    count = lax.axis_size("dom")
    if by_permutes():
        routes = [[(i, i ^ mask) for i in range(count)] for mask in range(1, count)]
        return [block] + [lax.ppermute(block, "dom", route) for route in routes]
    whole = lax.all_gather(block, "dom")
    return [whole[d] for d in range(count)]


def domain_at(place):
    return lax.axis_index("dom") ^ place if by_permutes() else place


def tile_of(extent, most):
    return max(w for w in range(128, most + 1, 128) if extent % w == 0)


def turn_kernel(coupling_ref, out_ref):
    owned, rank = coupling_ref.shape
    whole = coupling_ref[...]
    high = whole.astype(BF16)
    unit = lax.broadcasted_iota(jnp.int32, (rank, rank), 0) == lax.broadcasted_iota(
        jnp.int32, (rank, rank), 1
    )
    unit = jnp.where(unit, 1.0, 0.0).astype(BF16)
    for i, piece in enumerate((high, (whole - high.astype(F32)).astype(BF16))):
        turned = lax.dot_general(unit, piece, NT, preferred_element_type=F32)
        out_ref[:, i * owned : (i + 1) * owned] = turned.astype(BF16)


def project_kernel(orb_ref, proj_ref, turned_ref, out_ref):
    width, points = orb_ref.shape
    out_ref[width:, : turned_ref.shape[1]] = turned_ref[...]
    tile = tile_of(points, 1024)
    total = None
    for at in range(0, points, tile):
        term = lax.dot_general(
            proj_ref[:, at : at + tile], orb_ref[:, at : at + tile], NT, preferred_element_type=F32
        )
        total = term if total is None else total + term
    out_ref[:width, :] = total.T.astype(BF16)


def project(orbitals, proj, coupling):
    width, points = orbitals.shape
    owned, rank = coupling.shape
    turned = call(
        turn_kernel, "turn", [((rank, 2 * owned), BF16)], [coupling], cost=TURN
    )[0]
    outs = [((width + rank, proj.shape[0]), BF16)]
    return call(project_kernel, "project", outs, [orbitals, proj, turned])[0]


def couple_kernel(count, slots, owned, slot_ref, *refs):
    loads = refs[:count]
    out_ref, pick, high_ref, low_ref = refs[count:]
    width, flat = out_ref.shape
    rank = flat // slots
    me = lax.axis_index("dom")
    lanes = lax.broadcasted_iota(jnp.int32, (rank, flat), 1)
    unit = lanes % rank == lax.broadcasted_iota(jnp.int32, (rank, flat), 0)
    lane_slot = lanes // rank

    atoms = jnp.zeros((rank, flat), jnp.int32)
    for k in range(slots):
        atoms = jnp.where(lane_slot == k, slot_ref[me, k], atoms)

    columns = None
    for place in range(count):
        owner = domain_at(place)
        for a in range(owned):
            hit = unit & (atoms == owner * owned + a)
            pick[a * rank : (a + 1) * rank, :] = jnp.where(hit, 1.0, 0.0).astype(BF16)
        parts = [loads[place][width:, i * owned * rank : (i + 1) * owned * rank] for i in (0, 1)]
        term = jnp.dot(jnp.concatenate(parts, 0), pick[...], preferred_element_type=F32)
        columns = term if columns is None else columns + term
    high, low = columns[:rank], columns[rank:]

    total = None
    for place in range(count):
        domain = domain_at(place)
        for k in range(slots):
            hit = atoms == slot_ref[domain, k]
            rows = slice(k * rank, (k + 1) * rank)
            high_ref[rows, :] = jnp.where(hit, high, 0.0).astype(BF16)
            low_ref[rows, :] = jnp.where(hit, low, 0.0).astype(BF16)
        block = loads[place][:width, :]
        term = jnp.dot(block, high_ref[...], preferred_element_type=F32)
        term += jnp.dot(block, low_ref[...], preferred_element_type=F32)
        total = term if total is None else total + term
    out_ref[...] = total.astype(BF16)


def match_kernel(count, slots, owned, slot_ref, *refs):
    picks, matches = refs[:count], refs[count:]
    flat = matches[0].shape[0]
    rank = flat // slots
    me = lax.axis_index("dom")
    lanes = lax.broadcasted_iota(jnp.int32, (rank, flat), 1)
    unit = lanes % rank == lax.broadcasted_iota(jnp.int32, (rank, flat), 0)
    atoms = jnp.zeros((rank, flat), jnp.int32)
    for k in range(slots):
        atoms = jnp.where(lanes // rank == k, slot_ref[me, k], atoms)
    for place in range(count):
        domain = domain_at(place)
        for a in range(owned):
            hit = unit & (atoms == domain * owned + a)
            rows = slice(a * rank, (a + 1) * rank)
            picks[place][rows, :] = jnp.where(hit, 1.0, 0.0).astype(BF16)
        for k in range(slots):
            hit = unit & (atoms == slot_ref[domain, k])
            rows = slice(k * rank, (k + 1) * rank)
            matches[place][rows, :] = jnp.where(hit, 1.0, 0.0).astype(BF16)


def match(slot_atom, owned, rank):
    count, slots = slot_atom.shape
    flat = slots * rank
    outs = [((owned * rank, flat), BF16)] * count + [((flat, flat), BF16)] * count
    kernel = functools.partial(match_kernel, count, slots, owned)
    return call(kernel, "match", outs, [slot_atom], first=SMEM)


def couple_matched_kernel(count, *refs):
    loads, picks, matches = (refs[i * count : (i + 1) * count] for i in range(3))
    out_ref, high_ref, low_ref = refs[3 * count :]
    width, flat = out_ref.shape
    rank = loads[0].shape[0] - width
    size = picks[0].shape[0]

    columns = None
    for load, pick in zip(loads, picks):
        parts = [load[width:, i * size : (i + 1) * size] for i in (0, 1)]
        term = jnp.dot(jnp.concatenate(parts, 0), pick[...], preferred_element_type=F32)
        columns = term if columns is None else columns + term
    lane_slot = lax.broadcasted_iota(jnp.int32, (rank, flat), 1) // rank
    for k in range(flat // rank):
        rows = slice(k * rank, (k + 1) * rank)
        high_ref[rows, :] = jnp.where(lane_slot == k, columns[:rank], 0.0).astype(BF16)
        low_ref[rows, :] = jnp.where(lane_slot == k, columns[rank:], 0.0).astype(BF16)

    total = sum(
        jnp.dot(load[:width, :], x[...], preferred_element_type=F32)
        for load, x in zip(loads, matches)
    )
    high = total.astype(BF16)
    low = (total - high.astype(F32)).astype(BF16)
    terms = ((high, high_ref), (low, high_ref), (high, low_ref))
    coupled = sum(jnp.dot(x, y[...], preferred_element_type=F32) for x, y in terms)
    out_ref[...] = coupled.astype(BF16)


def couple_matched(loads, matched, width):
    flat = loads[0].shape[1]
    return call(
        functools.partial(couple_matched_kernel, len(loads)),
        "couple",
        [((width, flat), BF16)],
        [*loads, *matched],
        [pltpu.VMEM((flat, flat), BF16)] * 2,
        cost=COUPLE,
    )[0]


def couple(slot_atom, loads, width, owned):
    flat = loads[0].shape[1]
    slots = slot_atom.shape[1]
    return call(
        functools.partial(couple_kernel, len(loads), slots, owned),
        "couple",
        [((width, flat), BF16)],
        [slot_atom, *loads],
        [
            pltpu.VMEM((owned * (flat // slots), flat), BF16),
            pltpu.VMEM((flat, flat), BF16),
            pltpu.VMEM((flat, flat), BF16),
        ],
        first=SMEM,
        cost=COUPLE,
    )[0]


def halves_kernel(block_ref, *refs):
    upper_ref, lower_ref = refs[-2:]
    half = upper_ref.shape[0]
    upper_ref[...] = block_ref[:half, :]
    lower_ref[...] = block_ref[half:, :]


def halves(block, after, cost=0):
    half = ((block.shape[0] // 2, block.shape[1]), block.dtype)
    return call(halves_kernel, "halves", [half, half], [block, *after], cost=cost)


def hold_kernel(upper_ref, lower_ref, after_ref, out_ref):
    rows = upper_ref.shape[0]
    out_ref[:rows, :] = upper_ref[...]
    out_ref[rows:, :] = lower_ref[: out_ref.shape[0] - rows, :]


def hold(upper, lower, rows, after):
    shape = (rows, upper.shape[1])
    return call(hold_kernel, "hold", [(shape, upper.dtype)], [upper, lower, after])[0]


def packed(coef_shape, rows):
    width, flat = coef_shape
    return [
        (slice(i * flat, (i + 1) * flat), slice(i * rows, (i + 1) * rows))
        for i in range(width // rows)
    ]


def choose_kernel(mine, mine_two, two, lower, swap_ref, held_ref):
    width = two.shape[0]
    parts = packed(mine.shape, swap_ref.shape[0] - width)
    swap_ref[:width, :] = two[...]

    @pl.when(on_even())
    def _():
        for columns, rows in parts:
            swap_ref[width:, columns] = mine[rows, :]

    @pl.when(jnp.logical_not(on_even()))
    def _():
        for columns, rows in parts:
            swap_ref[width:, columns] = mine_two[rows, :]

    held_ref[...] = lower[lower.shape[0] - held_ref.shape[0] :, :]


def choose(mine, mine_two, two, lower):
    width, points = two.shape
    part = width // 4
    outs = [((width + part, points), two.dtype), ((part, points), two.dtype)]
    return call(choose_kernel, "choose", outs, [mine, mine_two, two, lower])


def where_even(tile, even):
    here = on_even() if even else jnp.logical_not(on_even())
    return jnp.where(here, tile.astype(F32), 0.0).astype(BF16)


def gather_kernel(rot_ref, own, one, two, upper, lower, three_a, out_ref, stack):
    width, points = own.shape
    depth = stack.shape[0]
    turn = jnp.concatenate(
        [rot_ref[:, : 3 * width], where_even(rot_ref[:, 3 * width : depth], True)], axis=1
    )
    stack[:width, :] = own[...]
    stack[width : 2 * width, :] = one[...]
    stack[3 * width :, :] = three_a[...]

    @pl.when(on_even())
    def _():
        stack[2 * width : 3 * width, :] = two[...]

    @pl.when(jnp.logical_not(on_even()))
    def _():
        stack[2 * width : 2 * width + upper.shape[0], :] = upper[...]
        stack[2 * width + upper.shape[0] : 3 * width, :] = lower[...]

    tile = tile_of(points, 1024)
    for at in range(0, points, tile):
        here = slice(at, at + tile)
        out_ref[:, here] = jnp.dot(turn, stack[:, here], preferred_element_type=F32)


def gather(rotation, *blocks):
    (width, points), rows = blocks[0].shape, blocks[-1].shape[0]
    scratch = [pltpu.VMEM((3 * width + rows, points), BF16)]
    return call(
        gather_kernel, "gather", [((width, points), F32)], [rotation, *blocks], scratch, cost=GATHER
    )[0]


def apply_kernel(rot_ref, mine, swap_ref, two, three, proj_ref, after_ref, out_ref):
    width, flat = mine.shape
    points = proj_ref.shape[1]
    one = [swap_ref[width:, columns] for columns, _ in packed(mine.shape, swap_ref.shape[0] - width)]
    blocks = (mine[...], jnp.concatenate(one, axis=0), two[...], three[...])
    mixed = sum(
        jnp.dot(rot_ref[:, s * width : (s + 1) * width], block, preferred_element_type=F32)
        for s, block in enumerate(blocks)
    )
    mixed = mixed.astype(BF16)
    tile = tile_of(points, 1024)
    for at in range(0, points, tile):
        out_ref[:, at : at + tile] = jnp.dot(
            mixed, proj_ref[:, at : at + tile], preferred_element_type=F32
        )


def add_kernel(rot_ref, partial_ref, swap_ref, applied, out_ref):
    width, points = out_ref.shape
    turn = where_even(rot_ref[:, 3 * width : 4 * width], False)
    tile = tile_of(points, 1024)
    for at in range(0, points, tile):
        here = slice(at, at + tile)
        out_ref[:, here] = partial_ref[:, here] + jnp.dot(
            turn, swap_ref[:width, here], preferred_element_type=F32
        )


def finish_kernel(rot_ref, partial_ref, last_ref, applied, out_hbm, out_ref, sems):
    width, points = out_ref.shape
    pieces = sems.shape[0]
    tile = points // pieces
    turn = where_even(rot_ref[:, 4 * width - last_ref.shape[0] : 4 * width], True)
    copies = []
    for i in range(pieces):
        here = slice(i * tile, (i + 1) * tile)
        rotated = partial_ref[:, here] + jnp.dot(
            turn, last_ref[:, here], preferred_element_type=F32
        )
        added = rotated.astype(BF16).astype(F32) + applied[:, here]
        out_ref[:, here] = added.astype(out_ref.dtype)
        part = (slice(None), pl.ds(i * tile, tile))
        copies.append(pltpu.make_async_copy(out_ref.at[part], out_hbm.at[part], sems.at[i]))
        copies[-1].start()
    for copy in copies:
        copy.wait()


def finish(*args):
    width, points = args[-1].shape
    pieces = points // tile_of(points, 1024)
    return pl.pallas_call(
        finish_kernel,
        in_specs=[VMEM] * len(args),
        out_specs=pl.BlockSpec(memory_space=pl.ANY),
        out_shape=jax.ShapeDtypeStruct((width, points), BF16),
        scratch_shapes=[pltpu.VMEM((width, points), BF16), pltpu.SemaphoreType.DMA((pieces,))],
        compiler_params=ROOM,
        cost_estimate=flops(0),
        name="finish",
    )(*args)


def on_device(orbitals, rotation, projectors, coupling, slot_atom):
    width, points = orbitals.shape
    slot_count, rank, _ = projectors.shape
    owned = coupling.shape[0]
    proj = projectors.reshape(slot_count * rank, points)

    one = along_bands(orbitals, 1)
    upper, lower = [swapped(block) for block in halves(orbitals, [], CUT)]
    two = along_bands(hold(upper, lower, width, upper), 1)
    loads = from_all_domains(project(orbitals, proj, coupling.reshape(owned * rank, rank)))
    matched = list(match(slot_atom, owned, rank)) if by_permutes() else []
    upper, lower = [swapped(block) for block in halves(one, loads[-1:] + matched[:1])]
    if by_permutes():
        mine = couple_matched(loads, matched, width)
    else:
        mine = couple(slot_atom, loads, width, owned)
    mine_two = along_bands(mine, 2)
    three_a = along_bands(hold(upper, lower, width * 3 // 4, mine), 1)
    swap, held = choose(mine, mine_two, two, lower)
    mine_three = along_bands(mine_two, 1)
    three_b = along_bands(held, 1)
    swap = swapped(swap)
    partial = gather(rotation, orbitals, one, two, upper, lower, three_a)
    applied = call(
        apply_kernel,
        "apply",
        [((width, points), F32)],
        [rotation, mine, swap, mine_two, mine_three, proj, partial],
        cost=APPLY,
    )[0]
    outs = [(partial.shape, F32)]
    partial = call(add_kernel, "add", outs, [rotation, partial, swap, applied])[0]
    return finish(rotation, partial, three_b, applied)


def solution(mesh):
    in_specs = (P("band", "dom"), P("band", None), P(None, None, "dom"), P("dom", None, None), P())
    out_specs = P("band", "dom")
    return jax.shard_map(
        on_device, mesh=mesh, in_specs=in_specs, out_specs=out_specs, check_vma=False
    )
```

```python
import functools

import jax
import jax.numpy as jnp
from jax import lax
from jax.experimental import pallas as pl
from jax.experimental.pallas import tpu as pltpu
from jax.sharding import PartitionSpec as P

TURN = 0 * 10**9
CUT = 30 * 10**8
COUPLE = 4 * 10**9
APPLY = 50 * 10**8
GATHER = 45 * 10**8

F32 = jnp.float32
BF16 = jnp.bfloat16
ROOM = pltpu.CompilerParams(vmem_limit_bytes=8 * 2**20)
NT = (((1,), (1,)), ((), ()))
VMEM = pl.BlockSpec(memory_space=pltpu.VMEM)
SMEM = pl.BlockSpec(memory_space=pltpu.SMEM)


def flops(count):
    return pl.CostEstimate(flops=count, bytes_accessed=0, transcendentals=0)


def call(kernel, name, outs, args, scratch=(), first=VMEM, cost=0):
    shapes = [jax.ShapeDtypeStruct(*o) for o in outs]
    return pl.pallas_call(
        kernel,
        in_specs=[first] + [VMEM] * (len(args) - 1),
        out_specs=[VMEM] * len(outs),
        out_shape=shapes,
        scratch_shapes=list(scratch),
        compiler_params=ROOM,
        cost_estimate=flops(cost),
        name=name,
    )(*args)


def along_bands(block, distance):
    count = lax.axis_size("band")
    return lax.ppermute(block, "band", [(i, (i + distance) % count) for i in range(count)])


def swapped(block):
    count = lax.axis_size("band")
    return lax.ppermute(block, "band", [(i, i ^ 1) for i in range(count)])


def on_even():
    return lax.axis_index("band") % 2 == 0


def by_permutes():
    count = lax.axis_size("dom")
    return count <= 8 and count & (count - 1) == 0


def from_all_domains(block):
    count = lax.axis_size("dom")
    if by_permutes():
        routes = [[(i, i ^ mask) for i in range(count)] for mask in range(1, count)]
        return [block] + [lax.ppermute(block, "dom", route) for route in routes]
    whole = lax.all_gather(block, "dom")
    return [whole[d] for d in range(count)]


def domain_at(place):
    return lax.axis_index("dom") ^ place if by_permutes() else place


def tile_of(extent, most):
    return max(w for w in range(128, most + 1, 128) if extent % w == 0)


def turn_kernel(coupling_ref, out_ref):
    owned, rank = coupling_ref.shape
    whole = coupling_ref[...]
    high = whole.astype(BF16)
    unit = lax.broadcasted_iota(jnp.int32, (rank, rank), 0) == lax.broadcasted_iota(
        jnp.int32, (rank, rank), 1
    )
    unit = jnp.where(unit, 1.0, 0.0).astype(BF16)
    for i, piece in enumerate((high, (whole - high.astype(F32)).astype(BF16))):
        turned = lax.dot_general(unit, piece, NT, preferred_element_type=F32)
        out_ref[:, i * owned : (i + 1) * owned] = turned.astype(BF16)


def project_kernel(orb_ref, proj_ref, turned_ref, out_ref):
    width, points = orb_ref.shape
    out_ref[width:, : turned_ref.shape[1]] = turned_ref[...]
    tile = tile_of(points, 1024)
    total = None
    for at in range(0, points, tile):
        term = lax.dot_general(
            proj_ref[:, at : at + tile], orb_ref[:, at : at + tile], NT, preferred_element_type=F32
        )
        total = term if total is None else total + term
    out_ref[:width, :] = total.T.astype(BF16)


def project(orbitals, proj, coupling):
    width, points = orbitals.shape
    owned, rank = coupling.shape
    turned = call(
        turn_kernel, "turn", [((rank, 2 * owned), BF16)], [coupling], cost=TURN
    )[0]
    outs = [((width + rank, proj.shape[0]), BF16)]
    return call(project_kernel, "project", outs, [orbitals, proj, turned])[0]


def couple_kernel(count, slots, owned, slot_ref, *refs):
    loads = refs[:count]
    out_ref, pick, high_ref, low_ref = refs[count:]
    width, flat = out_ref.shape
    rank = flat // slots
    me = lax.axis_index("dom")
    lanes = lax.broadcasted_iota(jnp.int32, (rank, flat), 1)
    unit = lanes % rank == lax.broadcasted_iota(jnp.int32, (rank, flat), 0)
    lane_slot = lanes // rank

    atoms = jnp.zeros((rank, flat), jnp.int32)
    for k in range(slots):
        atoms = jnp.where(lane_slot == k, slot_ref[me, k], atoms)

    columns = None
    for place in range(count):
        owner = domain_at(place)
        for a in range(owned):
            hit = unit & (atoms == owner * owned + a)
            pick[a * rank : (a + 1) * rank, :] = jnp.where(hit, 1.0, 0.0).astype(BF16)
        parts = [loads[place][width:, i * owned * rank : (i + 1) * owned * rank] for i in (0, 1)]
        term = jnp.dot(jnp.concatenate(parts, 0), pick[...], preferred_element_type=F32)
        columns = term if columns is None else columns + term
    high, low = columns[:rank], columns[rank:]

    total = None
    for place in range(count):
        domain = domain_at(place)
        for k in range(slots):
            hit = atoms == slot_ref[domain, k]
            rows = slice(k * rank, (k + 1) * rank)
            high_ref[rows, :] = jnp.where(hit, high, 0.0).astype(BF16)
            low_ref[rows, :] = jnp.where(hit, low, 0.0).astype(BF16)
        block = loads[place][:width, :]
        term = jnp.dot(block, high_ref[...], preferred_element_type=F32)
        term += jnp.dot(block, low_ref[...], preferred_element_type=F32)
        total = term if total is None else total + term
    out_ref[...] = total.astype(BF16)


def match_kernel(count, slots, owned, slot_ref, *refs):
    picks, matches = refs[:count], refs[count:]
    flat = matches[0].shape[0]
    rank = flat // slots
    me = lax.axis_index("dom")
    lanes = lax.broadcasted_iota(jnp.int32, (rank, flat), 1)
    unit = lanes % rank == lax.broadcasted_iota(jnp.int32, (rank, flat), 0)
    atoms = jnp.zeros((rank, flat), jnp.int32)
    for k in range(slots):
        atoms = jnp.where(lanes // rank == k, slot_ref[me, k], atoms)
    for place in range(count):
        domain = domain_at(place)
        for a in range(owned):
            hit = unit & (atoms == domain * owned + a)
            rows = slice(a * rank, (a + 1) * rank)
            picks[place][rows, :] = jnp.where(hit, 1.0, 0.0).astype(BF16)
        for k in range(slots):
            hit = unit & (atoms == slot_ref[domain, k])
            rows = slice(k * rank, (k + 1) * rank)
            matches[place][rows, :] = jnp.where(hit, 1.0, 0.0).astype(BF16)


def match(slot_atom, owned, rank):
    count, slots = slot_atom.shape
    flat = slots * rank
    outs = [((owned * rank, flat), BF16)] * count + [((flat, flat), BF16)] * count
    kernel = functools.partial(match_kernel, count, slots, owned)
    return call(kernel, "match", outs, [slot_atom], first=SMEM)


def matched_terms(width, loads, picks, matches):
    size = picks[0].shape[0]
    columns = total = None
    for load, pick, same in zip(loads, picks, matches):
        parts = [load[width:, i * size : (i + 1) * size] for i in (0, 1)]
        rows = jnp.dot(jnp.concatenate(parts, 0), pick[...], preferred_element_type=F32)
        coefs = jnp.dot(load[:width, :], same[...], preferred_element_type=F32)
        columns = rows if columns is None else columns + rows
        total = coefs if total is None else total + coefs
    return columns, total


def partly_kernel(count, *refs):
    groups = [refs[i * count : (i + 1) * count] for i in range(3)]
    columns_ref, total_ref = refs[3 * count :]
    columns, total = matched_terms(total_ref.shape[0], *groups)
    columns_ref[...] = columns
    total_ref[...] = total


def couple_matched_kernel(load, pick, same, columns_ref, total_ref, out_ref, high_ref, low_ref):
    width, flat = out_ref.shape
    rank = load.shape[0] - width
    columns, total = matched_terms(width, [load], [pick], [same])
    columns += columns_ref[...]
    total += total_ref[...]
    lane_slot = lax.broadcasted_iota(jnp.int32, (rank, flat), 1) // rank
    for k in range(flat // rank):
        rows = slice(k * rank, (k + 1) * rank)
        high_ref[rows, :] = jnp.where(lane_slot == k, columns[:rank], 0.0).astype(BF16)
        low_ref[rows, :] = jnp.where(lane_slot == k, columns[rank:], 0.0).astype(BF16)
    high = total.astype(BF16)
    low = (total - high.astype(F32)).astype(BF16)
    terms = ((high, high_ref), (low, high_ref), (high, low_ref))
    coupled = sum(jnp.dot(x, y[...], preferred_element_type=F32) for x, y in terms)
    out_ref[...] = coupled.astype(BF16)


def couple_matched(loads, matched, width):
    count, flat = len(loads), loads[0].shape[1]
    picks, matches = matched[:count], matched[count:]
    early = [i for i in range(count) if i != 1]
    groups = [[x[i] for i in early] for x in (loads, picks, matches)]
    rank = loads[0].shape[0] - width
    outs = [((2 * rank, flat), F32), ((width, flat), F32)]
    kernel = functools.partial(partly_kernel, len(early))
    partly = call(kernel, "partly", outs, sum(groups, []))
    return call(
        couple_matched_kernel,
        "couple",
        [((width, flat), BF16)],
        [loads[1], picks[1], matches[1], *partly],
        [pltpu.VMEM((flat, flat), BF16)] * 2,
        cost=COUPLE,
    )[0]


def couple(slot_atom, loads, width, owned):
    flat = loads[0].shape[1]
    slots = slot_atom.shape[1]
    return call(
        functools.partial(couple_kernel, len(loads), slots, owned),
        "couple",
        [((width, flat), BF16)],
        [slot_atom, *loads],
        [
            pltpu.VMEM((owned * (flat // slots), flat), BF16),
            pltpu.VMEM((flat, flat), BF16),
            pltpu.VMEM((flat, flat), BF16),
        ],
        first=SMEM,
        cost=COUPLE,
    )[0]


def halves_kernel(block_ref, *refs):
    upper_ref, lower_ref = refs[-2:]
    half = upper_ref.shape[0]
    upper_ref[...] = block_ref[:half, :]
    lower_ref[...] = block_ref[half:, :]


def halves(block, after, cost=0):
    half = ((block.shape[0] // 2, block.shape[1]), block.dtype)
    return call(halves_kernel, "halves", [half, half], [block, *after], cost=cost)


def hold_kernel(upper_ref, lower_ref, after_ref, out_ref):
    rows = upper_ref.shape[0]
    out_ref[:rows, :] = upper_ref[...]
    out_ref[rows:, :] = lower_ref[: out_ref.shape[0] - rows, :]


def hold(upper, lower, rows, after):
    shape = (rows, upper.shape[1])
    return call(hold_kernel, "hold", [(shape, upper.dtype)], [upper, lower, after])[0]


def packed(coef_shape, rows):
    width, flat = coef_shape
    return [
        (slice(i * flat, (i + 1) * flat), slice(i * rows, (i + 1) * rows))
        for i in range(width // rows)
    ]


def choose_kernel(mine, mine_two, two, lower, swap_ref, held_ref):
    width = two.shape[0]
    parts = packed(mine.shape, swap_ref.shape[0] - width)
    swap_ref[:width, :] = two[...]

    @pl.when(on_even())
    def _():
        for columns, rows in parts:
            swap_ref[width:, columns] = mine[rows, :]

    @pl.when(jnp.logical_not(on_even()))
    def _():
        for columns, rows in parts:
            swap_ref[width:, columns] = mine_two[rows, :]

    held_ref[...] = lower[lower.shape[0] - held_ref.shape[0] :, :]


def choose(mine, mine_two, two, lower):
    width, points = two.shape
    part = width // 4
    outs = [((width + part, points), two.dtype), ((part, points), two.dtype)]
    return call(choose_kernel, "choose", outs, [mine, mine_two, two, lower])


def where_even(tile, even):
    here = on_even() if even else jnp.logical_not(on_even())
    return jnp.where(here, tile.astype(F32), 0.0).astype(BF16)


def gather_kernel(rot_ref, own, one, two, upper, lower, three_a, out_ref, stack):
    width, points = own.shape
    depth = stack.shape[0]
    turn = jnp.concatenate(
        [rot_ref[:, : 3 * width], where_even(rot_ref[:, 3 * width : depth], True)], axis=1
    )
    stack[:width, :] = own[...]
    stack[width : 2 * width, :] = one[...]
    stack[3 * width :, :] = three_a[...]

    @pl.when(on_even())
    def _():
        stack[2 * width : 3 * width, :] = two[...]

    @pl.when(jnp.logical_not(on_even()))
    def _():
        stack[2 * width : 2 * width + upper.shape[0], :] = upper[...]
        stack[2 * width + upper.shape[0] : 3 * width, :] = lower[...]

    tile = tile_of(points, 1024)
    for at in range(0, points, tile):
        here = slice(at, at + tile)
        out_ref[:, here] = jnp.dot(turn, stack[:, here], preferred_element_type=F32)


def gather(rotation, *blocks):
    (width, points), rows = blocks[0].shape, blocks[-1].shape[0]
    scratch = [pltpu.VMEM((3 * width + rows, points), BF16)]
    return call(
        gather_kernel, "gather", [((width, points), F32)], [rotation, *blocks], scratch, cost=GATHER
    )[0]


def apply_kernel(rot_ref, mine, swap_ref, two, three, proj_ref, after_ref, out_ref):
    width, flat = mine.shape
    points = proj_ref.shape[1]
    one = [swap_ref[width:, columns] for columns, _ in packed(mine.shape, swap_ref.shape[0] - width)]
    blocks = (mine[...], jnp.concatenate(one, axis=0), two[...], three[...])
    mixed = sum(
        jnp.dot(rot_ref[:, s * width : (s + 1) * width], block, preferred_element_type=F32)
        for s, block in enumerate(blocks)
    )
    mixed = mixed.astype(BF16)
    tile = tile_of(points, 1024)
    for at in range(0, points, tile):
        out_ref[:, at : at + tile] = jnp.dot(
            mixed, proj_ref[:, at : at + tile], preferred_element_type=F32
        )


def finish_kernel(
    rot_ref, partial_ref, swap_ref, last_ref, applied, out_hbm, out_ref, sems
):
    width, points = out_ref.shape
    rows = last_ref.shape[0]
    pieces = sems.shape[0]
    tile = points // pieces
    turn = jnp.concatenate(
        [
            where_even(rot_ref[:, 3 * width : 4 * width], False),
            where_even(rot_ref[:, 4 * width - rows : 4 * width], True),
        ],
        axis=1,
    )
    copies = []
    for i in range(pieces):
        here = slice(i * tile, (i + 1) * tile)
        last = jnp.concatenate([swap_ref[:width, here], last_ref[:, here]], axis=0)
        rotated = partial_ref[:, here] + jnp.dot(turn, last, preferred_element_type=F32)
        added = rotated.astype(BF16).astype(F32) + applied[:, here]
        out_ref[:, here] = added.astype(out_ref.dtype)
        part = (slice(None), pl.ds(i * tile, tile))
        copies.append(pltpu.make_async_copy(out_ref.at[part], out_hbm.at[part], sems.at[i]))
        copies[-1].start()
    for copy in copies:
        copy.wait()


def finish(*args):
    width, points = args[-1].shape
    pieces = points // tile_of(points, 1024)
    return pl.pallas_call(
        finish_kernel,
        in_specs=[VMEM] * len(args),
        out_specs=pl.BlockSpec(memory_space=pl.ANY),
        out_shape=jax.ShapeDtypeStruct((width, points), BF16),
        scratch_shapes=[pltpu.VMEM((width, points), BF16), pltpu.SemaphoreType.DMA((pieces,))],
        compiler_params=ROOM,
        cost_estimate=flops(0),
        name="finish",
    )(*args)


def on_device(orbitals, rotation, projectors, coupling, slot_atom):
    width, points = orbitals.shape
    slot_count, rank, _ = projectors.shape
    owned = coupling.shape[0]
    proj = projectors.reshape(slot_count * rank, points)

    one = along_bands(orbitals, 1)
    upper, lower = [swapped(block) for block in halves(orbitals, [], CUT)]
    two = along_bands(hold(upper, lower, width, upper), 1)
    loads = from_all_domains(project(orbitals, proj, coupling.reshape(owned * rank, rank)))
    matched = list(match(slot_atom, owned, rank)) if by_permutes() else []
    upper, lower = [swapped(block) for block in halves(one, loads[-1:] + matched[:1])]
    if by_permutes():
        mine = couple_matched(loads, matched, width)
    else:
        mine = couple(slot_atom, loads, width, owned)
    mine_two = along_bands(mine, 2)
    three_a = along_bands(hold(upper, lower, width * 3 // 4, mine), 1)
    swap, held = choose(mine, mine_two, two, lower)
    mine_three = along_bands(mine_two, 1)
    three_b = along_bands(held, 1)
    swap = swapped(swap)
    partial = gather(rotation, orbitals, one, two, upper, lower, three_a)
    applied = call(
        apply_kernel,
        "apply",
        [((width, points), F32)],
        [rotation, mine, swap, mine_two, mine_three, proj, partial],
        cost=APPLY,
    )[0]
    return finish(rotation, partial, swap, three_b, applied)


def solution(mesh):
    in_specs = (P("band", "dom"), P("band", None), P(None, None, "dom"), P("dom", None, None), P())
    out_specs = P("band", "dom")
    return jax.shard_map(
        on_device, mesh=mesh, in_specs=in_specs, out_specs=out_specs, check_vma=False
    )
```

```python
import functools

import jax
import jax.numpy as jnp
from jax import lax
from jax.experimental import pallas as pl
from jax.experimental.pallas import tpu as pltpu
from jax.sharding import PartitionSpec as P

TURN = 0 * 10**9
CUT = 30 * 10**8
COUPLE = 4 * 10**9
APPLY = 50 * 10**8
GATHER = 45 * 10**8

F32 = jnp.float32
BF16 = jnp.bfloat16
ROOM = pltpu.CompilerParams(vmem_limit_bytes=8 * 2**20)
NT = (((1,), (1,)), ((), ()))
VMEM = pl.BlockSpec(memory_space=pltpu.VMEM)
SMEM = pl.BlockSpec(memory_space=pltpu.SMEM)


def flops(count):
    return pl.CostEstimate(flops=count, bytes_accessed=0, transcendentals=0)


def call(kernel, name, outs, args, scratch=(), first=VMEM, cost=0):
    shapes = [jax.ShapeDtypeStruct(*o) for o in outs]
    return pl.pallas_call(
        kernel,
        in_specs=[first] + [VMEM] * (len(args) - 1),
        out_specs=[VMEM] * len(outs),
        out_shape=shapes,
        scratch_shapes=list(scratch),
        compiler_params=ROOM,
        cost_estimate=flops(cost),
        name=name,
    )(*args)


def along_bands(block, distance):
    count = lax.axis_size("band")
    return lax.ppermute(block, "band", [(i, (i + distance) % count) for i in range(count)])


def swapped(block):
    count = lax.axis_size("band")
    return lax.ppermute(block, "band", [(i, i ^ 1) for i in range(count)])


def on_even():
    return lax.axis_index("band") % 2 == 0


def by_permutes():
    count = lax.axis_size("dom")
    return count <= 8 and count & (count - 1) == 0


def from_all_domains(block):
    count = lax.axis_size("dom")
    if by_permutes():
        routes = [[(i, i ^ mask) for i in range(count)] for mask in range(1, count)]
        return [block] + [lax.ppermute(block, "dom", route) for route in routes]
    whole = lax.all_gather(block, "dom")
    return [whole[d] for d in range(count)]


def domain_at(place):
    return lax.axis_index("dom") ^ place if by_permutes() else place


def tile_of(extent, most):
    return max(w for w in range(128, most + 1, 128) if extent % w == 0)


def turn_kernel(coupling_ref, out_ref):
    owned, rank = coupling_ref.shape
    whole = coupling_ref[...]
    high = whole.astype(BF16)
    unit = lax.broadcasted_iota(jnp.int32, (rank, rank), 0) == lax.broadcasted_iota(
        jnp.int32, (rank, rank), 1
    )
    unit = jnp.where(unit, 1.0, 0.0).astype(BF16)
    for i, piece in enumerate((high, (whole - high.astype(F32)).astype(BF16))):
        turned = lax.dot_general(unit, piece, NT, preferred_element_type=F32)
        out_ref[:, i * owned : (i + 1) * owned] = turned.astype(BF16)


def project_kernel(orb_ref, proj_ref, turned_ref, out_ref):
    width, points = orb_ref.shape
    out_ref[width:, : turned_ref.shape[1]] = turned_ref[...]
    tile = tile_of(points, 1024)
    total = None
    for at in range(0, points, tile):
        term = lax.dot_general(
            proj_ref[:, at : at + tile], orb_ref[:, at : at + tile], NT, preferred_element_type=F32
        )
        total = term if total is None else total + term
    out_ref[:width, :] = total.T.astype(BF16)


def project(orbitals, proj, coupling):
    width, points = orbitals.shape
    owned, rank = coupling.shape
    turned = call(
        turn_kernel, "turn", [((rank, 2 * owned), BF16)], [coupling], cost=TURN
    )[0]
    outs = [((width + rank, proj.shape[0]), BF16)]
    return call(project_kernel, "project", outs, [orbitals, proj, turned])[0]


def couple_kernel(count, slots, owned, slot_ref, *refs):
    loads = refs[:count]
    out_ref, pick, high_ref, low_ref = refs[count:]
    width, flat = out_ref.shape
    rank = flat // slots
    me = lax.axis_index("dom")
    lanes = lax.broadcasted_iota(jnp.int32, (rank, flat), 1)
    unit = lanes % rank == lax.broadcasted_iota(jnp.int32, (rank, flat), 0)
    lane_slot = lanes // rank

    atoms = jnp.zeros((rank, flat), jnp.int32)
    for k in range(slots):
        atoms = jnp.where(lane_slot == k, slot_ref[me, k], atoms)

    columns = None
    for place in range(count):
        owner = domain_at(place)
        for a in range(owned):
            hit = unit & (atoms == owner * owned + a)
            pick[a * rank : (a + 1) * rank, :] = jnp.where(hit, 1.0, 0.0).astype(BF16)
        parts = [loads[place][width:, i * owned * rank : (i + 1) * owned * rank] for i in (0, 1)]
        term = jnp.dot(jnp.concatenate(parts, 0), pick[...], preferred_element_type=F32)
        columns = term if columns is None else columns + term
    high, low = columns[:rank], columns[rank:]

    total = None
    for place in range(count):
        domain = domain_at(place)
        for k in range(slots):
            hit = atoms == slot_ref[domain, k]
            rows = slice(k * rank, (k + 1) * rank)
            high_ref[rows, :] = jnp.where(hit, high, 0.0).astype(BF16)
            low_ref[rows, :] = jnp.where(hit, low, 0.0).astype(BF16)
        block = loads[place][:width, :]
        term = jnp.dot(block, high_ref[...], preferred_element_type=F32)
        term += jnp.dot(block, low_ref[...], preferred_element_type=F32)
        total = term if total is None else total + term
    out_ref[...] = total.astype(BF16)


def match_kernel(count, slots, owned, slot_ref, *refs):
    picks, matches = refs[:count], refs[count:]
    flat = matches[0].shape[0]
    rank = flat // slots
    me = lax.axis_index("dom")
    lanes = lax.broadcasted_iota(jnp.int32, (rank, flat), 1)
    unit = lanes % rank == lax.broadcasted_iota(jnp.int32, (rank, flat), 0)
    atoms = jnp.zeros((rank, flat), jnp.int32)
    for k in range(slots):
        atoms = jnp.where(lanes // rank == k, slot_ref[me, k], atoms)
    for place in range(count):
        domain = domain_at(place)
        for a in range(owned):
            hit = unit & (atoms == domain * owned + a)
            rows = slice(a * rank, (a + 1) * rank)
            picks[place][rows, :] = jnp.where(hit, 1.0, 0.0).astype(BF16)
        for k in range(slots):
            hit = unit & (atoms == slot_ref[domain, k])
            rows = slice(k * rank, (k + 1) * rank)
            matches[place][rows, :] = jnp.where(hit, 1.0, 0.0).astype(BF16)


def match(slot_atom, owned, rank):
    count, slots = slot_atom.shape
    flat = slots * rank
    outs = [((owned * rank, flat), BF16)] * count + [((flat, flat), BF16)] * count
    kernel = functools.partial(match_kernel, count, slots, owned)
    return call(kernel, "match", outs, [slot_atom], first=SMEM)


def matched_terms(width, loads, picks, matches):
    size = picks[0].shape[0]
    columns = total = None
    for load, pick, same in zip(loads, picks, matches):
        parts = [load[width:, i * size : (i + 1) * size] for i in (0, 1)]
        rows = jnp.dot(jnp.concatenate(parts, 0), pick[...], preferred_element_type=F32)
        coefs = jnp.dot(load[:width, :], same[...], preferred_element_type=F32)
        columns = rows if columns is None else columns + rows
        total = coefs if total is None else total + coefs
    return columns, total


def partly_kernel(count, *refs):
    groups = [refs[i * count : (i + 1) * count] for i in range(3)]
    columns_ref, total_ref = refs[3 * count :]
    columns, total = matched_terms(total_ref.shape[0], *groups)
    columns_ref[...] = columns
    total_ref[...] = total


def couple_matched_kernel(count, *refs):
    groups = [refs[i * count : (i + 1) * count] for i in range(3)]
    columns_ref, total_ref, out_ref, high_ref, low_ref = refs[3 * count :]
    width, flat = out_ref.shape
    columns, total = matched_terms(width, *groups)
    columns += columns_ref[...]
    total += total_ref[...]
    rank = columns.shape[0] // 2
    lane_slot = lax.broadcasted_iota(jnp.int32, (rank, flat), 1) // rank
    for k in range(flat // rank):
        rows = slice(k * rank, (k + 1) * rank)
        high_ref[rows, :] = jnp.where(lane_slot == k, columns[:rank], 0.0).astype(BF16)
        low_ref[rows, :] = jnp.where(lane_slot == k, columns[rank:], 0.0).astype(BF16)
    high = total.astype(BF16)
    low = (total - high.astype(F32)).astype(BF16)
    terms = ((high, high_ref), (low, high_ref), (high, low_ref))
    coupled = sum(jnp.dot(x, y[...], preferred_element_type=F32) for x, y in terms)
    out_ref[...] = coupled.astype(BF16)


def couple_matched(loads, matched, width):
    count, flat = len(loads), loads[0].shape[1]
    lists = (loads, matched[:count], matched[count:])
    early = sum([[x[0], x[-1]] for x in lists], [])
    late = sum([x[1:-1] for x in lists], [])
    rank = loads[0].shape[0] - width
    outs = [((2 * rank, flat), F32), ((width, flat), F32)]
    partly = call(functools.partial(partly_kernel, 2), "partly", outs, early)
    return call(
        functools.partial(couple_matched_kernel, count - 2),
        "couple",
        [((width, flat), BF16)],
        [*late, *partly],
        [pltpu.VMEM((flat, flat), BF16)] * 2,
        cost=COUPLE,
    )[0]


def couple(slot_atom, loads, width, owned):
    flat = loads[0].shape[1]
    slots = slot_atom.shape[1]
    return call(
        functools.partial(couple_kernel, len(loads), slots, owned),
        "couple",
        [((width, flat), BF16)],
        [slot_atom, *loads],
        [
            pltpu.VMEM((owned * (flat // slots), flat), BF16),
            pltpu.VMEM((flat, flat), BF16),
            pltpu.VMEM((flat, flat), BF16),
        ],
        first=SMEM,
        cost=COUPLE,
    )[0]


def halves_kernel(block_ref, *refs):
    upper_ref, lower_ref = refs[-2:]
    half = upper_ref.shape[0]
    upper_ref[...] = block_ref[:half, :]
    lower_ref[...] = block_ref[half:, :]


def halves(block, after, cost=0):
    half = ((block.shape[0] // 2, block.shape[1]), block.dtype)
    return call(halves_kernel, "halves", [half, half], [block, *after], cost=cost)


def hold_kernel(upper_ref, lower_ref, after_ref, out_ref):
    rows = upper_ref.shape[0]
    out_ref[:rows, :] = upper_ref[...]
    out_ref[rows:, :] = lower_ref[: out_ref.shape[0] - rows, :]


def hold(upper, lower, rows, after):
    shape = (rows, upper.shape[1])
    return call(hold_kernel, "hold", [(shape, upper.dtype)], [upper, lower, after])[0]


def packed(coef_shape, rows):
    width, flat = coef_shape
    return [
        (slice(i * flat, (i + 1) * flat), slice(i * rows, (i + 1) * rows))
        for i in range(width // rows)
    ]


def choose_kernel(mine, mine_two, two, lower, swap_ref, held_ref):
    width = two.shape[0]
    parts = packed(mine.shape, swap_ref.shape[0] - width)
    swap_ref[:width, :] = two[...]

    @pl.when(on_even())
    def _():
        for columns, rows in parts:
            swap_ref[width:, columns] = mine[rows, :]

    @pl.when(jnp.logical_not(on_even()))
    def _():
        for columns, rows in parts:
            swap_ref[width:, columns] = mine_two[rows, :]

    held_ref[...] = lower[lower.shape[0] - held_ref.shape[0] :, :]


def choose(mine, mine_two, two, lower):
    width, points = two.shape
    part = width // 4
    outs = [((width + part, points), two.dtype), ((part, points), two.dtype)]
    return call(choose_kernel, "choose", outs, [mine, mine_two, two, lower])


def where_even(tile, even):
    here = on_even() if even else jnp.logical_not(on_even())
    return jnp.where(here, tile.astype(F32), 0.0).astype(BF16)


def gather_kernel(rot_ref, own, one, two, upper, lower, three_a, out_ref, stack):
    width, points = own.shape
    depth = stack.shape[0]
    turn = jnp.concatenate(
        [rot_ref[:, : 3 * width], where_even(rot_ref[:, 3 * width : depth], True)], axis=1
    )
    stack[:width, :] = own[...]
    stack[width : 2 * width, :] = one[...]
    stack[3 * width :, :] = three_a[...]

    @pl.when(on_even())
    def _():
        stack[2 * width : 3 * width, :] = two[...]

    @pl.when(jnp.logical_not(on_even()))
    def _():
        stack[2 * width : 2 * width + upper.shape[0], :] = upper[...]
        stack[2 * width + upper.shape[0] : 3 * width, :] = lower[...]

    tile = tile_of(points, 1024)
    for at in range(0, points, tile):
        here = slice(at, at + tile)
        out_ref[:, here] = jnp.dot(turn, stack[:, here], preferred_element_type=F32)


def gather(rotation, *blocks):
    (width, points), rows = blocks[0].shape, blocks[-1].shape[0]
    scratch = [pltpu.VMEM((3 * width + rows, points), BF16)]
    return call(
        gather_kernel, "gather", [((width, points), F32)], [rotation, *blocks], scratch, cost=GATHER
    )[0]


def apply_kernel(rot_ref, mine, swap_ref, two, three, proj_ref, after_ref, out_ref):
    width, flat = mine.shape
    points = proj_ref.shape[1]
    one = [swap_ref[width:, columns] for columns, _ in packed(mine.shape, swap_ref.shape[0] - width)]
    blocks = (mine[...], jnp.concatenate(one, axis=0), two[...], three[...])
    mixed = sum(
        jnp.dot(rot_ref[:, s * width : (s + 1) * width], block, preferred_element_type=F32)
        for s, block in enumerate(blocks)
    )
    mixed = mixed.astype(BF16)
    tile = tile_of(points, 1024)
    for at in range(0, points, tile):
        out_ref[:, at : at + tile] = jnp.dot(
            mixed, proj_ref[:, at : at + tile], preferred_element_type=F32
        )


def finish_kernel(
    rot_ref, partial_ref, swap_ref, last_ref, applied, out_hbm, out_ref, sems
):
    width, points = out_ref.shape
    rows = last_ref.shape[0]
    pieces = sems.shape[0]
    tile = points // pieces
    turn = jnp.concatenate(
        [
            where_even(rot_ref[:, 3 * width : 4 * width], False),
            where_even(rot_ref[:, 4 * width - rows : 4 * width], True),
        ],
        axis=1,
    )
    copies = []
    for i in range(pieces):
        here = slice(i * tile, (i + 1) * tile)
        last = jnp.concatenate([swap_ref[:width, here], last_ref[:, here]], axis=0)
        rotated = partial_ref[:, here] + jnp.dot(turn, last, preferred_element_type=F32)
        added = rotated.astype(BF16).astype(F32) + applied[:, here]
        out_ref[:, here] = added.astype(out_ref.dtype)
        part = (slice(None), pl.ds(i * tile, tile))
        copies.append(pltpu.make_async_copy(out_ref.at[part], out_hbm.at[part], sems.at[i]))
        copies[-1].start()
    for copy in copies:
        copy.wait()


def finish(*args):
    width, points = args[-1].shape
    pieces = points // tile_of(points, 1024)
    return pl.pallas_call(
        finish_kernel,
        in_specs=[VMEM] * len(args),
        out_specs=pl.BlockSpec(memory_space=pl.ANY),
        out_shape=jax.ShapeDtypeStruct((width, points), BF16),
        scratch_shapes=[pltpu.VMEM((width, points), BF16), pltpu.SemaphoreType.DMA((pieces,))],
        compiler_params=ROOM,
        cost_estimate=flops(0),
        name="finish",
    )(*args)


def on_device(orbitals, rotation, projectors, coupling, slot_atom):
    width, points = orbitals.shape
    slot_count, rank, _ = projectors.shape
    owned = coupling.shape[0]
    proj = projectors.reshape(slot_count * rank, points)

    one = along_bands(orbitals, 1)
    upper, lower = [swapped(block) for block in halves(orbitals, [], CUT)]
    two = along_bands(hold(upper, lower, width, upper), 1)
    loads = from_all_domains(project(orbitals, proj, coupling.reshape(owned * rank, rank)))
    matched = list(match(slot_atom, owned, rank)) if by_permutes() else []
    upper, lower = [swapped(block) for block in halves(one, loads[-1:] + matched[:1])]
    if by_permutes():
        mine = couple_matched(loads, matched, width)
    else:
        mine = couple(slot_atom, loads, width, owned)
    mine_two = along_bands(mine, 2)
    three_a = along_bands(hold(upper, lower, width * 3 // 4, mine), 1)
    swap, held = choose(mine, mine_two, two, lower)
    mine_three = along_bands(mine_two, 1)
    three_b = along_bands(held, 1)
    swap = swapped(swap)
    partial = gather(rotation, orbitals, one, two, upper, lower, three_a)
    applied = call(
        apply_kernel,
        "apply",
        [((width, points), F32)],
        [rotation, mine, swap, mine_two, mine_three, proj, partial],
        cost=APPLY,
    )[0]
    return finish(rotation, partial, swap, three_b, applied)


def solution(mesh):
    in_specs = (P("band", "dom"), P("band", None), P(None, None, "dom"), P("dom", None, None), P())
    out_specs = P("band", "dom")
    return jax.shard_map(
        on_device, mesh=mesh, in_specs=in_specs, out_specs=out_specs, check_vma=False
    )
```

```python
import functools

import jax
import jax.numpy as jnp
from jax import lax
from jax.experimental import pallas as pl
from jax.experimental.pallas import tpu as pltpu
from jax.sharding import PartitionSpec as P

TURN = 0 * 10**9
CUT = 30 * 10**8
COUPLE = 4 * 10**9
APPLY = 50 * 10**8
GATHER = 45 * 10**8

F32 = jnp.float32
BF16 = jnp.bfloat16
ROOM = pltpu.CompilerParams(vmem_limit_bytes=8 * 2**20)
NT = (((1,), (1,)), ((), ()))
VMEM = pl.BlockSpec(memory_space=pltpu.VMEM)
SMEM = pl.BlockSpec(memory_space=pltpu.SMEM)


def flops(count):
    return pl.CostEstimate(flops=count, bytes_accessed=0, transcendentals=0)


def call(kernel, name, outs, args, scratch=(), first=VMEM, cost=0):
    shapes = [jax.ShapeDtypeStruct(*o) for o in outs]
    return pl.pallas_call(
        kernel,
        in_specs=[first] + [VMEM] * (len(args) - 1),
        out_specs=[VMEM] * len(outs),
        out_shape=shapes,
        scratch_shapes=list(scratch),
        compiler_params=ROOM,
        cost_estimate=flops(cost),
        name=name,
    )(*args)


def along_bands(block, distance):
    count = lax.axis_size("band")
    return lax.ppermute(block, "band", [(i, (i + distance) % count) for i in range(count)])


def swapped(block):
    count = lax.axis_size("band")
    return lax.ppermute(block, "band", [(i, i ^ 1) for i in range(count)])


def on_even():
    return lax.axis_index("band") % 2 == 0


def by_permutes():
    count = lax.axis_size("dom")
    return count <= 8 and count & (count - 1) == 0


def from_all_domains(block):
    count = lax.axis_size("dom")
    if by_permutes():
        routes = [[(i, i ^ mask) for i in range(count)] for mask in range(1, count)]
        return [block] + [lax.ppermute(block, "dom", route) for route in routes]
    whole = lax.all_gather(block, "dom")
    return [whole[d] for d in range(count)]


def domain_at(place):
    return lax.axis_index("dom") ^ place if by_permutes() else place


def tile_of(extent, most):
    return max(w for w in range(128, most + 1, 128) if extent % w == 0)


def turn_kernel(coupling_ref, out_ref):
    owned, rank = coupling_ref.shape
    whole = coupling_ref[...]
    high = whole.astype(BF16)
    unit = lax.broadcasted_iota(jnp.int32, (rank, rank), 0) == lax.broadcasted_iota(
        jnp.int32, (rank, rank), 1
    )
    unit = jnp.where(unit, 1.0, 0.0).astype(BF16)
    for i, piece in enumerate((high, (whole - high.astype(F32)).astype(BF16))):
        turned = lax.dot_general(unit, piece, NT, preferred_element_type=F32)
        out_ref[:, i * owned : (i + 1) * owned] = turned.astype(BF16)


def project_kernel(orb_ref, proj_ref, turned_ref, out_ref):
    width, points = orb_ref.shape
    out_ref[width:, : turned_ref.shape[1]] = turned_ref[...]
    tile = tile_of(points, 1024)
    total = None
    for at in range(0, points, tile):
        term = lax.dot_general(
            proj_ref[:, at : at + tile], orb_ref[:, at : at + tile], NT, preferred_element_type=F32
        )
        total = term if total is None else total + term
    out_ref[:width, :] = total.T.astype(BF16)


def project(orbitals, proj, coupling):
    width, points = orbitals.shape
    owned, rank = coupling.shape
    turned = call(
        turn_kernel, "turn", [((rank, 2 * owned), BF16)], [coupling], cost=TURN
    )[0]
    outs = [((width + rank, proj.shape[0]), BF16)]
    return call(project_kernel, "project", outs, [orbitals, proj, turned])[0]


def couple_kernel(count, slots, owned, slot_ref, *refs):
    loads = refs[:count]
    out_ref, pick, high_ref, low_ref = refs[count:]
    width, flat = out_ref.shape
    rank = flat // slots
    me = lax.axis_index("dom")
    lanes = lax.broadcasted_iota(jnp.int32, (rank, flat), 1)
    unit = lanes % rank == lax.broadcasted_iota(jnp.int32, (rank, flat), 0)
    lane_slot = lanes // rank

    atoms = jnp.zeros((rank, flat), jnp.int32)
    for k in range(slots):
        atoms = jnp.where(lane_slot == k, slot_ref[me, k], atoms)

    columns = None
    for place in range(count):
        owner = domain_at(place)
        for a in range(owned):
            hit = unit & (atoms == owner * owned + a)
            pick[a * rank : (a + 1) * rank, :] = jnp.where(hit, 1.0, 0.0).astype(BF16)
        parts = [loads[place][width:, i * owned * rank : (i + 1) * owned * rank] for i in (0, 1)]
        term = jnp.dot(jnp.concatenate(parts, 0), pick[...], preferred_element_type=F32)
        columns = term if columns is None else columns + term
    high, low = columns[:rank], columns[rank:]

    total = None
    for place in range(count):
        domain = domain_at(place)
        for k in range(slots):
            hit = atoms == slot_ref[domain, k]
            rows = slice(k * rank, (k + 1) * rank)
            high_ref[rows, :] = jnp.where(hit, high, 0.0).astype(BF16)
            low_ref[rows, :] = jnp.where(hit, low, 0.0).astype(BF16)
        block = loads[place][:width, :]
        term = jnp.dot(block, high_ref[...], preferred_element_type=F32)
        term += jnp.dot(block, low_ref[...], preferred_element_type=F32)
        total = term if total is None else total + term
    out_ref[...] = total.astype(BF16)


def match_kernel(count, slots, owned, slot_ref, *refs):
    picks, matches = refs[:count], refs[count:]
    flat = matches[0].shape[0]
    rank = flat // slots
    me = lax.axis_index("dom")
    lanes = lax.broadcasted_iota(jnp.int32, (rank, flat), 1)
    unit = lanes % rank == lax.broadcasted_iota(jnp.int32, (rank, flat), 0)
    atoms = jnp.zeros((rank, flat), jnp.int32)
    for k in range(slots):
        atoms = jnp.where(lanes // rank == k, slot_ref[me, k], atoms)
    for place in range(count):
        domain = domain_at(place)
        for a in range(owned):
            hit = unit & (atoms == domain * owned + a)
            rows = slice(a * rank, (a + 1) * rank)
            picks[place][rows, :] = jnp.where(hit, 1.0, 0.0).astype(BF16)
        for k in range(slots):
            hit = unit & (atoms == slot_ref[domain, k])
            rows = slice(k * rank, (k + 1) * rank)
            matches[place][rows, :] = jnp.where(hit, 1.0, 0.0).astype(BF16)


def match(slot_atom, owned, rank):
    count, slots = slot_atom.shape
    flat = slots * rank
    outs = [((owned * rank, flat), BF16)] * count + [((flat, flat), BF16)] * count
    kernel = functools.partial(match_kernel, count, slots, owned)
    return call(kernel, "match", outs, [slot_atom], first=SMEM)


def matched_terms(width, loads, picks, matches):
    size = picks[0].shape[0]
    columns = total = None
    for load, pick, same in zip(loads, picks, matches):
        parts = [load[width:, i * size : (i + 1) * size] for i in (0, 1)]
        rows = jnp.dot(jnp.concatenate(parts, 0), pick[...], preferred_element_type=F32)
        coefs = jnp.dot(load[:width, :], same[...], preferred_element_type=F32)
        columns = rows if columns is None else columns + rows
        total = coefs if total is None else total + coefs
    return columns, total


def partly_kernel(count, *refs):
    groups = [refs[i * count : (i + 1) * count] for i in range(3)]
    columns_ref, total_ref = refs[3 * count :]
    columns, total = matched_terms(total_ref.shape[0], *groups)
    columns_ref[...] = columns
    total_ref[...] = total


def couple_matched_kernel(count, *refs):
    groups = [refs[i * count : (i + 1) * count] for i in range(3)]
    columns_ref, total_ref, out_ref, high_ref, low_ref = refs[3 * count :]
    width, flat = out_ref.shape
    columns, total = matched_terms(width, *groups)
    columns += columns_ref[...]
    total += total_ref[...]
    rank = columns.shape[0] // 2
    lane_slot = lax.broadcasted_iota(jnp.int32, (rank, flat), 1) // rank
    for k in range(flat // rank):
        rows = slice(k * rank, (k + 1) * rank)
        high_ref[rows, :] = jnp.where(lane_slot == k, columns[:rank], 0.0).astype(BF16)
        low_ref[rows, :] = jnp.where(lane_slot == k, columns[rank:], 0.0).astype(BF16)
    high = total.astype(BF16)
    low = (total - high.astype(F32)).astype(BF16)
    terms = ((high, high_ref), (low, high_ref), (high, low_ref))
    coupled = sum(jnp.dot(x, y[...], preferred_element_type=F32) for x, y in terms)
    out_ref[...] = coupled.astype(BF16)


def couple_matched(loads, matched, width):
    count, flat = len(loads), loads[0].shape[1]
    lists = (loads, matched[:count], matched[count:])
    early = sum([[x[0], x[-1]] for x in lists], [])
    late = sum([x[1:-1] for x in lists], [])
    rank = loads[0].shape[0] - width
    outs = [((2 * rank, flat), F32), ((width, flat), F32)]
    partly = call(functools.partial(partly_kernel, 2), "partly", outs, early)
    return call(
        functools.partial(couple_matched_kernel, count - 2),
        "couple",
        [((width, flat), BF16)],
        [*late, *partly],
        [pltpu.VMEM((flat, flat), BF16)] * 2,
        cost=COUPLE,
    )[0]


def couple(slot_atom, loads, width, owned):
    flat = loads[0].shape[1]
    slots = slot_atom.shape[1]
    return call(
        functools.partial(couple_kernel, len(loads), slots, owned),
        "couple",
        [((width, flat), BF16)],
        [slot_atom, *loads],
        [
            pltpu.VMEM((owned * (flat // slots), flat), BF16),
            pltpu.VMEM((flat, flat), BF16),
            pltpu.VMEM((flat, flat), BF16),
        ],
        first=SMEM,
        cost=COUPLE,
    )[0]


def halves_kernel(block_ref, *refs):
    upper_ref, lower_ref = refs[-2:]
    half = upper_ref.shape[0]
    upper_ref[...] = block_ref[:half, :]
    lower_ref[...] = block_ref[half:, :]


def halves(block, after, cost=0):
    half = ((block.shape[0] // 2, block.shape[1]), block.dtype)
    return call(halves_kernel, "halves", [half, half], [block, *after], cost=cost)


def hold_kernel(upper_ref, lower_ref, after_ref, out_ref):
    rows = upper_ref.shape[0]
    out_ref[:rows, :] = upper_ref[...]
    out_ref[rows:, :] = lower_ref[: out_ref.shape[0] - rows, :]


def hold(upper, lower, rows, after):
    shape = (rows, upper.shape[1])
    return call(hold_kernel, "hold", [(shape, upper.dtype)], [upper, lower, after])[0]


def packed(coef_shape, rows):
    width, flat = coef_shape
    return [
        (slice(i * flat, (i + 1) * flat), slice(i * rows, (i + 1) * rows))
        for i in range(width // rows)
    ]


def choose_kernel(mine, mine_two, two, lower, swap_ref, held_ref):
    width = two.shape[0]
    parts = packed(mine.shape, swap_ref.shape[0] - width)
    swap_ref[:width, :] = two[...]

    @pl.when(on_even())
    def _():
        for columns, rows in parts:
            swap_ref[width:, columns] = mine[rows, :]

    @pl.when(jnp.logical_not(on_even()))
    def _():
        for columns, rows in parts:
            swap_ref[width:, columns] = mine_two[rows, :]

    held_ref[...] = lower[lower.shape[0] - held_ref.shape[0] :, :]


def choose(mine, mine_two, two, lower):
    width, points = two.shape
    part = width // 4
    outs = [((width + part, points), two.dtype), ((part, points), two.dtype)]
    return call(choose_kernel, "choose", outs, [mine, mine_two, two, lower])


def where_even(tile, even):
    here = on_even() if even else jnp.logical_not(on_even())
    return jnp.where(here, tile.astype(F32), 0.0).astype(BF16)


def gather_kernel(rot_ref, own, one, two, upper, lower, three_a, out_ref, stack):
    width, points = own.shape
    depth = stack.shape[0]
    turn = jnp.concatenate(
        [rot_ref[:, : 3 * width], where_even(rot_ref[:, 3 * width : depth], True)], axis=1
    )
    stack[:width, :] = own[...]
    stack[width : 2 * width, :] = one[...]
    stack[3 * width :, :] = three_a[...]

    @pl.when(on_even())
    def _():
        stack[2 * width : 3 * width, :] = two[...]

    @pl.when(jnp.logical_not(on_even()))
    def _():
        stack[2 * width : 2 * width + upper.shape[0], :] = upper[...]
        stack[2 * width + upper.shape[0] : 3 * width, :] = lower[...]

    tile = tile_of(points, 1024)
    for at in range(0, points, tile):
        here = slice(at, at + tile)
        out_ref[:, here] = jnp.dot(turn, stack[:, here], preferred_element_type=F32)


def gather(rotation, *blocks):
    (width, points), rows = blocks[0].shape, blocks[-1].shape[0]
    scratch = [pltpu.VMEM((3 * width + rows, points), BF16)]
    return call(
        gather_kernel, "gather", [((width, points), F32)], [rotation, *blocks], scratch, cost=GATHER
    )[0]


def apply_kernel(rot_ref, mine, swap_ref, two, three, proj_ref, after_ref, out_ref):
    width, flat = mine.shape
    points = proj_ref.shape[1]
    one = [swap_ref[width:, columns] for columns, _ in packed(mine.shape, swap_ref.shape[0] - width)]
    blocks = (mine[...], jnp.concatenate(one, axis=0), two[...], three[...])
    mixed = sum(
        jnp.dot(rot_ref[:, s * width : (s + 1) * width], block, preferred_element_type=F32)
        for s, block in enumerate(blocks)
    )
    mixed = mixed.astype(BF16)
    tile = tile_of(points, 1024)
    for at in range(0, points, tile):
        out_ref[:, at : at + tile] = jnp.dot(
            mixed, proj_ref[:, at : at + tile], preferred_element_type=F32
        )


def add_kernel(rot_ref, partial_ref, swap_ref, applied, out_ref):
    width, points = out_ref.shape
    turn = where_even(rot_ref[:, 3 * width : 4 * width], False)
    tile = tile_of(points, 1024)
    for at in range(0, points, tile):
        here = slice(at, at + tile)
        out_ref[:, here] = partial_ref[:, here] + jnp.dot(
            turn, swap_ref[:width, here], preferred_element_type=F32
        )


def finish_kernel(rot_ref, partial_ref, last_ref, applied, out_hbm, out_ref, sems):
    width, points = out_ref.shape
    pieces = sems.shape[0]
    tile = points // pieces
    turn = where_even(rot_ref[:, 4 * width - last_ref.shape[0] : 4 * width], True)
    copies = []
    for i in range(pieces):
        here = slice(i * tile, (i + 1) * tile)
        rotated = partial_ref[:, here] + jnp.dot(
            turn, last_ref[:, here], preferred_element_type=F32
        )
        added = rotated.astype(BF16).astype(F32) + applied[:, here]
        out_ref[:, here] = added.astype(out_ref.dtype)
        part = (slice(None), pl.ds(i * tile, tile))
        copies.append(pltpu.make_async_copy(out_ref.at[part], out_hbm.at[part], sems.at[i]))
        copies[-1].start()
    for copy in copies:
        copy.wait()


def finish(*args):
    width, points = args[-1].shape
    pieces = points // tile_of(points, 1536)
    return pl.pallas_call(
        finish_kernel,
        in_specs=[VMEM] * len(args),
        out_specs=pl.BlockSpec(memory_space=pl.ANY),
        out_shape=jax.ShapeDtypeStruct((width, points), BF16),
        scratch_shapes=[pltpu.VMEM((width, points), BF16), pltpu.SemaphoreType.DMA((pieces,))],
        compiler_params=ROOM,
        cost_estimate=flops(0),
        name="finish",
    )(*args)


def on_device(orbitals, rotation, projectors, coupling, slot_atom):
    width, points = orbitals.shape
    slot_count, rank, _ = projectors.shape
    owned = coupling.shape[0]
    proj = projectors.reshape(slot_count * rank, points)

    one = along_bands(orbitals, 1)
    upper, lower = [swapped(block) for block in halves(orbitals, [], CUT)]
    two = along_bands(hold(upper, lower, width, upper), 1)
    loads = from_all_domains(project(orbitals, proj, coupling.reshape(owned * rank, rank)))
    matched = list(match(slot_atom, owned, rank)) if by_permutes() else []
    upper, lower = [swapped(block) for block in halves(one, loads[-1:] + matched[:1])]
    if by_permutes():
        mine = couple_matched(loads, matched, width)
    else:
        mine = couple(slot_atom, loads, width, owned)
    mine_two = along_bands(mine, 2)
    three_a = along_bands(hold(upper, lower, width * 3 // 4, mine), 1)
    swap, held = choose(mine, mine_two, two, lower)
    mine_three = along_bands(mine_two, 1)
    three_b = along_bands(held, 1)
    swap = swapped(swap)
    partial = gather(rotation, orbitals, one, two, upper, lower, three_a)
    applied = call(
        apply_kernel,
        "apply",
        [((width, points), F32)],
        [rotation, mine, swap, mine_two, mine_three, proj, partial],
        cost=APPLY,
    )[0]
    outs = [(partial.shape, F32)]
    partial = call(add_kernel, "add", outs, [rotation, partial, swap, applied])[0]
    return finish(rotation, partial, three_b, applied)


def solution(mesh):
    in_specs = (P("band", "dom"), P("band", None), P(None, None, "dom"), P("dom", None, None), P())
    out_specs = P("band", "dom")
    return jax.shard_map(
        on_device, mesh=mesh, in_specs=in_specs, out_specs=out_specs, check_vma=False
    )
```

```python
import functools

import jax
import jax.numpy as jnp
from jax import lax
from jax.experimental import pallas as pl
from jax.experimental.pallas import tpu as pltpu
from jax.sharding import PartitionSpec as P

TURN = 0 * 10**9
CUT = 30 * 10**8
COUPLE = 4 * 10**9
APPLY = 50 * 10**8
GATHER = 45 * 10**8

F32 = jnp.float32
BF16 = jnp.bfloat16
ROOM = pltpu.CompilerParams(vmem_limit_bytes=8 * 2**20)
NT = (((1,), (1,)), ((), ()))
VMEM = pl.BlockSpec(memory_space=pltpu.VMEM)
SMEM = pl.BlockSpec(memory_space=pltpu.SMEM)


def flops(count):
    return pl.CostEstimate(flops=count, bytes_accessed=0, transcendentals=0)


def call(kernel, name, outs, args, scratch=(), first=VMEM, cost=0):
    shapes = [jax.ShapeDtypeStruct(*o) for o in outs]
    return pl.pallas_call(
        kernel,
        in_specs=[first] + [VMEM] * (len(args) - 1),
        out_specs=[VMEM] * len(outs),
        out_shape=shapes,
        scratch_shapes=list(scratch),
        compiler_params=ROOM,
        cost_estimate=flops(cost),
        name=name,
    )(*args)


def along_bands(block, distance):
    count = lax.axis_size("band")
    return lax.ppermute(block, "band", [(i, (i + distance) % count) for i in range(count)])


def swapped(block):
    count = lax.axis_size("band")
    return lax.ppermute(block, "band", [(i, i ^ 1) for i in range(count)])


def on_even():
    return lax.axis_index("band") % 2 == 0


def by_permutes():
    count = lax.axis_size("dom")
    return count <= 8 and count & (count - 1) == 0


def from_all_domains(block):
    count = lax.axis_size("dom")
    if by_permutes():
        routes = [[(i, i ^ mask) for i in range(count)] for mask in range(1, count)]
        return [block] + [lax.ppermute(block, "dom", route) for route in routes]
    whole = lax.all_gather(block, "dom")
    return [whole[d] for d in range(count)]


def domain_at(place):
    return lax.axis_index("dom") ^ place if by_permutes() else place


def tile_of(extent, most):
    return max(w for w in range(128, most + 1, 128) if extent % w == 0)


def turn_kernel(coupling_ref, out_ref):
    owned, rank = coupling_ref.shape
    whole = coupling_ref[...]
    high = whole.astype(BF16)
    unit = lax.broadcasted_iota(jnp.int32, (rank, rank), 0) == lax.broadcasted_iota(
        jnp.int32, (rank, rank), 1
    )
    unit = jnp.where(unit, 1.0, 0.0).astype(BF16)
    for i, piece in enumerate((high, (whole - high.astype(F32)).astype(BF16))):
        turned = lax.dot_general(unit, piece, NT, preferred_element_type=F32)
        out_ref[:, i * owned : (i + 1) * owned] = turned.astype(BF16)


def project_kernel(orb_ref, proj_ref, turned_ref, out_ref):
    width, points = orb_ref.shape
    out_ref[width:, : turned_ref.shape[1]] = turned_ref[...]
    tile = tile_of(points, 1024)
    total = None
    for at in range(0, points, tile):
        term = lax.dot_general(
            proj_ref[:, at : at + tile], orb_ref[:, at : at + tile], NT, preferred_element_type=F32
        )
        total = term if total is None else total + term
    out_ref[:width, :] = total.T.astype(BF16)


def project(orbitals, proj, coupling):
    width, points = orbitals.shape
    owned, rank = coupling.shape
    turned = call(
        turn_kernel, "turn", [((rank, 2 * owned), BF16)], [coupling], cost=TURN
    )[0]
    outs = [((width + rank, proj.shape[0]), BF16)]
    return call(project_kernel, "project", outs, [orbitals, proj, turned])[0]


def couple_kernel(count, slots, owned, slot_ref, *refs):
    loads = refs[:count]
    out_ref, pick, high_ref, low_ref = refs[count:]
    width, flat = out_ref.shape
    rank = flat // slots
    me = lax.axis_index("dom")
    lanes = lax.broadcasted_iota(jnp.int32, (rank, flat), 1)
    unit = lanes % rank == lax.broadcasted_iota(jnp.int32, (rank, flat), 0)
    lane_slot = lanes // rank

    atoms = jnp.zeros((rank, flat), jnp.int32)
    for k in range(slots):
        atoms = jnp.where(lane_slot == k, slot_ref[me, k], atoms)

    columns = None
    for place in range(count):
        owner = domain_at(place)
        for a in range(owned):
            hit = unit & (atoms == owner * owned + a)
            pick[a * rank : (a + 1) * rank, :] = jnp.where(hit, 1.0, 0.0).astype(BF16)
        parts = [loads[place][width:, i * owned * rank : (i + 1) * owned * rank] for i in (0, 1)]
        term = jnp.dot(jnp.concatenate(parts, 0), pick[...], preferred_element_type=F32)
        columns = term if columns is None else columns + term
    high, low = columns[:rank], columns[rank:]

    total = None
    for place in range(count):
        domain = domain_at(place)
        for k in range(slots):
            hit = atoms == slot_ref[domain, k]
            rows = slice(k * rank, (k + 1) * rank)
            high_ref[rows, :] = jnp.where(hit, high, 0.0).astype(BF16)
            low_ref[rows, :] = jnp.where(hit, low, 0.0).astype(BF16)
        block = loads[place][:width, :]
        term = jnp.dot(block, high_ref[...], preferred_element_type=F32)
        term += jnp.dot(block, low_ref[...], preferred_element_type=F32)
        total = term if total is None else total + term
    out_ref[...] = total.astype(BF16)


def match_kernel(count, slots, owned, slot_ref, *refs):
    picks, matches = refs[:count], refs[count:]
    flat = matches[0].shape[0]
    rank = flat // slots
    me = lax.axis_index("dom")
    lanes = lax.broadcasted_iota(jnp.int32, (rank, flat), 1)
    unit = lanes % rank == lax.broadcasted_iota(jnp.int32, (rank, flat), 0)
    atoms = jnp.zeros((rank, flat), jnp.int32)
    for k in range(slots):
        atoms = jnp.where(lanes // rank == k, slot_ref[me, k], atoms)
    for place in range(count):
        domain = domain_at(place)
        for a in range(owned):
            hit = unit & (atoms == domain * owned + a)
            rows = slice(a * rank, (a + 1) * rank)
            picks[place][rows, :] = jnp.where(hit, 1.0, 0.0).astype(BF16)
        for k in range(slots):
            hit = unit & (atoms == slot_ref[domain, k])
            rows = slice(k * rank, (k + 1) * rank)
            matches[place][rows, :] = jnp.where(hit, 1.0, 0.0).astype(BF16)


def match(slot_atom, owned, rank):
    count, slots = slot_atom.shape
    flat = slots * rank
    outs = [((owned * rank, flat), BF16)] * count + [((flat, flat), BF16)] * count
    kernel = functools.partial(match_kernel, count, slots, owned)
    return call(kernel, "match", outs, [slot_atom], first=SMEM)


def matched_terms(width, loads, picks, matches):
    size = picks[0].shape[0]
    columns = total = None
    for load, pick, same in zip(loads, picks, matches):
        parts = [load[width:, i * size : (i + 1) * size] for i in (0, 1)]
        rows = jnp.dot(jnp.concatenate(parts, 0), pick[...], preferred_element_type=F32)
        coefs = jnp.dot(load[:width, :], same[...], preferred_element_type=F32)
        columns = rows if columns is None else columns + rows
        total = coefs if total is None else total + coefs
    return columns, total


def partly_kernel(count, *refs):
    groups = [refs[i * count : (i + 1) * count] for i in range(3)]
    columns_ref, total_ref = refs[3 * count :]
    columns, total = matched_terms(total_ref.shape[0], *groups)
    columns_ref[...] = columns
    total_ref[...] = total


def couple_matched_kernel(count, *refs):
    groups = [refs[i * count : (i + 1) * count] for i in range(3)]
    columns_ref, total_ref, out_ref, high_ref, low_ref = refs[3 * count :]
    width, flat = out_ref.shape
    columns, total = matched_terms(width, *groups)
    columns += columns_ref[...]
    total += total_ref[...]
    rank = columns.shape[0] // 2
    lane_slot = lax.broadcasted_iota(jnp.int32, (rank, flat), 1) // rank
    for k in range(flat // rank):
        rows = slice(k * rank, (k + 1) * rank)
        high_ref[rows, :] = jnp.where(lane_slot == k, columns[:rank], 0.0).astype(BF16)
        low_ref[rows, :] = jnp.where(lane_slot == k, columns[rank:], 0.0).astype(BF16)
    high = total.astype(BF16)
    low = (total - high.astype(F32)).astype(BF16)
    terms = ((high, high_ref), (low, high_ref), (high, low_ref))
    coupled = sum(jnp.dot(x, y[...], preferred_element_type=F32) for x, y in terms)
    out_ref[...] = coupled.astype(BF16)


def couple_matched(loads, matched, width):
    count, flat = len(loads), loads[0].shape[1]
    lists = (loads, matched[:count], matched[count:])
    early = sum([[x[0], x[-1]] for x in lists], [])
    late = sum([x[1:-1] for x in lists], [])
    rank = loads[0].shape[0] - width
    outs = [((2 * rank, flat), F32), ((width, flat), F32)]
    partly = call(functools.partial(partly_kernel, 2), "partly", outs, early)
    return call(
        functools.partial(couple_matched_kernel, count - 2),
        "couple",
        [((width, flat), BF16)],
        [*late, *partly],
        [pltpu.VMEM((flat, flat), BF16)] * 2,
        cost=COUPLE,
    )[0]


def couple(slot_atom, loads, width, owned):
    flat = loads[0].shape[1]
    slots = slot_atom.shape[1]
    return call(
        functools.partial(couple_kernel, len(loads), slots, owned),
        "couple",
        [((width, flat), BF16)],
        [slot_atom, *loads],
        [
            pltpu.VMEM((owned * (flat // slots), flat), BF16),
            pltpu.VMEM((flat, flat), BF16),
            pltpu.VMEM((flat, flat), BF16),
        ],
        first=SMEM,
        cost=COUPLE,
    )[0]


def halves_kernel(block_ref, *refs):
    upper_ref, lower_ref = refs[-2:]
    half = upper_ref.shape[0]
    upper_ref[...] = block_ref[:half, :]
    lower_ref[...] = block_ref[half:, :]


def halves(block, after, cost=0):
    half = ((block.shape[0] // 2, block.shape[1]), block.dtype)
    return call(halves_kernel, "halves", [half, half], [block, *after], cost=cost)


def hold_kernel(upper_ref, lower_ref, after_ref, out_ref):
    rows = upper_ref.shape[0]
    out_ref[:rows, :] = upper_ref[...]
    out_ref[rows:, :] = lower_ref[: out_ref.shape[0] - rows, :]


def hold(upper, lower, rows, after):
    shape = (rows, upper.shape[1])
    return call(hold_kernel, "hold", [(shape, upper.dtype)], [upper, lower, after])[0]


def packed(coef_shape, rows):
    width, flat = coef_shape
    return [
        (slice(i * flat, (i + 1) * flat), slice(i * rows, (i + 1) * rows))
        for i in range(width // rows)
    ]


def choose_kernel(mine, mine_two, two, lower, swap_ref, held_ref):
    width = two.shape[0]
    parts = packed(mine.shape, swap_ref.shape[0] - width)
    swap_ref[:width, :] = two[...]

    @pl.when(on_even())
    def _():
        for columns, rows in parts:
            swap_ref[width:, columns] = mine[rows, :]

    @pl.when(jnp.logical_not(on_even()))
    def _():
        for columns, rows in parts:
            swap_ref[width:, columns] = mine_two[rows, :]

    held_ref[...] = lower[lower.shape[0] - held_ref.shape[0] :, :]


def choose(mine, mine_two, two, lower):
    width, points = two.shape
    part = width // 4
    outs = [((width + part, points), two.dtype), ((part, points), two.dtype)]
    return call(choose_kernel, "choose", outs, [mine, mine_two, two, lower])


def where_even(tile, even):
    here = on_even() if even else jnp.logical_not(on_even())
    return jnp.where(here, tile.astype(F32), 0.0).astype(BF16)


def gather_kernel(rot_ref, own, one, two, upper, lower, three_a, out_ref, stack):
    width, points = own.shape
    depth = stack.shape[0]
    turn = jnp.concatenate(
        [rot_ref[:, : 3 * width], where_even(rot_ref[:, 3 * width : depth], True)], axis=1
    )
    stack[:width, :] = own[...]
    stack[width : 2 * width, :] = one[...]
    stack[3 * width :, :] = three_a[...]

    @pl.when(on_even())
    def _():
        stack[2 * width : 3 * width, :] = two[...]

    @pl.when(jnp.logical_not(on_even()))
    def _():
        stack[2 * width : 2 * width + upper.shape[0], :] = upper[...]
        stack[2 * width + upper.shape[0] : 3 * width, :] = lower[...]

    tile = tile_of(points, 1024)
    for at in range(0, points, tile):
        here = slice(at, at + tile)
        out_ref[:, here] = jnp.dot(turn, stack[:, here], preferred_element_type=F32)


def gather(rotation, *blocks):
    (width, points), rows = blocks[0].shape, blocks[-1].shape[0]
    scratch = [pltpu.VMEM((3 * width + rows, points), BF16)]
    return call(
        gather_kernel, "gather", [((width, points), F32)], [rotation, *blocks], scratch, cost=GATHER
    )[0]


def apply_kernel(rot_ref, mine, swap_ref, two, three, proj_ref, after_ref, out_ref):
    width, flat = mine.shape
    points = proj_ref.shape[1]
    one = [swap_ref[width:, columns] for columns, _ in packed(mine.shape, swap_ref.shape[0] - width)]
    blocks = (mine[...], jnp.concatenate(one, axis=0), two[...], three[...])
    mixed = sum(
        jnp.dot(rot_ref[:, s * width : (s + 1) * width], block, preferred_element_type=F32)
        for s, block in enumerate(blocks)
    )
    mixed = mixed.astype(BF16)
    tile = tile_of(points, 1024)
    for at in range(0, points, tile):
        out_ref[:, at : at + tile] = jnp.dot(
            mixed, proj_ref[:, at : at + tile], preferred_element_type=F32
        )


def add_kernel(rot_ref, partial_ref, swap_ref, applied, out_ref):
    width, points = out_ref.shape
    turn = where_even(rot_ref[:, 3 * width : 4 * width], False)
    tile = tile_of(points, 1024)
    for at in range(0, points, tile):
        here = slice(at, at + tile)
        out_ref[:, here] = partial_ref[:, here] + jnp.dot(
            turn, swap_ref[:width, here], preferred_element_type=F32
        )


def finish_kernel(rot_ref, partial_ref, last_ref, applied, out_hbm, out_ref, sems):
    width, points = out_ref.shape
    pieces = sems.shape[0]
    tile = points // pieces
    turn = where_even(rot_ref[:, 4 * width - last_ref.shape[0] : 4 * width], True)
    copies = []
    for i in range(pieces):
        here = slice(i * tile, (i + 1) * tile)
        rotated = partial_ref[:, here] + jnp.dot(
            turn, last_ref[:, here], preferred_element_type=F32
        )
        added = rotated.astype(BF16).astype(F32) + applied[:, here]
        out_ref[:, here] = added.astype(out_ref.dtype)
        part = (slice(None), pl.ds(i * tile, tile))
        copies.append(pltpu.make_async_copy(out_ref.at[part], out_hbm.at[part], sems.at[i]))
        copies[-1].start()
    for copy in copies:
        copy.wait()


def finish(*args):
    width, points = args[-1].shape
    pieces = points // tile_of(points, 2048)
    return pl.pallas_call(
        finish_kernel,
        in_specs=[VMEM] * len(args),
        out_specs=pl.BlockSpec(memory_space=pl.ANY),
        out_shape=jax.ShapeDtypeStruct((width, points), BF16),
        scratch_shapes=[pltpu.VMEM((width, points), BF16), pltpu.SemaphoreType.DMA((pieces,))],
        compiler_params=ROOM,
        cost_estimate=flops(0),
        name="finish",
    )(*args)


def on_device(orbitals, rotation, projectors, coupling, slot_atom):
    width, points = orbitals.shape
    slot_count, rank, _ = projectors.shape
    owned = coupling.shape[0]
    proj = projectors.reshape(slot_count * rank, points)

    one = along_bands(orbitals, 1)
    upper, lower = [swapped(block) for block in halves(orbitals, [], CUT)]
    two = along_bands(hold(upper, lower, width, upper), 1)
    loads = from_all_domains(project(orbitals, proj, coupling.reshape(owned * rank, rank)))
    matched = list(match(slot_atom, owned, rank)) if by_permutes() else []
    upper, lower = [swapped(block) for block in halves(one, loads[-1:] + matched[:1])]
    if by_permutes():
        mine = couple_matched(loads, matched, width)
    else:
        mine = couple(slot_atom, loads, width, owned)
    mine_two = along_bands(mine, 2)
    three_a = along_bands(hold(upper, lower, width * 3 // 4, mine), 1)
    swap, held = choose(mine, mine_two, two, lower)
    mine_three = along_bands(mine_two, 1)
    three_b = along_bands(held, 1)
    swap = swapped(swap)
    partial = gather(rotation, orbitals, one, two, upper, lower, three_a)
    applied = call(
        apply_kernel,
        "apply",
        [((width, points), F32)],
        [rotation, mine, swap, mine_two, mine_three, proj, partial],
        cost=APPLY,
    )[0]
    outs = [(partial.shape, F32)]
    partial = call(add_kernel, "add", outs, [rotation, partial, swap, applied])[0]
    return finish(rotation, partial, three_b, applied)


def solution(mesh):
    in_specs = (P("band", "dom"), P("band", None), P(None, None, "dom"), P("dom", None, None), P())
    out_specs = P("band", "dom")
    return jax.shard_map(
        on_device, mesh=mesh, in_specs=in_specs, out_specs=out_specs, check_vma=False
    )
```

```python
import functools

import jax
import jax.numpy as jnp
from jax import lax
from jax.experimental import pallas as pl
from jax.experimental.pallas import tpu as pltpu
from jax.sharding import PartitionSpec as P

TURN = 0 * 10**9
CUT = 30 * 10**8
COUPLE = 4 * 10**9
APPLY = 50 * 10**8
GATHER = 45 * 10**8

F32 = jnp.float32
BF16 = jnp.bfloat16
ROOM = pltpu.CompilerParams(vmem_limit_bytes=8 * 2**20)
NT = (((1,), (1,)), ((), ()))
VMEM = pl.BlockSpec(memory_space=pltpu.VMEM)
SMEM = pl.BlockSpec(memory_space=pltpu.SMEM)


def flops(count):
    return pl.CostEstimate(flops=count, bytes_accessed=0, transcendentals=0)


def call(kernel, name, outs, args, scratch=(), first=VMEM, cost=0):
    shapes = [jax.ShapeDtypeStruct(*o) for o in outs]
    return pl.pallas_call(
        kernel,
        in_specs=[first] + [VMEM] * (len(args) - 1),
        out_specs=[VMEM] * len(outs),
        out_shape=shapes,
        scratch_shapes=list(scratch),
        compiler_params=ROOM,
        cost_estimate=flops(cost),
        name=name,
    )(*args)


def along_bands(block, distance):
    count = lax.axis_size("band")
    return lax.ppermute(block, "band", [(i, (i + distance) % count) for i in range(count)])


def swapped(block):
    count = lax.axis_size("band")
    return lax.ppermute(block, "band", [(i, i ^ 1) for i in range(count)])


def on_even():
    return lax.axis_index("band") % 2 == 0


def by_permutes():
    count = lax.axis_size("dom")
    return count <= 8 and count & (count - 1) == 0


def from_all_domains(block):
    count = lax.axis_size("dom")
    if by_permutes():
        routes = [[(i, i ^ mask) for i in range(count)] for mask in range(1, count)]
        return [block] + [lax.ppermute(block, "dom", route) for route in routes]
    whole = lax.all_gather(block, "dom")
    return [whole[d] for d in range(count)]


def domain_at(place):
    return lax.axis_index("dom") ^ place if by_permutes() else place


def tile_of(extent, most):
    return max(w for w in range(128, most + 1, 128) if extent % w == 0)


def turn_kernel(coupling_ref, out_ref):
    owned, rank = coupling_ref.shape
    whole = coupling_ref[...]
    high = whole.astype(BF16)
    unit = lax.broadcasted_iota(jnp.int32, (rank, rank), 0) == lax.broadcasted_iota(
        jnp.int32, (rank, rank), 1
    )
    unit = jnp.where(unit, 1.0, 0.0).astype(BF16)
    for i, piece in enumerate((high, (whole - high.astype(F32)).astype(BF16))):
        turned = lax.dot_general(unit, piece, NT, preferred_element_type=F32)
        out_ref[:, i * owned : (i + 1) * owned] = turned.astype(BF16)


def project_kernel(orb_ref, proj_ref, turned_ref, out_ref):
    width, points = orb_ref.shape
    out_ref[width:, : turned_ref.shape[1]] = turned_ref[...]
    tile = tile_of(points, 1024)
    total = None
    for at in range(0, points, tile):
        term = lax.dot_general(
            proj_ref[:, at : at + tile], orb_ref[:, at : at + tile], NT, preferred_element_type=F32
        )
        total = term if total is None else total + term
    out_ref[:width, :] = total.T.astype(BF16)


def project(orbitals, proj, coupling):
    width, points = orbitals.shape
    owned, rank = coupling.shape
    turned = call(
        turn_kernel, "turn", [((rank, 2 * owned), BF16)], [coupling], cost=TURN
    )[0]
    outs = [((width + rank, proj.shape[0]), BF16)]
    return call(project_kernel, "project", outs, [orbitals, proj, turned])[0]


def couple_kernel(count, slots, owned, slot_ref, *refs):
    loads = refs[:count]
    out_ref, pick, high_ref, low_ref = refs[count:]
    width, flat = out_ref.shape
    rank = flat // slots
    me = lax.axis_index("dom")
    lanes = lax.broadcasted_iota(jnp.int32, (rank, flat), 1)
    unit = lanes % rank == lax.broadcasted_iota(jnp.int32, (rank, flat), 0)
    lane_slot = lanes // rank

    atoms = jnp.zeros((rank, flat), jnp.int32)
    for k in range(slots):
        atoms = jnp.where(lane_slot == k, slot_ref[me, k], atoms)

    columns = None
    for place in range(count):
        owner = domain_at(place)
        for a in range(owned):
            hit = unit & (atoms == owner * owned + a)
            pick[a * rank : (a + 1) * rank, :] = jnp.where(hit, 1.0, 0.0).astype(BF16)
        parts = [loads[place][width:, i * owned * rank : (i + 1) * owned * rank] for i in (0, 1)]
        term = jnp.dot(jnp.concatenate(parts, 0), pick[...], preferred_element_type=F32)
        columns = term if columns is None else columns + term
    high, low = columns[:rank], columns[rank:]

    total = None
    for place in range(count):
        domain = domain_at(place)
        for k in range(slots):
            hit = atoms == slot_ref[domain, k]
            rows = slice(k * rank, (k + 1) * rank)
            high_ref[rows, :] = jnp.where(hit, high, 0.0).astype(BF16)
            low_ref[rows, :] = jnp.where(hit, low, 0.0).astype(BF16)
        block = loads[place][:width, :]
        term = jnp.dot(block, high_ref[...], preferred_element_type=F32)
        term += jnp.dot(block, low_ref[...], preferred_element_type=F32)
        total = term if total is None else total + term
    out_ref[...] = total.astype(BF16)


def match_kernel(count, slots, owned, slot_ref, *refs):
    picks, matches = refs[:count], refs[count:]
    flat = matches[0].shape[0]
    rank = flat // slots
    me = lax.axis_index("dom")
    lanes = lax.broadcasted_iota(jnp.int32, (rank, flat), 1)
    unit = lanes % rank == lax.broadcasted_iota(jnp.int32, (rank, flat), 0)
    atoms = jnp.zeros((rank, flat), jnp.int32)
    for k in range(slots):
        atoms = jnp.where(lanes // rank == k, slot_ref[me, k], atoms)
    for place in range(count):
        domain = domain_at(place)
        for a in range(owned):
            hit = unit & (atoms == domain * owned + a)
            rows = slice(a * rank, (a + 1) * rank)
            picks[place][rows, :] = jnp.where(hit, 1.0, 0.0).astype(BF16)
        for k in range(slots):
            hit = unit & (atoms == slot_ref[domain, k])
            rows = slice(k * rank, (k + 1) * rank)
            matches[place][rows, :] = jnp.where(hit, 1.0, 0.0).astype(BF16)


def match(slot_atom, owned, rank):
    count, slots = slot_atom.shape
    flat = slots * rank
    outs = [((owned * rank, flat), BF16)] * count + [((flat, flat), BF16)] * count
    kernel = functools.partial(match_kernel, count, slots, owned)
    return call(kernel, "match", outs, [slot_atom], first=SMEM)


def matched_terms(width, loads, picks, matches):
    size = picks[0].shape[0]
    columns = total = None
    for load, pick, same in zip(loads, picks, matches):
        parts = [load[width:, i * size : (i + 1) * size] for i in (0, 1)]
        rows = jnp.dot(jnp.concatenate(parts, 0), pick[...], preferred_element_type=F32)
        coefs = jnp.dot(load[:width, :], same[...], preferred_element_type=F32)
        columns = rows if columns is None else columns + rows
        total = coefs if total is None else total + coefs
    return columns, total


def partly_kernel(count, *refs):
    groups = [refs[i * count : (i + 1) * count] for i in range(3)]
    columns_ref, total_ref = refs[3 * count :]
    columns, total = matched_terms(total_ref.shape[0], *groups)
    columns_ref[...] = columns
    total_ref[...] = total


def couple_matched_kernel(count, *refs):
    groups = [refs[i * count : (i + 1) * count] for i in range(3)]
    columns_ref, total_ref, out_ref, high_ref, low_ref = refs[3 * count :]
    width, flat = out_ref.shape
    columns, total = matched_terms(width, *groups)
    columns += columns_ref[...]
    total += total_ref[...]
    rank = columns.shape[0] // 2
    lane_slot = lax.broadcasted_iota(jnp.int32, (rank, flat), 1) // rank
    for k in range(flat // rank):
        rows = slice(k * rank, (k + 1) * rank)
        high_ref[rows, :] = jnp.where(lane_slot == k, columns[:rank], 0.0).astype(BF16)
        low_ref[rows, :] = jnp.where(lane_slot == k, columns[rank:], 0.0).astype(BF16)
    high = total.astype(BF16)
    low = (total - high.astype(F32)).astype(BF16)
    terms = ((high, high_ref), (low, high_ref), (high, low_ref))
    coupled = sum(jnp.dot(x, y[...], preferred_element_type=F32) for x, y in terms)
    out_ref[...] = coupled.astype(BF16)


def couple_matched(loads, matched, width):
    count, flat = len(loads), loads[0].shape[1]
    lists = (loads, matched[:count], matched[count:])
    early = sum([[x[0], x[-1]] for x in lists], [])
    late = sum([x[1:-1] for x in lists], [])
    rank = loads[0].shape[0] - width
    outs = [((2 * rank, flat), F32), ((width, flat), F32)]
    partly = call(functools.partial(partly_kernel, 2), "partly", outs, early)
    return call(
        functools.partial(couple_matched_kernel, count - 2),
        "couple",
        [((width, flat), BF16)],
        [*late, *partly],
        [pltpu.VMEM((flat, flat), BF16)] * 2,
        cost=COUPLE,
    )[0]


def couple(slot_atom, loads, width, owned):
    flat = loads[0].shape[1]
    slots = slot_atom.shape[1]
    return call(
        functools.partial(couple_kernel, len(loads), slots, owned),
        "couple",
        [((width, flat), BF16)],
        [slot_atom, *loads],
        [
            pltpu.VMEM((owned * (flat // slots), flat), BF16),
            pltpu.VMEM((flat, flat), BF16),
            pltpu.VMEM((flat, flat), BF16),
        ],
        first=SMEM,
        cost=COUPLE,
    )[0]


def halves_kernel(block_ref, *refs):
    upper_ref, lower_ref = refs[-2:]
    half = upper_ref.shape[0]
    upper_ref[...] = block_ref[:half, :]
    lower_ref[...] = block_ref[half:, :]


def halves(block, after, cost=0):
    half = ((block.shape[0] // 2, block.shape[1]), block.dtype)
    return call(halves_kernel, "halves", [half, half], [block, *after], cost=cost)


def hold_kernel(upper_ref, lower_ref, after_ref, out_ref):
    rows = upper_ref.shape[0]
    out_ref[:rows, :] = upper_ref[...]
    out_ref[rows:, :] = lower_ref[: out_ref.shape[0] - rows, :]


def hold(upper, lower, rows, after):
    shape = (rows, upper.shape[1])
    return call(hold_kernel, "hold", [(shape, upper.dtype)], [upper, lower, after])[0]


def packed(coef_shape, rows):
    width, flat = coef_shape
    return [
        (slice(i * flat, (i + 1) * flat), slice(i * rows, (i + 1) * rows))
        for i in range(width // rows)
    ]


def choose_kernel(mine, mine_two, two, lower, swap_ref, held_ref):
    width = two.shape[0]
    parts = packed(mine.shape, swap_ref.shape[0] - width)
    swap_ref[:width, :] = two[...]

    @pl.when(on_even())
    def _():
        for columns, rows in parts:
            swap_ref[width:, columns] = mine[rows, :]

    @pl.when(jnp.logical_not(on_even()))
    def _():
        for columns, rows in parts:
            swap_ref[width:, columns] = mine_two[rows, :]

    held_ref[...] = lower[lower.shape[0] - held_ref.shape[0] :, :]


def choose(mine, mine_two, two, lower):
    width, points = two.shape
    part = width // 4
    outs = [((width + part, points), two.dtype), ((part, points), two.dtype)]
    return call(choose_kernel, "choose", outs, [mine, mine_two, two, lower])


def where_even(tile, even):
    here = on_even() if even else jnp.logical_not(on_even())
    return jnp.where(here, tile.astype(F32), 0.0).astype(BF16)


def gather_kernel(rot_ref, own, one, two, upper, lower, three_a, out_ref, stack):
    width, points = own.shape
    depth = stack.shape[0]
    turn = jnp.concatenate(
        [rot_ref[:, : 3 * width], where_even(rot_ref[:, 3 * width : depth], True)], axis=1
    )
    stack[:width, :] = own[...]
    stack[width : 2 * width, :] = one[...]
    stack[3 * width :, :] = three_a[...]

    @pl.when(on_even())
    def _():
        stack[2 * width : 3 * width, :] = two[...]

    @pl.when(jnp.logical_not(on_even()))
    def _():
        stack[2 * width : 2 * width + upper.shape[0], :] = upper[...]
        stack[2 * width + upper.shape[0] : 3 * width, :] = lower[...]

    tile = tile_of(points, 1024)
    for at in range(0, points, tile):
        here = slice(at, at + tile)
        out_ref[:, here] = jnp.dot(turn, stack[:, here], preferred_element_type=F32)


def gather(rotation, *blocks):
    (width, points), rows = blocks[0].shape, blocks[-1].shape[0]
    scratch = [pltpu.VMEM((3 * width + rows, points), BF16)]
    return call(
        gather_kernel, "gather", [((width, points), F32)], [rotation, *blocks], scratch, cost=GATHER
    )[0]


def apply_kernel(rot_ref, mine, swap_ref, two, three, proj_ref, after_ref, out_ref):
    width, flat = mine.shape
    points = proj_ref.shape[1]
    one = [swap_ref[width:, columns] for columns, _ in packed(mine.shape, swap_ref.shape[0] - width)]
    blocks = (mine[...], jnp.concatenate(one, axis=0), two[...], three[...])
    mixed = sum(
        jnp.dot(rot_ref[:, s * width : (s + 1) * width], block, preferred_element_type=F32)
        for s, block in enumerate(blocks)
    )
    mixed = mixed.astype(BF16)
    tile = tile_of(points, 2048)
    for at in range(0, points, tile):
        out_ref[:, at : at + tile] = jnp.dot(
            mixed, proj_ref[:, at : at + tile], preferred_element_type=F32
        )


def add_kernel(rot_ref, partial_ref, swap_ref, applied, out_ref):
    width, points = out_ref.shape
    turn = where_even(rot_ref[:, 3 * width : 4 * width], False)
    tile = tile_of(points, 2048)
    for at in range(0, points, tile):
        here = slice(at, at + tile)
        out_ref[:, here] = partial_ref[:, here] + jnp.dot(
            turn, swap_ref[:width, here], preferred_element_type=F32
        )


def finish_kernel(rot_ref, partial_ref, last_ref, applied, out_hbm, out_ref, sems):
    width, points = out_ref.shape
    pieces = sems.shape[0]
    tile = points // pieces
    turn = where_even(rot_ref[:, 4 * width - last_ref.shape[0] : 4 * width], True)
    copies = []
    for i in range(pieces):
        here = slice(i * tile, (i + 1) * tile)
        rotated = partial_ref[:, here] + jnp.dot(
            turn, last_ref[:, here], preferred_element_type=F32
        )
        added = rotated.astype(BF16).astype(F32) + applied[:, here]
        out_ref[:, here] = added.astype(out_ref.dtype)
        part = (slice(None), pl.ds(i * tile, tile))
        copies.append(pltpu.make_async_copy(out_ref.at[part], out_hbm.at[part], sems.at[i]))
        copies[-1].start()
    for copy in copies:
        copy.wait()


def finish(*args):
    width, points = args[-1].shape
    pieces = points // tile_of(points, 1536)
    return pl.pallas_call(
        finish_kernel,
        in_specs=[VMEM] * len(args),
        out_specs=pl.BlockSpec(memory_space=pl.ANY),
        out_shape=jax.ShapeDtypeStruct((width, points), BF16),
        scratch_shapes=[pltpu.VMEM((width, points), BF16), pltpu.SemaphoreType.DMA((pieces,))],
        compiler_params=ROOM,
        cost_estimate=flops(0),
        name="finish",
    )(*args)


def on_device(orbitals, rotation, projectors, coupling, slot_atom):
    width, points = orbitals.shape
    slot_count, rank, _ = projectors.shape
    owned = coupling.shape[0]
    proj = projectors.reshape(slot_count * rank, points)

    one = along_bands(orbitals, 1)
    upper, lower = [swapped(block) for block in halves(orbitals, [], CUT)]
    two = along_bands(hold(upper, lower, width, upper), 1)
    loads = from_all_domains(project(orbitals, proj, coupling.reshape(owned * rank, rank)))
    matched = list(match(slot_atom, owned, rank)) if by_permutes() else []
    upper, lower = [swapped(block) for block in halves(one, loads[-1:] + matched[:1])]
    if by_permutes():
        mine = couple_matched(loads, matched, width)
    else:
        mine = couple(slot_atom, loads, width, owned)
    mine_two = along_bands(mine, 2)
    three_a = along_bands(hold(upper, lower, width * 3 // 4, mine), 1)
    swap, held = choose(mine, mine_two, two, lower)
    mine_three = along_bands(mine_two, 1)
    three_b = along_bands(held, 1)
    swap = swapped(swap)
    partial = gather(rotation, orbitals, one, two, upper, lower, three_a)
    applied = call(
        apply_kernel,
        "apply",
        [((width, points), F32)],
        [rotation, mine, swap, mine_two, mine_three, proj, partial],
        cost=APPLY,
    )[0]
    outs = [(partial.shape, F32)]
    partial = call(add_kernel, "add", outs, [rotation, partial, swap, applied])[0]
    return finish(rotation, partial, three_b, applied)


def solution(mesh):
    in_specs = (P("band", "dom"), P("band", None), P(None, None, "dom"), P("dom", None, None), P())
    out_specs = P("band", "dom")
    return jax.shard_map(
        on_device, mesh=mesh, in_specs=in_specs, out_specs=out_specs, check_vma=False
    )
```
